32 devices in a mesh: seq: 8 (over z, y), head: 4 (over x, core).
Axes of the slice: x: 2, y: 2, z: 4, core: 2. Of those that a mesh axis runs over, the one named last changes fastest.
Arguments:
- queries: bfloat16 [12288, 2048], P('seq', 'head'), may hold values from -200 to 200
- keys_values: bfloat16 [2, 12288, 2048], P(None, 'seq', 'head'), may hold values from -6 to 6
- global_ids: int32 [2], replicated, may hold values from 0 to 191
- rand_ids: int32 [192, 3], replicated, may hold values from 0 to 191, as said below
- out_weight: bfloat16 [2048, 4096], P(None, 'head'), may hold values from -2 to 2
Outputs:
- projected: bfloat16 [12288, 4096], P('seq', 'head')
The draws below stay inside these ranges and needn't reach their ends.
Inputs may be any that keep to these rules, and one draw needn't show every extreme that they name: `rand_ids`: row i lists the 3 random key blocks of query block i. Among the 24 rows of one seq shard, at most 9 listed blocks lie on any one shard, and at most 3 of one column do; both bounds are reached.
All inputs are finite; a program needn't handle non-finite values.
Results may differ from the reference program's by a relative error of at most 0.0057.
Values may be sent and summed in bfloat16 or wider, within the bound.
No kernel may reach another device: no remote copies, remote signals or barrier semaphores. Data moves between devices by JAX's collectives and lax.ppermute only.
A program may use at most 128 MiB of HBM per device.

```python
import jax
import jax.numpy as jnp
from jax import lax

D = 4096
HEADS = 16
HEAD_DIM = 128
BLOCK = 64
NGLOBAL = 2
NRANDOM = 3
BLOCKS_DEV = 24
NBLOCKS = 192
TOKENS = 12288


def key_field(key):
    return jax.random.truncated_normal(jax.random.fold_in(key, 11), -6.0, 6.0, (TOKENS, HEADS * HEAD_DIM), jnp.float32)


def draw_keys_values(key, part):
    keys = key_field(key)
    values = jax.random.truncated_normal(jax.random.fold_in(key, 12), -6.0, 6.0, (TOKENS, HEADS * HEAD_DIM), jnp.float32)
    return jnp.stack([keys, values]).astype(jnp.bfloat16)


def draw_queries(key, part):
    base = jax.random.truncated_normal(jax.random.fold_in(key, 13), -6.0, 6.0, (TOKENS, HEADS * HEAD_DIM), jnp.float32)
    return base.astype(jnp.bfloat16)


def draw_rand_ids(key, part):
    shards = NBLOCKS // BLOCKS_DEV
    heat = jax.random.permutation(jax.random.fold_in(key, 21), shards)
    jitter = jax.random.randint(jax.random.fold_in(key, 22), (shards, shards), 0, max(shards // 4, 1) + 1)
    scores = (heat[None, :] + jitter) * shards + jnp.arange(shards)[None, :]
    ordering = jnp.argsort(scores, axis=1, stable=True)
    position = (jnp.arange(BLOCKS_DEV)[None, :] + BLOCKS_DEV * jnp.arange(NRANDOM)[:, None]) % shards
    sources = ordering[:, position]
    offsets = jax.random.randint(jax.random.fold_in(key, 23), (shards, NRANDOM, BLOCKS_DEV), 0, BLOCKS_DEV)
    listed = sources * BLOCKS_DEV + offsets
    return jnp.transpose(listed, (0, 2, 1)).reshape(NBLOCKS, NRANDOM).astype(jnp.int32)


def block_scale(stream_key, dims, cuts, least, high):
    def one(dim, shards_of):
        steps = jax.random.uniform(jax.random.fold_in(jax.random.fold_in(stream_key, 6), dim), (shards_of,), jnp.float32, least / len(cuts), high / len(cuts))
        return jnp.repeat(jnp.exp(steps), dims[dim] // shards_of).reshape((-1,) + (1,) * (len(dims) - dim - 1))

    level = one(*cuts[0])
    for cut in cuts[1:]:
        level = level * one(*cut)
    return level


def scatter_about(key, shape, scale, limit, split=(), held_as=jnp.bfloat16):
    loudness = block_scale(key, shape, split, -0.22, 0.18) if split else 1.0
    result = jax.random.normal(key, shape, jnp.float32) * scale * loudness
    return jnp.minimum(jnp.maximum(result, -limit), limit).astype(held_as)


def setup_inputs(seed: int = 0) -> dict:
    streams_of = jax.random.split(jax.random.key(seed), 6)
    queries = draw_queries(jax.random.fold_in(streams_of[5], 71), 0)
    keys_values = draw_keys_values(jax.random.fold_in(streams_of[5], 71), 0)
    global_ids = jax.random.randint(streams_of[2], (NGLOBAL,), 0, NBLOCKS).astype(jnp.int32)
    rand_ids = draw_rand_ids(jax.random.fold_in(streams_of[5], 71), 0)
    out_weight = scatter_about(streams_of[4], (HEADS * HEAD_DIM, D), (max(HEADS * HEAD_DIM // 256, 1)) ** -0.5, 2.0, ((1, 4),))
    return {"queries": queries, "keys_values": keys_values, "global_ids": global_ids, "rand_ids": rand_ids, "out_weight": out_weight}


group_blocks = 8


def attend_blocks(query_part, local_keys, local_values, glob_keys, glob_values, valid):
    scale = 1.0 / (HEAD_DIM ** 0.5)
    near_scores = jnp.einsum("bqhd,bkhd->bhqk", query_part, local_keys) * scale
    near_scores = jnp.where(valid[:, None, None, :], near_scores, -jnp.inf)
    glob_scores = jnp.einsum("bqhd,khd->bhqk", query_part, glob_keys) * scale
    highest = jnp.maximum(jnp.max(near_scores, axis=-1), jnp.max(glob_scores, axis=-1))
    near_exp = jnp.exp(near_scores - highest[..., None])
    glob_exp = jnp.exp(glob_scores - highest[..., None])
    total = jnp.sum(near_exp, axis=-1) + jnp.sum(glob_exp, axis=-1)
    near_weights = (near_exp / total[..., None]).astype(jnp.bfloat16).astype(jnp.float32)
    glob_weights = (glob_exp / total[..., None]).astype(jnp.bfloat16).astype(jnp.float32)
    mixed = jnp.einsum("bhqk,bkhd->bqhd", near_weights, local_values)
    mixed = mixed + jnp.einsum("bhqk,khd->bqhd", glob_weights, glob_values)
    return mixed.astype(jnp.bfloat16)


def reference(queries, keys_values, global_ids, rand_ids, out_weight):
    query_blocks = queries.reshape(NBLOCKS, BLOCK, HEADS, HEAD_DIM)
    pair_blocks = keys_values.reshape(2, NBLOCKS, BLOCK, HEADS, HEAD_DIM)
    glob = pair_blocks[:, global_ids].reshape(2, NGLOBAL * BLOCK, HEADS, HEAD_DIM).astype(jnp.float32)
    segment = jnp.arange((3 + NRANDOM) * BLOCK, dtype=jnp.int32) // BLOCK

    def one_group(first):
        block_ids = first + jnp.arange(group_blocks, dtype=jnp.int32)
        before = pair_blocks[:, jnp.clip(block_ids - 1, 0, NBLOCKS - 1)]
        current = pair_blocks[:, block_ids]
        after = pair_blocks[:, jnp.clip(block_ids + 1, 0, NBLOCKS - 1)]
        remote = pair_blocks[:, rand_ids[block_ids]].reshape(2, group_blocks, NRANDOM * BLOCK, HEADS, HEAD_DIM)
        local = jnp.concatenate([before, current, after, remote], axis=2).astype(jnp.float32)
        drop_before = (segment[None, :] == 0) & (block_ids[:, None] == 0)
        drop_after = (segment[None, :] == 2) & (block_ids[:, None] == NBLOCKS - 1)
        valid = jnp.logical_not(drop_before | drop_after)
        query_part = query_blocks[block_ids].astype(jnp.float32)
        return attend_blocks(query_part, local[0], local[1], glob[0], glob[1], valid)

    starts = jnp.arange(NBLOCKS // group_blocks, dtype=jnp.int32) * group_blocks
    attended = lax.map(one_group, starts).reshape(TOKENS, HEADS * HEAD_DIM)
    return jnp.dot(attended, out_weight, preferred_element_type=jnp.float32).astype(jnp.bfloat16)
```

```python
import functools

import jax
import jax.numpy as jnp
from jax import lax
from jax.experimental import pallas as pl
from jax.experimental.pallas import tpu as pltpu
from jax.sharding import PartitionSpec as P

HEAD_DIM = 128
BLOCK = 64
NGLOBAL = 2
NRANDOM = 3
NLIST = 3 + NGLOBAL + NRANDOM
MASKED = -1e30
EXP2_SCALE = 1.4426950408889634 / HEAD_DIM**0.5
STAT_ROWS = 32
VMEM_LIMIT = 32 * 1024 * 1024


group_blocks = 8


def eye_mask():
    rows = lax.broadcasted_iota(jnp.int32, (BLOCK, BLOCK), 0)
    columns = lax.broadcasted_iota(jnp.int32, (BLOCK, BLOCK), 1)
    return rows == columns


def attend_one(i, starts_ref, bias_ref, q_ref, pool):
    rows = pl.ds(pl.multiple_of(i * BLOCK, BLOCK), BLOCK)
    query = q_ref[rows, :]
    where_ = [
        pl.ds(pl.multiple_of(starts_ref[i * NLIST + e], BLOCK), BLOCK) for e in range(NLIST)
    ]
    keys = jnp.concatenate([pool[0, w, :] for w in where_], axis=0)
    scores = lax.dot_general(
        query, keys, (((1,), (1,)), ((), ())), preferred_element_type=jnp.float32
    )
    scores = scores + bias_ref[pl.ds(i, 1), :]
    highest = jnp.max(scores, axis=1, keepdims=True)
    weights = jnp.exp2((scores - highest) * EXP2_SCALE)
    total = jnp.sum(weights, axis=1, keepdims=True)
    values = jnp.concatenate([pool[1, w, :] for w in where_], axis=0)
    mixed = jnp.dot(weights.astype(jnp.bfloat16), values, preferred_element_type=jnp.float32)
    return rows, mixed, highest, total


def put_stats(i, stats_ref, highest, total):
    eye = eye_mask()
    high_row = jnp.sum(jnp.where(eye, highest, 0.0), axis=0, keepdims=True)
    total_row = jnp.sum(jnp.where(eye, total, 0.0), axis=0, keepdims=True)
    stats_ref[pl.ds(i, 1), :] = jnp.concatenate([high_row, total_row], axis=1)


def load_pool(parts, pool, sems):
    size = parts[0].shape[1]
    copies = [
        pltpu.make_async_copy(part, pool.at[:, pl.ds(n * size, size), :], sems.at[n])
        for n, part in enumerate(parts)
    ]
    for copy in copies:
        copy.start()
    for copy in copies:
        copy.wait()


def guest_kernel(
    unroll, starts_ref, bias_ref, q_ref, p0, p1, p2, p3, message_ref, pool, stats, sems
):
    load_pool((p0, p1, p2, p3), pool, sems)
    blocks = q_ref.shape[0] // BLOCK
    stats[...] = jnp.zeros_like(stats)

    def step(n, _):
        for u in range(unroll):
            i = n * unroll + u
            rows, mixed, highest, total = attend_one(i, starts_ref, bias_ref, q_ref, pool)
            message_ref[rows, :] = (mixed / total).astype(jnp.bfloat16)
            put_stats(i, stats, highest, total)
        return 0

    lax.fori_loop(0, blocks // unroll, step, 0)
    rest = stats[...]
    base = q_ref.shape[0]
    for n in range(3):
        piece = rest.astype(jnp.bfloat16)
        message_ref[pl.ds(base + n * STAT_ROWS, STAT_ROWS), :] = piece
        rest = rest - piece.astype(jnp.float32)


def home_kernel(
    unroll, starts_ref, bias_ref, q_ref, p0, p1, p2, p3, mixed_ref, stats_ref, pool, sems
):
    load_pool((p0, p1, p2, p3), pool, sems)
    blocks = q_ref.shape[0] // BLOCK
    stats_ref[...] = jnp.zeros_like(stats_ref)

    def step(n, _):
        for u in range(unroll):
            i = n * unroll + u
            rows, mixed, highest, total = attend_one(i, starts_ref, bias_ref, q_ref, pool)
            mixed_ref[rows, :] = mixed
            put_stats(i, stats_ref, highest, total)
        return 0

    lax.fori_loop(0, blocks // unroll, step, 0)


def merge_kernel(mixed_ref, stats_ref, message_ref, out_ref, home_scale, guest_scale):
    base = mixed_ref.shape[0]
    blocks = base // BLOCK
    other = message_ref[pl.ds(base, STAT_ROWS), :].astype(jnp.float32)
    for n in (1, 2):
        other = other + message_ref[pl.ds(base + n * STAT_ROWS, STAT_ROWS), :].astype(jnp.float32)
    here = stats_ref[...]
    high_h, total_h = here[:, :BLOCK], here[:, BLOCK:]
    high_g, total_g = other[:, :BLOCK], other[:, BLOCK:]
    highest = jnp.maximum(high_h, high_g)
    factor_h = jnp.exp2((high_h - highest) * EXP2_SCALE)
    factor_g = jnp.exp2((high_g - highest) * EXP2_SCALE) * total_g
    total = factor_h * total_h + factor_g
    total = jnp.where(total > 0, total, 1.0)
    home_scale[...] = factor_h / total
    guest_scale[...] = factor_g / total
    eye = eye_mask()

    def step(i, _):
        rows = pl.ds(pl.multiple_of(i * BLOCK, BLOCK), BLOCK)
        scale_h = jnp.sum(jnp.where(eye, home_scale[pl.ds(i, 1), :], 0.0), axis=1, keepdims=True)
        scale_g = jnp.sum(jnp.where(eye, guest_scale[pl.ds(i, 1), :], 0.0), axis=1, keepdims=True)
        mixed = mixed_ref[rows, :] * scale_h + message_ref[rows, :].astype(jnp.float32) * scale_g
        out_ref[rows, :] = mixed.astype(jnp.bfloat16)
        return 0

    lax.fori_loop(0, blocks, step, 0, unroll=4)


VMEM = pl.BlockSpec(memory_space=pltpu.VMEM)
SMEM = pl.BlockSpec(memory_space=pltpu.SMEM)
ANY = pl.BlockSpec(memory_space=pl.ANY)


def pool_scratch(rows):
    return pltpu.VMEM((2, 4 * rows, HEAD_DIM), jnp.bfloat16)


def attend_cost(rows):
    area = rows * NLIST * BLOCK
    return pl.CostEstimate(
        flops=4 * area * HEAD_DIM, bytes_accessed=20 * rows * HEAD_DIM, transcendentals=area
    )


def guest_call(starts, bias, query, parts):
    rows = query.shape[0]
    return pl.pallas_call(
        functools.partial(guest_kernel, 4),
        out_shape=jax.ShapeDtypeStruct((rows + 3 * STAT_ROWS, HEAD_DIM), jnp.bfloat16),
        in_specs=[SMEM, VMEM, VMEM, ANY, ANY, ANY, ANY],
        out_specs=VMEM,
        scratch_shapes=[
            pool_scratch(rows),
            pltpu.VMEM((STAT_ROWS, 2 * BLOCK), jnp.float32),
            pltpu.SemaphoreType.DMA((4,)),
        ],
        compiler_params=pltpu.CompilerParams(vmem_limit_bytes=VMEM_LIMIT),
        cost_estimate=attend_cost(rows),
        name="guest_attention",
    )(starts, bias, query, *parts)


def home_call(starts, bias, query, parts):
    rows = query.shape[0]
    return pl.pallas_call(
        functools.partial(home_kernel, 4),
        out_shape=(
            jax.ShapeDtypeStruct((rows, HEAD_DIM), jnp.float32),
            jax.ShapeDtypeStruct((STAT_ROWS, 2 * BLOCK), jnp.float32),
        ),
        in_specs=[SMEM, VMEM, VMEM, ANY, ANY, ANY, ANY],
        out_specs=(VMEM, VMEM),
        scratch_shapes=[pool_scratch(rows), pltpu.SemaphoreType.DMA((4,))],
        compiler_params=pltpu.CompilerParams(vmem_limit_bytes=VMEM_LIMIT),
        cost_estimate=attend_cost(rows),
        name="home_attention",
    )(starts, bias, query, *parts)


def merge_call(mixed, stats, message):
    rows = mixed.shape[0]
    return pl.pallas_call(
        merge_kernel,
        out_shape=jax.ShapeDtypeStruct((rows, HEAD_DIM), jnp.bfloat16),
        in_specs=[VMEM, VMEM, VMEM],
        out_specs=VMEM,
        scratch_shapes=[
            pltpu.VMEM((STAT_ROWS, BLOCK), jnp.float32),
            pltpu.VMEM((STAT_ROWS, BLOCK), jnp.float32),
        ],
        compiler_params=pltpu.CompilerParams(vmem_limit_bytes=VMEM_LIMIT),
        cost_estimate=pl.CostEstimate(
            flops=4 * rows * HEAD_DIM, bytes_accessed=8 * rows * HEAD_DIM, transcendentals=0
        ),
        name="merge_halves",
    )(mixed, stats, message)


def key_places(shard, myself, global_ids, rand_ids, local_blocks, shards):
    half = shards // 2
    total_blocks = local_blocks * shards
    block_ids = shard * local_blocks + jnp.arange(local_blocks, dtype=jnp.int32)
    near = block_ids[:, None] + jnp.arange(-1, 2, dtype=jnp.int32)[None, :]
    inside = (near >= 0) & (near < total_blocks)
    listed = lax.dynamic_slice_in_dim(rand_ids, shard * local_blocks, local_blocks, 0)
    glob = jnp.broadcast_to(global_ids[None, :], (local_blocks, NGLOBAL))
    ids = jnp.concatenate([jnp.clip(near, 0, total_blocks - 1), glob, listed], axis=1)
    owner = ids // local_blocks
    here = (owner // half) == (myself // half)
    here = here & jnp.concatenate(
        [inside, jnp.ones((local_blocks, NGLOBAL + NRANDOM), jnp.bool_)], axis=1
    )
    relative = (owner ^ myself) & (half - 1)
    starts = jnp.where(here, (relative * local_blocks + ids % local_blocks) * BLOCK, 0)
    bias = jnp.repeat(jnp.where(here, 0.0, MASKED).astype(jnp.float32), BLOCK, axis=1)
    return starts.reshape(-1).astype(jnp.int32), bias


def swap(value, distance, shards):
    return lax.ppermute(value, "seq", [(i, i ^ distance) for i in range(shards)])


def halves_body(queries, keys_values, global_ids, rand_ids, out_weight):
    rows, width = queries.shape
    heads_here = width // HEAD_DIM
    local_blocks = rows // BLOCK
    shards = lax.axis_size("seq")
    myself = lax.axis_index("seq")
    groups = lax.axis_size("head")
    opposite = shards // 2

    def column(array, head):
        return lax.slice_in_dim(array, head * HEAD_DIM, (head + 1) * HEAD_DIM, axis=array.ndim - 1)

    own_pairs = [column(keys_values, h) for h in range(heads_here)]
    own_queries = [column(queries, h) for h in range(heads_here)]
    home = key_places(myself, myself, global_ids, rand_ids, local_blocks, shards)
    guest = key_places(myself ^ opposite, myself, global_ids, rand_ids, local_blocks, shards)

    parts, visitors = [], []
    for h in range(heads_here):
        along_z = swap(own_pairs[h], 2, shards)
        along_y = swap(own_pairs[h], 1, shards)
        visitors.append(swap(own_queries[h], opposite, shards))
        diagonal = swap(along_z, 1, shards)
        parts.append((own_pairs[h], along_y, along_z, diagonal))

    weights = out_weight.reshape(groups, heads_here, HEAD_DIM, out_weight.shape[1])
    summed = None
    for h in range(heads_here):
        message = guest_call(*guest, visitors[h], parts[h])
        answer = swap(message, opposite, shards)
        mixed, stats = home_call(*home, own_queries[h], parts[h])
        attended = merge_call(mixed, stats, answer)
        gathered = lax.all_gather(attended, "head", axis=1, tiled=True)
        weight = weights[:, h].reshape(groups * HEAD_DIM, -1)
        term = jnp.dot(gathered, weight, preferred_element_type=jnp.float32)
        summed = term if summed is None else summed + term
    return summed.astype(jnp.bfloat16)


def padded_2(block, sides, width):
    for axis, dim in sides:
        count = lax.axis_size(axis)
        forward = [(i, i + 1) for i in range(count - 1)]
        backward = [(target, source) for source, target in forward]
        low = lax.ppermute(
            lax.slice_in_dim(block, block.shape[dim] - width, None, axis=dim), axis, forward
        )
        high = lax.ppermute(lax.slice_in_dim(block, 0, width, axis=dim), axis, backward)
        block = jnp.concatenate([low, block, high], axis=dim)
    return block


def broadcast(block, axis, owner):
    block = jnp.where(lax.axis_index(axis) == owner, block, jnp.zeros_like(block))
    return lax.psum(block, axis)


def plan_slots(requests, myself, capacity, per_shard):
    sources = requests // per_shard
    offsets = requests % per_shard
    count = requests.shape[1]
    order = jnp.arange(count, dtype=jnp.int32)
    earlier = (order[:, None] < order[None, :]).astype(jnp.int32)
    matches = (sources[:, :, None] == sources[:, None, :]).astype(jnp.int32)
    ranks = jnp.sum(matches * earlier[None], axis=1)
    slot_range = jnp.arange(capacity, dtype=jnp.int32)
    wanted = (
        (sources == myself)[:, None, :] & (ranks[:, None, :] == slot_range[None, :, None])
    ).astype(jnp.int32)
    chosen = jnp.sum(wanted * offsets[:, None, :], axis=2).reshape(-1)
    own_sources = lax.dynamic_index_in_dim(sources, myself, 0, keepdims=False)
    own_ranks = lax.dynamic_index_in_dim(ranks, myself, 0, keepdims=False)
    return (chosen, own_sources * capacity + own_ranks)


def attend_blocks(query_part, local_keys, local_values, glob_keys, glob_values, valid):
    scale = 1.0 / HEAD_DIM**0.5
    near_scores = (
        jnp.einsum("bqhd,bkhd->bhqk", query_part, local_keys, preferred_element_type=jnp.float32)
        * scale
    )
    near_scores = jnp.where(valid[:, None, None, :], near_scores, -jnp.inf)
    glob_scores = (
        jnp.einsum("bqhd,khd->bhqk", query_part, glob_keys, preferred_element_type=jnp.float32)
        * scale
    )
    highest = jnp.maximum(jnp.max(near_scores, axis=-1), jnp.max(glob_scores, axis=-1))
    near_exp = jnp.exp(near_scores - highest[..., None])
    glob_exp = jnp.exp(glob_scores - highest[..., None])
    total = jnp.sum(near_exp, axis=-1) + jnp.sum(glob_exp, axis=-1)
    near_weights = (near_exp / total[..., None]).astype(jnp.bfloat16)
    glob_weights = (glob_exp / total[..., None]).astype(jnp.bfloat16)
    mixed = jnp.einsum(
        "bhqk,bkhd->bqhd", near_weights, local_values, preferred_element_type=jnp.float32
    )
    mixed = mixed + jnp.einsum(
        "bhqk,khd->bqhd", glob_weights, glob_values, preferred_element_type=jnp.float32
    )
    return mixed.astype(jnp.bfloat16)


def exchange_body(queries, keys_values, global_ids, rand_ids, out_weight):
    rows = queries.shape[0]
    width = queries.shape[1]
    heads_here = width // HEAD_DIM
    local_blocks = rows // BLOCK
    shards = lax.axis_size("seq")
    myself = lax.axis_index("seq")
    total_blocks = local_blocks * shards
    pair_blocks = keys_values.reshape(2, local_blocks, BLOCK, width)
    padded = padded_2(keys_values, (("seq", 1),), BLOCK)
    padded = padded.reshape(2, local_blocks + 2, BLOCK, width)
    panel_list = []
    for which in range(NGLOBAL):
        target = global_ids[which]
        owner = target // local_blocks
        local_panel = lax.dynamic_index_in_dim(
            pair_blocks, target % local_blocks, 1, keepdims=False
        )
        panel_list.append(broadcast(local_panel, "seq", owner))
    glob = jnp.stack(panel_list, axis=1).reshape(2, NGLOBAL * BLOCK, heads_here, HEAD_DIM)
    requests = rand_ids.reshape(shards, local_blocks, NRANDOM)
    capacity = (local_blocks + shards - 1) // shards
    fetched = []
    for column in range(NRANDOM):
        chosen, slots = plan_slots(requests[:, :, column], myself, capacity, local_blocks)
        outgoing = jnp.take(pair_blocks, chosen, axis=1)
        incoming = lax.all_to_all(outgoing, "seq", split_axis=1, concat_axis=1, tiled=True)
        fetched.append(jnp.take(incoming, slots, axis=1))
    remote = jnp.stack(fetched, axis=2)
    segment = jnp.arange((3 + NRANDOM) * BLOCK, dtype=jnp.int32) // BLOCK

    def one_group(index):
        first = index * group_blocks
        query_part = lax.dynamic_slice_in_dim(queries, first * BLOCK, group_blocks * BLOCK, 0)
        query_part = query_part.reshape(group_blocks, BLOCK, heads_here, HEAD_DIM)
        window = lax.dynamic_slice_in_dim(padded, first, group_blocks + 2, 1)
        farther = lax.dynamic_slice_in_dim(remote, first, group_blocks, 1)
        farther = farther.reshape(2, group_blocks, NRANDOM * BLOCK, width)
        local = jnp.concatenate(
            [
                window[:, 0:group_blocks],
                window[:, 1 : group_blocks + 1],
                window[:, 2 : group_blocks + 2],
                farther,
            ],
            axis=2,
        )
        local = local.reshape(2, group_blocks, (3 + NRANDOM) * BLOCK, heads_here, HEAD_DIM)
        block_ids = myself * local_blocks + first + jnp.arange(group_blocks, dtype=jnp.int32)
        drop_before = (segment[None, :] == 0) & (block_ids[:, None] == 0)
        drop_after = (segment[None, :] == 2) & (block_ids[:, None] == total_blocks - 1)
        valid = jnp.logical_not(drop_before | drop_after)
        mixed = attend_blocks(query_part, local[0], local[1], glob[0], glob[1], valid)
        return mixed.reshape(group_blocks * BLOCK, width)

    attended = lax.map(
        one_group, jnp.arange(local_blocks // group_blocks, dtype=jnp.int32)
    ).reshape(rows, width)
    summed = jnp.dot(
        lax.all_gather(attended, "head", axis=1, tiled=True),
        out_weight,
        preferred_element_type=jnp.float32,
    )
    return summed.astype(jnp.bfloat16)


def solution(mesh):
    body = halves_body if mesh.shape["seq"] == 8 else exchange_body
    in_specs = (P("seq", "head"), P(None, "seq", "head"), P(), P(), P(None, "head"))
    out_specs = P("seq", "head")
    return jax.shard_map(body, mesh=mesh, in_specs=in_specs, out_specs=out_specs, check_vma=False)
```

```python
import functools

import jax
import jax.numpy as jnp
from jax import lax
from jax.experimental import pallas as pl
from jax.experimental.pallas import tpu as pltpu
from jax.sharding import PartitionSpec as P

HEAD_DIM = 128
BLOCK = 64
NGLOBAL = 2
NRANDOM = 3
NLIST = 3 + NGLOBAL + NRANDOM
MASKED = -1e30
EXP2_SCALE = 1.4426950408889634 / HEAD_DIM**0.5
STAT_ROWS = 32
VMEM_LIMIT = 32 * 1024 * 1024


group_blocks = 8


def eye_mask():
    rows = lax.broadcasted_iota(jnp.int32, (BLOCK, BLOCK), 0)
    columns = lax.broadcasted_iota(jnp.int32, (BLOCK, BLOCK), 1)
    return rows == columns


def attend_group(blocks, head, starts_ref, bias_ref, q_ref, pool):
    lanes = pl.ds(head * HEAD_DIM, HEAD_DIM)
    listed = [
        [
            pl.ds(pl.multiple_of(starts_ref[i * NLIST + e], BLOCK), BLOCK)
            for e in range(NLIST)
        ]
        for i in blocks
    ]
    places = [pl.ds(pl.multiple_of(i * BLOCK, BLOCK), BLOCK) for i in blocks]
    scores = []
    for i, rows, listing in zip(blocks, places, listed):
        keys = jnp.concatenate([pool[0, w, lanes] for w in listing], axis=0)
        product = lax.dot_general(
            q_ref[rows, lanes],
            keys,
            (((1,), (1,)), ((), ())),
            preferred_element_type=jnp.float32,
        )
        scores.append(product + bias_ref[pl.ds(i, 1), :])
    weighed = []
    for score in scores:
        highest = jnp.max(score, axis=1, keepdims=True)
        weights = jnp.exp2((score - highest) * EXP2_SCALE)
        total = jnp.sum(weights, axis=1, keepdims=True)
        weighed.append((weights.astype(jnp.bfloat16), highest, total))
    results = []
    for rows, listing, (weights, highest, total) in zip(places, listed, weighed):
        values = jnp.concatenate([pool[1, w, lanes] for w in listing], axis=0)
        mixed = jnp.dot(weights, values, preferred_element_type=jnp.float32)
        results.append((rows, lanes, mixed, highest, total))
    return results


def put_stats(i, head, stats_ref, highest, total):
    eye = eye_mask()
    high_row = jnp.sum(jnp.where(eye, highest, 0.0), axis=0, keepdims=True)
    total_row = jnp.sum(jnp.where(eye, total, 0.0), axis=0, keepdims=True)
    stats_ref[head, pl.ds(i, 1), :] = jnp.concatenate([high_row, total_row], axis=1)


def load_pool(parts, pool, sems):
    size = parts[0].shape[1]
    copies = [
        pltpu.make_async_copy(part, pool.at[:, pl.ds(n * size, size), :], sems.at[n])
        for n, part in enumerate(parts)
    ]
    for copy in copies:
        copy.start()
    for copy in copies:
        copy.wait()


def guest_kernel(
    unroll, starts_ref, bias_ref, q_ref, p0, p1, p2, p3, message_ref, pool, stats, sems
):
    load_pool((p0, p1, p2, p3), pool, sems)
    blocks = q_ref.shape[0] // BLOCK
    stats[...] = jnp.zeros_like(stats)

    for head in range(q_ref.shape[1] // HEAD_DIM):

        def step(n, _):
            ids = [n * unroll + u for u in range(unroll)]
            results = attend_group(ids, head, starts_ref, bias_ref, q_ref, pool)
            for i, (rows, lanes, mixed, highest, total) in zip(ids, results):
                message_ref[rows, lanes] = (mixed / total).astype(jnp.bfloat16)
                put_stats(i, head, stats, highest, total)
            return 0

        lax.fori_loop(0, blocks // unroll, step, 0)
    base = q_ref.shape[0]
    for head in range(q_ref.shape[1] // HEAD_DIM):
        rest = stats[head]
        for n in range(3):
            piece = rest.astype(jnp.bfloat16)
            rows = pl.ds(base + n * STAT_ROWS, STAT_ROWS)
            message_ref[rows, pl.ds(head * HEAD_DIM, HEAD_DIM)] = piece
            rest = rest - piece.astype(jnp.float32)


def home_kernel(
    unroll, starts_ref, bias_ref, q_ref, p0, p1, p2, p3, mixed_ref, stats_ref, pool, sems
):
    load_pool((p0, p1, p2, p3), pool, sems)
    blocks = q_ref.shape[0] // BLOCK
    stats_ref[...] = jnp.zeros_like(stats_ref)

    for head in range(q_ref.shape[1] // HEAD_DIM):

        def step(n, _):
            ids = [n * unroll + u for u in range(unroll)]
            results = attend_group(ids, head, starts_ref, bias_ref, q_ref, pool)
            for i, (rows, lanes, mixed, highest, total) in zip(ids, results):
                mixed_ref[rows, lanes] = mixed
                put_stats(i, head, stats_ref, highest, total)
            return 0

        lax.fori_loop(0, blocks // unroll, step, 0)


def merge_kernel(mixed_ref, stats_ref, message_ref, out_ref, home_scale, guest_scale):
    base, width = mixed_ref.shape
    blocks = base // BLOCK
    other = message_ref[pl.ds(base, STAT_ROWS), :].astype(jnp.float32)
    for n in (1, 2):
        other = other + message_ref[pl.ds(base + n * STAT_ROWS, STAT_ROWS), :].astype(jnp.float32)
    eye = eye_mask()
    for head in range(width // HEAD_DIM):
        low = head * HEAD_DIM
        lanes = pl.ds(low, HEAD_DIM)
        high_h = stats_ref[head, :, :BLOCK]
        total_h = stats_ref[head, :, BLOCK:]
        high_g = other[:, low : low + BLOCK]
        total_g = other[:, low + BLOCK : low + HEAD_DIM]
        highest = jnp.maximum(high_h, high_g)
        factor_h = jnp.exp2((high_h - highest) * EXP2_SCALE)
        factor_g = jnp.exp2((high_g - highest) * EXP2_SCALE) * total_g
        total = factor_h * total_h + factor_g
        total = jnp.where(total > 0, total, 1.0)
        home_scale[...] = factor_h / total
        guest_scale[...] = factor_g / total

        def step(i, _):
            rows = pl.ds(pl.multiple_of(i * BLOCK, BLOCK), BLOCK)
            scale_h = jnp.sum(
                jnp.where(eye, home_scale[pl.ds(i, 1), :], 0.0), axis=1, keepdims=True
            )
            scale_g = jnp.sum(
                jnp.where(eye, guest_scale[pl.ds(i, 1), :], 0.0), axis=1, keepdims=True
            )
            mixed = (
                mixed_ref[rows, lanes] * scale_h
                + message_ref[rows, lanes].astype(jnp.float32) * scale_g
            )
            out_ref[rows, lanes] = mixed.astype(jnp.bfloat16)
            return 0

        lax.fori_loop(0, blocks, step, 0, unroll=4)


def products(x_refs, w_refs):
    total = None
    for x_ref, w_ref in zip(x_refs, w_refs):
        weight = w_ref[...].reshape(-1, w_ref.shape[-1])
        term = jnp.dot(x_ref[...], weight, preferred_element_type=jnp.float32)
        total = term if total is None else total + term
    return total


def first_terms_kernel(count, _, *refs):
    refs[-1][...] = products(refs[:count], refs[count : 2 * count])


def last_term_kernel(count, _, sum_ref, *refs):
    total = sum_ref[...] + products(refs[:count], refs[count : 2 * count])
    refs[-1][...] = total.astype(refs[-1].dtype)


VMEM = pl.BlockSpec(memory_space=pltpu.VMEM)
SMEM = pl.BlockSpec(memory_space=pltpu.SMEM)
ANY = pl.BlockSpec(memory_space=pl.ANY)


def params():
    return pltpu.CompilerParams(vmem_limit_bytes=VMEM_LIMIT)


def pool_scratch(query):
    return pltpu.VMEM((2, 4 * query.shape[0], query.shape[1]), jnp.bfloat16)


def stats_shape(query, kind):
    return kind((query.shape[1] // HEAD_DIM, STAT_ROWS, 2 * BLOCK), jnp.float32)


def cost(micros):
    return pl.CostEstimate(flops=int(micros * 1.15e9), bytes_accessed=0, transcendentals=0)


def guest_call(starts, bias, query, parts):
    rows, width = query.shape
    return pl.pallas_call(
        functools.partial(guest_kernel, UNROLL),
        out_shape=jax.ShapeDtypeStruct((rows + 3 * STAT_ROWS, width), jnp.bfloat16),
        in_specs=[SMEM, VMEM, VMEM, ANY, ANY, ANY, ANY],
        out_specs=VMEM,
        scratch_shapes=[
            pool_scratch(query),
            stats_shape(query, pltpu.VMEM),
            pltpu.SemaphoreType.DMA((4,)),
        ],
        compiler_params=params(),
        cost_estimate=cost(ATTEND_US * width // HEAD_DIM),
        name="guest_attention",
    )(starts, bias, query, *parts)


def home_call(starts, bias, query, parts):
    rows, width = query.shape
    return pl.pallas_call(
        functools.partial(home_kernel, UNROLL),
        out_shape=(
            jax.ShapeDtypeStruct((rows, width), jnp.float32),
            stats_shape(query, jax.ShapeDtypeStruct),
        ),
        in_specs=[SMEM, VMEM, VMEM, ANY, ANY, ANY, ANY],
        out_specs=(VMEM, VMEM),
        scratch_shapes=[pool_scratch(query), pltpu.SemaphoreType.DMA((4,))],
        compiler_params=params(),
        cost_estimate=cost(ATTEND_US * width // HEAD_DIM),
        name="home_attention",
    )(starts, bias, query, *parts)


def merge_call(mixed, stats, message):
    return pl.pallas_call(
        merge_kernel,
        out_shape=jax.ShapeDtypeStruct(mixed.shape, jnp.bfloat16),
        in_specs=[VMEM, VMEM, VMEM],
        out_specs=VMEM,
        scratch_shapes=[
            pltpu.VMEM((STAT_ROWS, BLOCK), jnp.float32),
            pltpu.VMEM((STAT_ROWS, BLOCK), jnp.float32),
        ],
        compiler_params=params(),
        cost_estimate=cost(MERGE_US),
        name="merge_halves",
    )(mixed, stats, message)


ROW_TILE = 256


def weight_spec(weights, chunk, relation):
    first, count = chunk
    _, _, depth, columns = weights.shape
    return pl.BlockSpec(
        (1, count, depth, columns), lambda i, me: (me[0] ^ relation, first // count, 0, 0)
    )


def row_spec(array):
    return pl.BlockSpec((ROW_TILE, array.shape[1]), lambda i, me: (i, 0))


def project(kernel, name, summed, gathered, chunks, weights, result):
    rows = gathered[0][0].shape[0]
    columns = weights.shape[3]
    pieces = [piece for group in gathered for piece in group]
    specs = [
        weight_spec(weights, chunk, relation)
        for chunk, group in zip(chunks, gathered)
        for relation in range(len(group))
    ]
    sums = [] if summed is None else [summed]
    myself = lax.axis_index("head").astype(jnp.int32).reshape(1)
    return pl.pallas_call(
        functools.partial(kernel, len(pieces)),
        out_shape=jax.ShapeDtypeStruct((rows, columns), result),
        grid_spec=pltpu.PrefetchScalarGridSpec(
            num_scalar_prefetch=1,
            grid=(rows // ROW_TILE,),
            in_specs=[row_spec(v) for v in sums + pieces] + specs,
            out_specs=pl.BlockSpec((ROW_TILE, columns), lambda i, me: (i, 0)),
        ),
        compiler_params=params(),
        cost_estimate=cost(0),
        name=name,
    )(myself, *sums, *pieces, *[weights for _ in specs])


def key_places(shard, myself, global_ids, rand_ids, local_blocks, shards):
    half = shards // 2
    total_blocks = local_blocks * shards
    block_ids = shard * local_blocks + jnp.arange(local_blocks, dtype=jnp.int32)
    near = block_ids[:, None] + jnp.arange(-1, 2, dtype=jnp.int32)[None, :]
    inside = (near >= 0) & (near < total_blocks)
    listed = lax.dynamic_slice_in_dim(rand_ids, shard * local_blocks, local_blocks, 0)
    glob = jnp.broadcast_to(global_ids[None, :], (local_blocks, NGLOBAL))
    ids = jnp.concatenate([jnp.clip(near, 0, total_blocks - 1), glob, listed], axis=1)
    owner = ids // local_blocks
    here = (owner // half) == (myself // half)
    here = here & jnp.concatenate(
        [inside, jnp.ones((local_blocks, NGLOBAL + NRANDOM), jnp.bool_)], axis=1
    )
    relative = (owner ^ myself) & (half - 1)
    starts = jnp.where(here, (relative * local_blocks + ids % local_blocks) * BLOCK, 0)
    bias = jnp.repeat(jnp.where(here, 0.0, MASKED).astype(jnp.float32), BLOCK, axis=1)
    return starts.reshape(-1).astype(jnp.int32), bias


def swap(value, distance, shards):
    return lax.ppermute(value, "seq", [(i, i ^ distance) for i in range(shards)])


def after(value, *tokens):
    return lax.optimization_barrier((value, *tokens))[0]


def gather_heads(value):
    def hop(v, distance):
        return lax.ppermute(v, "head", [(i, i ^ distance) for i in range(4)])

    across = hop(value, 2)
    return value, hop(value, 1), across, hop(across, 1)


CHUNKS = ((0, 2), (2, 1), (3, 1))
UNROLL = 8
ATTEND_US = 0
MERGE_US = 0


def halves_body(queries, keys_values, global_ids, rand_ids, out_weight):
    rows, width = queries.shape
    heads_here = width // HEAD_DIM
    local_blocks = rows // BLOCK
    shards = lax.axis_size("seq")
    myself = lax.axis_index("seq")
    groups = lax.axis_size("head")
    opposite = shards // 2

    def column(array, chunk):
        low, count = chunk
        return lax.slice_in_dim(
            array, low * HEAD_DIM, (low + count) * HEAD_DIM, axis=array.ndim - 1
        )

    own_pairs = [column(keys_values, c) for c in CHUNKS]
    own_queries = [column(queries, c) for c in CHUNKS]

    along_y = [swap(own_pairs[0], 1, shards)]
    along_z = [swap(own_pairs[0], 2, shards)]
    diagonal = [swap(along_z[0], 1, shards)]
    visitors = [swap(after(own_queries[0], along_z[0]), opposite, shards)]
    for n in (1, 2):
        along_z.append(swap(after(own_pairs[n], along_z[n - 1]), 2, shards))
        along_y.append(swap(after(own_pairs[n], along_z[n - 1]), 1, shards))
        diagonal.append(swap(along_z[n], 1, shards))
        visitors.append(swap(after(own_queries[n], along_z[n]), opposite, shards))

    home = key_places(myself, myself, global_ids, rand_ids, local_blocks, shards)
    guest = key_places(myself ^ opposite, myself, global_ids, rand_ids, local_blocks, shards)
    weights = out_weight.reshape(groups, heads_here, HEAD_DIM, out_weight.shape[1])
    gathered = []
    for n in range(len(CHUNKS)):
        parts = (own_pairs[n], along_y[n], along_z[n], diagonal[n])
        visitor = visitors[n]
        message = guest_call(*guest, visitor, parts)
        answer = swap(message, opposite, shards)
        mixed, stats = home_call(*home, after(own_queries[n], message), parts)
        if n == 2:
            summed = project(
                first_terms_kernel,
                "first_terms",
                None,
                gathered,
                CHUNKS[:2],
                after(weights, mixed),
                jnp.float32,
            )
            answer = after(answer, summed)
        attended = merge_call(mixed, stats, answer)
        gathered.append(gather_heads(attended))
    return project(
        last_term_kernel,
        "last_term",
        summed,
        gathered[2:],
        CHUNKS[2:],
        weights,
        jnp.bfloat16,
    )


def padded_2(block, sides, width):
    for axis, dim in sides:
        count = lax.axis_size(axis)
        forward = [(i, i + 1) for i in range(count - 1)]
        backward = [(target, source) for source, target in forward]
        low = lax.ppermute(
            lax.slice_in_dim(block, block.shape[dim] - width, None, axis=dim), axis, forward
        )
        high = lax.ppermute(lax.slice_in_dim(block, 0, width, axis=dim), axis, backward)
        block = jnp.concatenate([low, block, high], axis=dim)
    return block


def broadcast(block, axis, owner):
    block = jnp.where(lax.axis_index(axis) == owner, block, jnp.zeros_like(block))
    return lax.psum(block, axis)


def plan_slots(requests, myself, capacity, per_shard):
    sources = requests // per_shard
    offsets = requests % per_shard
    count = requests.shape[1]
    order = jnp.arange(count, dtype=jnp.int32)
    earlier = (order[:, None] < order[None, :]).astype(jnp.int32)
    matches = (sources[:, :, None] == sources[:, None, :]).astype(jnp.int32)
    ranks = jnp.sum(matches * earlier[None], axis=1)
    slot_range = jnp.arange(capacity, dtype=jnp.int32)
    wanted = (
        (sources == myself)[:, None, :] & (ranks[:, None, :] == slot_range[None, :, None])
    ).astype(jnp.int32)
    chosen = jnp.sum(wanted * offsets[:, None, :], axis=2).reshape(-1)
    own_sources = lax.dynamic_index_in_dim(sources, myself, 0, keepdims=False)
    own_ranks = lax.dynamic_index_in_dim(ranks, myself, 0, keepdims=False)
    return (chosen, own_sources * capacity + own_ranks)


def attend_blocks(query_part, local_keys, local_values, glob_keys, glob_values, valid):
    scale = 1.0 / HEAD_DIM**0.5
    near_scores = (
        jnp.einsum("bqhd,bkhd->bhqk", query_part, local_keys, preferred_element_type=jnp.float32)
        * scale
    )
    near_scores = jnp.where(valid[:, None, None, :], near_scores, -jnp.inf)
    glob_scores = (
        jnp.einsum("bqhd,khd->bhqk", query_part, glob_keys, preferred_element_type=jnp.float32)
        * scale
    )
    highest = jnp.maximum(jnp.max(near_scores, axis=-1), jnp.max(glob_scores, axis=-1))
    near_exp = jnp.exp(near_scores - highest[..., None])
    glob_exp = jnp.exp(glob_scores - highest[..., None])
    total = jnp.sum(near_exp, axis=-1) + jnp.sum(glob_exp, axis=-1)
    near_weights = (near_exp / total[..., None]).astype(jnp.bfloat16)
    glob_weights = (glob_exp / total[..., None]).astype(jnp.bfloat16)
    mixed = jnp.einsum(
        "bhqk,bkhd->bqhd", near_weights, local_values, preferred_element_type=jnp.float32
    )
    mixed = mixed + jnp.einsum(
        "bhqk,khd->bqhd", glob_weights, glob_values, preferred_element_type=jnp.float32
    )
    return mixed.astype(jnp.bfloat16)


def exchange_body(queries, keys_values, global_ids, rand_ids, out_weight):
    rows = queries.shape[0]
    width = queries.shape[1]
    heads_here = width // HEAD_DIM
    local_blocks = rows // BLOCK
    shards = lax.axis_size("seq")
    myself = lax.axis_index("seq")
    total_blocks = local_blocks * shards
    pair_blocks = keys_values.reshape(2, local_blocks, BLOCK, width)
    padded = padded_2(keys_values, (("seq", 1),), BLOCK)
    padded = padded.reshape(2, local_blocks + 2, BLOCK, width)
    panel_list = []
    for which in range(NGLOBAL):
        target = global_ids[which]
        owner = target // local_blocks
        local_panel = lax.dynamic_index_in_dim(
            pair_blocks, target % local_blocks, 1, keepdims=False
        )
        panel_list.append(broadcast(local_panel, "seq", owner))
    glob = jnp.stack(panel_list, axis=1).reshape(2, NGLOBAL * BLOCK, heads_here, HEAD_DIM)
    requests = rand_ids.reshape(shards, local_blocks, NRANDOM)
    capacity = (local_blocks + shards - 1) // shards
    fetched = []
    for column in range(NRANDOM):
        chosen, slots = plan_slots(requests[:, :, column], myself, capacity, local_blocks)
        outgoing = jnp.take(pair_blocks, chosen, axis=1)
        incoming = lax.all_to_all(outgoing, "seq", split_axis=1, concat_axis=1, tiled=True)
        fetched.append(jnp.take(incoming, slots, axis=1))
    remote = jnp.stack(fetched, axis=2)
    segment = jnp.arange((3 + NRANDOM) * BLOCK, dtype=jnp.int32) // BLOCK

    def one_group(index):
        first = index * group_blocks
        query_part = lax.dynamic_slice_in_dim(queries, first * BLOCK, group_blocks * BLOCK, 0)
        query_part = query_part.reshape(group_blocks, BLOCK, heads_here, HEAD_DIM)
        window = lax.dynamic_slice_in_dim(padded, first, group_blocks + 2, 1)
        farther = lax.dynamic_slice_in_dim(remote, first, group_blocks, 1)
        farther = farther.reshape(2, group_blocks, NRANDOM * BLOCK, width)
        local = jnp.concatenate(
            [
                window[:, 0:group_blocks],
                window[:, 1 : group_blocks + 1],
                window[:, 2 : group_blocks + 2],
                farther,
            ],
            axis=2,
        )
        local = local.reshape(2, group_blocks, (3 + NRANDOM) * BLOCK, heads_here, HEAD_DIM)
        block_ids = myself * local_blocks + first + jnp.arange(group_blocks, dtype=jnp.int32)
        drop_before = (segment[None, :] == 0) & (block_ids[:, None] == 0)
        drop_after = (segment[None, :] == 2) & (block_ids[:, None] == total_blocks - 1)
        valid = jnp.logical_not(drop_before | drop_after)
        mixed = attend_blocks(query_part, local[0], local[1], glob[0], glob[1], valid)
        return mixed.reshape(group_blocks * BLOCK, width)

    attended = lax.map(
        one_group, jnp.arange(local_blocks // group_blocks, dtype=jnp.int32)
    ).reshape(rows, width)
    summed = jnp.dot(
        lax.all_gather(attended, "head", axis=1, tiled=True),
        out_weight,
        preferred_element_type=jnp.float32,
    )
    return summed.astype(jnp.bfloat16)


def solution(mesh):
    body = halves_body if dict(mesh.shape) == {"seq": 8, "head": 4} else exchange_body
    in_specs = (P("seq", "head"), P(None, "seq", "head"), P(), P(), P(None, "head"))
    out_specs = P("seq", "head")
    return jax.shard_map(body, mesh=mesh, in_specs=in_specs, out_specs=out_specs, check_vma=False)
```

```python
import functools

import jax
import jax.numpy as jnp
from jax import lax
from jax.experimental import pallas as pl
from jax.experimental.pallas import tpu as pltpu
from jax.sharding import PartitionSpec as P

HEAD_DIM = 128
BLOCK = 64
NGLOBAL = 2
NRANDOM = 3
NLIST = 3 + NGLOBAL + NRANDOM
MASKED = -1e30
EXP2_SCALE = 1.4426950408889634 / HEAD_DIM**0.5
STAT_TILE = 16
VMEM_LIMIT = 32 * 1024 * 1024
PROJECT_LIMIT = 32 * 1024 * 1024


group_blocks = 8


def eye_mask():
    rows = lax.broadcasted_iota(jnp.int32, (BLOCK, BLOCK), 0)
    columns = lax.broadcasted_iota(jnp.int32, (BLOCK, BLOCK), 1)
    return rows == columns


def attend_group(blocks, head, starts_ref, bias_ref, q_ref, pool):
    lanes = pl.ds(head * HEAD_DIM, HEAD_DIM)
    listed = [
        [
            pl.ds(pl.multiple_of(starts_ref[i * NLIST + e], BLOCK), BLOCK)
            for e in range(NLIST)
        ]
        for i in blocks
    ]
    places = [pl.ds(pl.multiple_of(i * BLOCK, BLOCK), BLOCK) for i in blocks]
    scores = []
    for i, rows, listing in zip(blocks, places, listed):
        keys = jnp.concatenate([pool[0, w, lanes] for w in listing], axis=0)
        product = lax.dot_general(
            q_ref[rows, lanes],
            keys,
            (((1,), (1,)), ((), ())),
            preferred_element_type=jnp.float32,
        )
        scores.append(product + bias_ref[pl.ds(i, 1), :])
    weighed = []
    for score in scores:
        highest = jnp.max(score, axis=1, keepdims=True)
        weights = jnp.exp2((score - highest) * EXP2_SCALE)
        total = jnp.sum(weights, axis=1, keepdims=True)
        weighed.append((weights.astype(jnp.bfloat16), highest, total))
    results = []
    for listing, (weights, highest, total) in zip(listed, weighed):
        values = jnp.concatenate([pool[1, w, lanes] for w in listing], axis=0)
        mixed = jnp.dot(weights, values, preferred_element_type=jnp.float32)
        results.append((lanes, mixed, highest, total))
    return results


def put_stats(i, head, stats_ref, highest, total):
    eye = eye_mask()
    high_row = jnp.sum(jnp.where(eye, highest, 0.0), axis=0, keepdims=True)
    total_row = jnp.sum(jnp.where(eye, total, 0.0), axis=0, keepdims=True)
    stats_ref[head, pl.ds(i, 1), :] = jnp.concatenate([high_row, total_row], axis=1)


def load_pool(parts, pool, sems):
    size = parts[0].shape[1]
    copies = [
        pltpu.make_async_copy(part, pool.at[:, pl.ds(n * size, size), :], sems.at[n])
        for n, part in enumerate(parts)
    ]
    for copy in copies:
        copy.start()
    for copy in copies:
        copy.wait()


def attend_part(part, parts, starts_ref, bias_ref, q_ref, pool, mixed_ref, stats_ref, normalise):
    blocks = q_ref.shape[0] // BLOCK // parts
    unroll = UNROLL if blocks % UNROLL == 0 else blocks
    stats_ref[...] = jnp.zeros_like(stats_ref)

    for head in range(q_ref.shape[1] // HEAD_DIM):

        def step(n, _):
            ids = [n * unroll + u for u in range(unroll)]
            results = attend_group(
                [part * blocks + i for i in ids], head, starts_ref, bias_ref, q_ref, pool
            )
            for i, (lanes, mixed, highest, total) in zip(ids, results):
                rows = pl.ds(pl.multiple_of(i * BLOCK, BLOCK), BLOCK)
                mixed = mixed / total if normalise else mixed
                mixed_ref[rows, lanes] = mixed.astype(mixed_ref.dtype)
                put_stats(i, head, stats_ref, highest, total)
            return 0

        lax.fori_loop(0, blocks // unroll, step, 0)


def guest_kernel(parts, starts_ref, bias_ref, q_ref, p0, p1, p2, p3, *refs):
    *message_refs, pool, stats, sems = refs
    load_pool((p0, p1, p2, p3), pool, sems)
    base = q_ref.shape[0] // parts
    for part, message_ref in enumerate(message_refs):
        attend_part(part, parts, starts_ref, bias_ref, q_ref, pool, message_ref, stats, True)
        for head in range(q_ref.shape[1] // HEAD_DIM):
            rest = stats[head]
            for n in range(3):
                piece = rest.astype(jnp.bfloat16)
                rows = pl.ds(base + n * rest.shape[0], rest.shape[0])
                message_ref[rows, pl.ds(head * HEAD_DIM, HEAD_DIM)] = piece
                rest = rest - piece.astype(jnp.float32)


def home_kernel(parts, starts_ref, bias_ref, q_ref, p0, p1, p2, p3, *refs):
    *result_refs, pool, sems = refs
    load_pool((p0, p1, p2, p3), pool, sems)
    for part in range(parts):
        mixed_ref, stats_ref = result_refs[2 * part : 2 * part + 2]
        attend_part(part, parts, starts_ref, bias_ref, q_ref, pool, mixed_ref, stats_ref, False)


def merge_kernel(mixed_ref, stats_ref, message_ref, out_ref, home_scale, guest_scale):
    base, width = mixed_ref.shape
    blocks = base // BLOCK
    size = stats_ref.shape[1]
    other = message_ref[pl.ds(base, size), :].astype(jnp.float32)
    for n in (1, 2):
        other = other + message_ref[pl.ds(base + n * size, size), :].astype(jnp.float32)
    eye = eye_mask()
    for head in range(width // HEAD_DIM):
        low = head * HEAD_DIM
        lanes = pl.ds(low, HEAD_DIM)
        high_h = stats_ref[head, :, :BLOCK]
        total_h = stats_ref[head, :, BLOCK:]
        high_g = other[:, low : low + BLOCK]
        total_g = other[:, low + BLOCK : low + HEAD_DIM]
        highest = jnp.maximum(high_h, high_g)
        factor_h = jnp.exp2((high_h - highest) * EXP2_SCALE)
        factor_g = jnp.exp2((high_g - highest) * EXP2_SCALE) * total_g
        total = factor_h * total_h + factor_g
        total = jnp.where(total > 0, total, 1.0)
        home_scale[...] = factor_h / total
        guest_scale[...] = factor_g / total

        def step(i, _):
            rows = pl.ds(pl.multiple_of(i * BLOCK, BLOCK), BLOCK)
            scale_h = jnp.sum(
                jnp.where(eye, home_scale[pl.ds(i, 1), :], 0.0), axis=1, keepdims=True
            )
            scale_g = jnp.sum(
                jnp.where(eye, guest_scale[pl.ds(i, 1), :], 0.0), axis=1, keepdims=True
            )
            mixed = (
                mixed_ref[rows, lanes] * scale_h
                + message_ref[rows, lanes].astype(jnp.float32) * scale_g
            )
            out_ref[rows, lanes] = mixed.astype(jnp.bfloat16)
            return 0

        lax.fori_loop(0, blocks, step, 0, unroll=4)


def project_kernel(heads, me_ref, w_ref, *refs):
    groups = w_ref.shape[0]
    *x_refs, out_ref = refs
    total = None
    for relation in range(groups):
        pieces = [x_refs[head * groups + relation][...] for head in range(heads)]
        weight = w_ref[me_ref[0] ^ relation].reshape(-1, w_ref.shape[-1])
        term = jnp.dot(
            jnp.concatenate(pieces, axis=1), weight, preferred_element_type=jnp.float32
        )
        total = term if total is None else total + term
    out_ref[...] = total.astype(out_ref.dtype)


VMEM = pl.BlockSpec(memory_space=pltpu.VMEM)
SMEM = pl.BlockSpec(memory_space=pltpu.SMEM)
ANY = pl.BlockSpec(memory_space=pl.ANY)


def params():
    return pltpu.CompilerParams(vmem_limit_bytes=VMEM_LIMIT)


def pool_scratch(query):
    return pltpu.VMEM((2, 4 * query.shape[0], query.shape[1]), jnp.bfloat16)


def stats_shape(query, parts, kind):
    blocks = query.shape[0] // BLOCK // parts
    size = -(-blocks // STAT_TILE) * STAT_TILE
    return kind((query.shape[1] // HEAD_DIM, size, 2 * BLOCK), jnp.float32)


def cost(micros):
    return pl.CostEstimate(flops=int(micros * 1.15e9), bytes_accessed=0, transcendentals=0)


def guest_call(starts, bias, query, pieces, parts=1):
    rows, width = query.shape
    size = stats_shape(query, parts, jax.ShapeDtypeStruct).shape[1]
    message = jax.ShapeDtypeStruct((rows // parts + 3 * size, width), jnp.bfloat16)
    return pl.pallas_call(
        functools.partial(guest_kernel, parts),
        out_shape=[message] * parts,
        in_specs=[SMEM, VMEM, VMEM, ANY, ANY, ANY, ANY],
        out_specs=[VMEM] * parts,
        scratch_shapes=[
            pool_scratch(query),
            stats_shape(query, parts, pltpu.VMEM),
            pltpu.SemaphoreType.DMA((4,)),
        ],
        compiler_params=params(),
        cost_estimate=cost(GUEST_US),
        name="guest_attention",
    )(starts, bias, query, *pieces)


def home_call(starts, bias, query, pieces, parts=1):
    rows, width = query.shape
    results = [
        jax.ShapeDtypeStruct((rows // parts, width), jnp.float32),
        stats_shape(query, parts, jax.ShapeDtypeStruct),
    ]
    return pl.pallas_call(
        functools.partial(home_kernel, parts),
        out_shape=results * parts,
        in_specs=[SMEM, VMEM, VMEM, ANY, ANY, ANY, ANY],
        out_specs=[VMEM] * (2 * parts),
        scratch_shapes=[pool_scratch(query), pltpu.SemaphoreType.DMA((4,))],
        compiler_params=params(),
        cost_estimate=cost(0),
        name="home_attention",
    )(starts, bias, query, *pieces)


def merge_call(mixed, stats, message):
    return pl.pallas_call(
        merge_kernel,
        out_shape=jax.ShapeDtypeStruct(mixed.shape, jnp.bfloat16),
        in_specs=[VMEM, VMEM, VMEM],
        out_specs=VMEM,
        scratch_shapes=[
            pltpu.VMEM((stats.shape[1], BLOCK), jnp.float32),
            pltpu.VMEM((stats.shape[1], BLOCK), jnp.float32),
        ],
        compiler_params=params(),
        cost_estimate=cost(0),
        name="merge_halves",
    )(mixed, stats, message)


ROW_TILE = 256


def project(pieces, weights, part, filled=None):
    groups, heads, _, columns = weights.shape
    number, parts = part
    rows = pieces[0].shape[0]
    tiles = rows // parts // ROW_TILE

    def row_spec(height, width):
        first = number * tiles if height == rows else 0
        return pl.BlockSpec((ROW_TILE, width), lambda i, me: (i + first, 0))

    others = [] if filled is None else [filled]
    myself = lax.axis_index("head").astype(jnp.int32).reshape(1)

    def kernel(me_ref, w_ref, *refs):
        x_refs = refs[: len(pieces)]
        project_kernel(heads, me_ref, w_ref, *x_refs, refs[-1])

    return pl.pallas_call(
        kernel,
        out_shape=jax.ShapeDtypeStruct((rows, columns), jnp.bfloat16),
        grid_spec=pltpu.PrefetchScalarGridSpec(
            num_scalar_prefetch=1,
            grid=(tiles,),
            in_specs=[VMEM] + [row_spec(*v.shape) for v in pieces] + [ANY] * len(others),
            out_specs=row_spec(rows, columns),
        ),
        input_output_aliases={2 + len(pieces): 0} if others else {},
        compiler_params=params(),
        cost_estimate=cost(PROJECT_US),
        name="project_rows",
    )(myself, weights, *pieces, *others)


def key_places(shard, myself, global_ids, rand_ids, local_blocks, shards):
    half = shards // 2
    total_blocks = local_blocks * shards
    block_ids = shard * local_blocks + jnp.arange(local_blocks, dtype=jnp.int32)
    near = block_ids[:, None] + jnp.arange(-1, 2, dtype=jnp.int32)[None, :]
    inside = (near >= 0) & (near < total_blocks)
    listed = lax.dynamic_slice_in_dim(rand_ids, shard * local_blocks, local_blocks, 0)
    glob = jnp.broadcast_to(global_ids[None, :], (local_blocks, NGLOBAL))
    ids = jnp.concatenate([jnp.clip(near, 0, total_blocks - 1), glob, listed], axis=1)
    owner = ids // local_blocks
    here = (owner // half) == (myself // half)
    here = here & jnp.concatenate(
        [inside, jnp.ones((local_blocks, NGLOBAL + NRANDOM), jnp.bool_)], axis=1
    )
    relative = (owner ^ myself) & (half - 1)
    starts = jnp.where(here, (relative * local_blocks + ids % local_blocks) * BLOCK, 0)
    bias = jnp.repeat(jnp.where(here, 0.0, MASKED).astype(jnp.float32), BLOCK, axis=1)
    return starts.reshape(-1).astype(jnp.int32), bias


def swap(value, distance, shards):
    return lax.ppermute(value, "seq", [(i, i ^ distance) for i in range(shards)])


def after(value, *tokens):
    return lax.optimization_barrier((value, *tokens))[0]


def hop(value, distance, groups):
    return lax.ppermute(value, "head", [(i, i ^ distance) for i in range(groups)])


def together(*values):
    return lax.optimization_barrier(values)


UNROLL = 8
GUEST_US = 0.1
PROJECT_US = 4


def halves_body(queries, keys_values, global_ids, rand_ids, out_weight):
    rows, width = queries.shape
    heads_here = width // HEAD_DIM
    local_blocks = rows // BLOCK
    shards = lax.axis_size("seq")
    myself = lax.axis_index("seq")
    groups = lax.axis_size("head")
    opposite = shards // 2

    def column(array, head):
        return lax.slice_in_dim(array, head * HEAD_DIM, (head + 1) * HEAD_DIM, axis=array.ndim - 1)

    def over_y(value):
        return swap(value, 1, shards)

    def over_z(value):
        return swap(value, 2, shards)

    def across(value):
        return swap(value, opposite, shards)

    home = key_places(myself, myself, global_ids, rand_ids, local_blocks, shards)
    guest = key_places(myself ^ opposite, myself, global_ids, rand_ids, local_blocks, shards)
    weights = out_weight.reshape(groups, heads_here, HEAD_DIM, out_weight.shape[1])
    k0, k1, k2, k3 = [column(keys_values, h) for h in range(heads_here)]
    q0, q1, q2, q3 = [column(queries, h) for h in range(heads_here)]

    y0, z0 = over_y(k0), over_z(k0)
    y0, z0, k1_, v0, v1, home, guest = together(y0, z0, k1, q0, q1, home, guest)

    d0, y1, z1, v0, v1 = over_y(z0), over_y(k1_), over_z(k1_), across(v0), across(v1)
    p0 = (k0, y0, z0, d0)
    (s0,) = guest_call(*guest, v0, p0)
    s0, y1, z1, v1, k2_, v2 = together(s0, y1, z1, v1, k2, q2)

    d1, y2, z2, v2, g0 = over_y(z1), over_y(k2_), over_z(k2_), across(v2), across(s0)
    m0 = home_call(*home, after(q0, s0), p0)
    p1 = (k1, y1, z1, d1)
    (s1,) = guest_call(*guest, after(v1, m0[1], v2), p1)
    s1, y2, z2, v2, g0, k3_, v3 = together(s1, y2, z2, v2, g0, k3, q3)

    d2, y3, z3, v3, g1 = over_y(z2), over_y(k3_), over_z(k3_), across(v3), across(s1)
    m1 = home_call(*home, after(q1, s1), p1)
    a0 = merge_call(*m0, after(g0, m1[1]))
    a0x, a0c = hop(a0, 2, groups), hop(a0, 1, groups)
    p2 = (k2, y2, z2, d2)
    (s2,) = guest_call(*guest, after(v2, m1[1], v3), p2)
    s2, y3, z3, v3, g1, a0x, a0c = together(s2, y3, z3, v3, g1, a0x, a0c)

    d3, g2 = over_y(z3), across(s2)
    m2 = home_call(*home, after(q2, s2), p2)
    a1 = merge_call(*m1, after(g1, m2[1]))
    a1x, a1c, a0d = hop(a1, 2, groups), hop(a1, 1, groups), hop(a0x, 1, groups)
    p3 = (k3, y3, z3, d3)
    s3a, s3b = guest_call(*guest, after(v3, a1), p3, 2)
    s3a, s3b, g2, a1x, a1c, a0d = together(s3a, s3b, g2, a1x, a1c, a0d)

    g3a, g3b = across(s3a), across(s3b)
    m3 = home_call(*home, after(q3, s3a), p3, 2)
    a2 = merge_call(*m2, after(g2, s3a))
    a1d = hop(a1x, 1, groups)
    a2x, a2c = hop(a2, 2, groups), hop(a2, 1, groups)
    a2d = hop(a2x, 1, groups)
    whole = (a0, a0c, a0x, a0d, a1, a1c, a1x, a1d, a2, a2c, a2x, a2d)
    a3a = merge_call(*m3[:2], after(g3a, a2))
    a3ax, a3ac = hop(a3a, 2, groups), hop(a3a, 1, groups)
    a3b = merge_call(*m3[2:], after(g3b, a3a))
    a3bx, a3bc = hop(a3b, 2, groups), hop(a3b, 1, groups)
    a3ad = hop(a3ax, 1, groups)
    upper = project((*whole, after(a3a, a3b), a3ac, a3ax, a3ad), weights, (0, 2))
    a3bd = hop(after(a3bx, upper), 1, groups)
    return project((*whole, a3b, a3bc, a3bx, a3bd), weights, (1, 2), upper)


def padded_2(block, sides, width):
    for axis, dim in sides:
        count = lax.axis_size(axis)
        forward = [(i, i + 1) for i in range(count - 1)]
        backward = [(target, source) for source, target in forward]
        low = lax.ppermute(
            lax.slice_in_dim(block, block.shape[dim] - width, None, axis=dim), axis, forward
        )
        high = lax.ppermute(lax.slice_in_dim(block, 0, width, axis=dim), axis, backward)
        block = jnp.concatenate([low, block, high], axis=dim)
    return block


def broadcast(block, axis, owner):
    block = jnp.where(lax.axis_index(axis) == owner, block, jnp.zeros_like(block))
    return lax.psum(block, axis)


def plan_slots(requests, myself, capacity, per_shard):
    sources = requests // per_shard
    offsets = requests % per_shard
    count = requests.shape[1]
    order = jnp.arange(count, dtype=jnp.int32)
    earlier = (order[:, None] < order[None, :]).astype(jnp.int32)
    matches = (sources[:, :, None] == sources[:, None, :]).astype(jnp.int32)
    ranks = jnp.sum(matches * earlier[None], axis=1)
    slot_range = jnp.arange(capacity, dtype=jnp.int32)
    wanted = (
        (sources == myself)[:, None, :] & (ranks[:, None, :] == slot_range[None, :, None])
    ).astype(jnp.int32)
    chosen = jnp.sum(wanted * offsets[:, None, :], axis=2).reshape(-1)
    own_sources = lax.dynamic_index_in_dim(sources, myself, 0, keepdims=False)
    own_ranks = lax.dynamic_index_in_dim(ranks, myself, 0, keepdims=False)
    return (chosen, own_sources * capacity + own_ranks)


def attend_blocks(query_part, local_keys, local_values, glob_keys, glob_values, valid):
    scale = 1.0 / HEAD_DIM**0.5
    near_scores = (
        jnp.einsum("bqhd,bkhd->bhqk", query_part, local_keys, preferred_element_type=jnp.float32)
        * scale
    )
    near_scores = jnp.where(valid[:, None, None, :], near_scores, -jnp.inf)
    glob_scores = (
        jnp.einsum("bqhd,khd->bhqk", query_part, glob_keys, preferred_element_type=jnp.float32)
        * scale
    )
    highest = jnp.maximum(jnp.max(near_scores, axis=-1), jnp.max(glob_scores, axis=-1))
    near_exp = jnp.exp(near_scores - highest[..., None])
    glob_exp = jnp.exp(glob_scores - highest[..., None])
    total = jnp.sum(near_exp, axis=-1) + jnp.sum(glob_exp, axis=-1)
    near_weights = (near_exp / total[..., None]).astype(jnp.bfloat16)
    glob_weights = (glob_exp / total[..., None]).astype(jnp.bfloat16)
    mixed = jnp.einsum(
        "bhqk,bkhd->bqhd", near_weights, local_values, preferred_element_type=jnp.float32
    )
    mixed = mixed + jnp.einsum(
        "bhqk,khd->bqhd", glob_weights, glob_values, preferred_element_type=jnp.float32
    )
    return mixed.astype(jnp.bfloat16)


def exchange_body(queries, keys_values, global_ids, rand_ids, out_weight):
    rows = queries.shape[0]
    width = queries.shape[1]
    heads_here = width // HEAD_DIM
    local_blocks = rows // BLOCK
    shards = lax.axis_size("seq")
    myself = lax.axis_index("seq")
    total_blocks = local_blocks * shards
    pair_blocks = keys_values.reshape(2, local_blocks, BLOCK, width)
    padded = padded_2(keys_values, (("seq", 1),), BLOCK)
    padded = padded.reshape(2, local_blocks + 2, BLOCK, width)
    panel_list = []
    for which in range(NGLOBAL):
        target = global_ids[which]
        owner = target // local_blocks
        local_panel = lax.dynamic_index_in_dim(
            pair_blocks, target % local_blocks, 1, keepdims=False
        )
        panel_list.append(broadcast(local_panel, "seq", owner))
    glob = jnp.stack(panel_list, axis=1).reshape(2, NGLOBAL * BLOCK, heads_here, HEAD_DIM)
    requests = rand_ids.reshape(shards, local_blocks, NRANDOM)
    capacity = (local_blocks + shards - 1) // shards
    fetched = []
    for column in range(NRANDOM):
        chosen, slots = plan_slots(requests[:, :, column], myself, capacity, local_blocks)
        outgoing = jnp.take(pair_blocks, chosen, axis=1)
        incoming = lax.all_to_all(outgoing, "seq", split_axis=1, concat_axis=1, tiled=True)
        fetched.append(jnp.take(incoming, slots, axis=1))
    remote = jnp.stack(fetched, axis=2)
    segment = jnp.arange((3 + NRANDOM) * BLOCK, dtype=jnp.int32) // BLOCK

    def one_group(index):
        first = index * group_blocks
        query_part = lax.dynamic_slice_in_dim(queries, first * BLOCK, group_blocks * BLOCK, 0)
        query_part = query_part.reshape(group_blocks, BLOCK, heads_here, HEAD_DIM)
        window = lax.dynamic_slice_in_dim(padded, first, group_blocks + 2, 1)
        farther = lax.dynamic_slice_in_dim(remote, first, group_blocks, 1)
        farther = farther.reshape(2, group_blocks, NRANDOM * BLOCK, width)
        local = jnp.concatenate(
            [
                window[:, 0:group_blocks],
                window[:, 1 : group_blocks + 1],
                window[:, 2 : group_blocks + 2],
                farther,
            ],
            axis=2,
        )
        local = local.reshape(2, group_blocks, (3 + NRANDOM) * BLOCK, heads_here, HEAD_DIM)
        block_ids = myself * local_blocks + first + jnp.arange(group_blocks, dtype=jnp.int32)
        drop_before = (segment[None, :] == 0) & (block_ids[:, None] == 0)
        drop_after = (segment[None, :] == 2) & (block_ids[:, None] == total_blocks - 1)
        valid = jnp.logical_not(drop_before | drop_after)
        mixed = attend_blocks(query_part, local[0], local[1], glob[0], glob[1], valid)
        return mixed.reshape(group_blocks * BLOCK, width)

    attended = lax.map(
        one_group, jnp.arange(local_blocks // group_blocks, dtype=jnp.int32)
    ).reshape(rows, width)
    summed = jnp.dot(
        lax.all_gather(attended, "head", axis=1, tiled=True),
        out_weight,
        preferred_element_type=jnp.float32,
    )
    return summed.astype(jnp.bfloat16)


def solution(mesh):
    body = halves_body if dict(mesh.shape) == {"seq": 8, "head": 4} else exchange_body
    in_specs = (P("seq", "head"), P(None, "seq", "head"), P(), P(), P(None, "head"))
    out_specs = P("seq", "head")
    return jax.shard_map(body, mesh=mesh, in_specs=in_specs, out_specs=out_specs, check_vma=False)
```

```python
import functools

import jax
import jax.numpy as jnp
from jax import lax
from jax.experimental import pallas as pl
from jax.experimental.pallas import tpu as pltpu
from jax.sharding import PartitionSpec as P

HEAD_DIM = 128
BLOCK = 64
NGLOBAL = 2
NRANDOM = 3
NLIST = 3 + NGLOBAL + NRANDOM
MASKED = -1e30
EXP2_SCALE = 1.4426950408889634 / HEAD_DIM**0.5
STAT_TILE = 16
VMEM_LIMIT = 14 * 1024 * 1024
PROJECT_LIMIT = 32 * 1024 * 1024


group_blocks = 8


def eye_mask():
    rows = lax.broadcasted_iota(jnp.int32, (BLOCK, BLOCK), 0)
    columns = lax.broadcasted_iota(jnp.int32, (BLOCK, BLOCK), 1)
    return rows == columns


def attend_group(blocks, head, starts_ref, bias_ref, q_ref, pool):
    lanes = pl.ds(head * HEAD_DIM, HEAD_DIM)
    listed = [
        [
            pl.ds(pl.multiple_of(starts_ref[i * NLIST + e], BLOCK), BLOCK)
            for e in range(NLIST)
        ]
        for i in blocks
    ]
    places = [pl.ds(pl.multiple_of(i * BLOCK, BLOCK), BLOCK) for i in blocks]
    scores = []
    for i, rows, listing in zip(blocks, places, listed):
        keys = jnp.concatenate([pool[0, w, lanes] for w in listing], axis=0)
        product = lax.dot_general(
            q_ref[rows, lanes],
            keys,
            (((1,), (1,)), ((), ())),
            preferred_element_type=jnp.float32,
        )
        scores.append(product + bias_ref[pl.ds(i, 1), :])
    weighed = []
    for score in scores:
        highest = jnp.max(score, axis=1, keepdims=True)
        weights = jnp.exp2((score - highest) * EXP2_SCALE)
        total = jnp.sum(weights, axis=1, keepdims=True)
        weighed.append((weights.astype(jnp.bfloat16), highest, total))
    results = []
    for listing, (weights, highest, total) in zip(listed, weighed):
        values = jnp.concatenate([pool[1, w, lanes] for w in listing], axis=0)
        mixed = jnp.dot(weights, values, preferred_element_type=jnp.float32)
        results.append((lanes, mixed, highest, total))
    return results


def put_stats(i, head, stats_ref, highest, total):
    eye = eye_mask()
    high_row = jnp.sum(jnp.where(eye, highest, 0.0), axis=0, keepdims=True)
    total_row = jnp.sum(jnp.where(eye, total, 0.0), axis=0, keepdims=True)
    stats_ref[head, pl.ds(i, 1), :] = jnp.concatenate([high_row, total_row], axis=1)


def load_pool(parts, pool, sems):
    copies, low = [], 0
    for n, part in enumerate(parts):
        size = part.shape[1]
        copies.append(
            pltpu.make_async_copy(part, pool.at[:, pl.ds(low, size), :], sems.at[n])
        )
        low += size
    for copy in copies:
        copy.start()
    for copy in copies:
        copy.wait()


def attend_part(part, parts, starts_ref, bias_ref, q_ref, pool, mixed_ref, stats_ref, normalise):
    blocks = q_ref.shape[0] // BLOCK // parts
    unroll = UNROLL if blocks % UNROLL == 0 else blocks
    stats_ref[...] = jnp.zeros_like(stats_ref)

    for head in range(q_ref.shape[1] // HEAD_DIM):

        def step(n, _):
            ids = [n * unroll + u for u in range(unroll)]
            results = attend_group(
                [part * blocks + i for i in ids], head, starts_ref, bias_ref, q_ref, pool
            )
            for i, (lanes, mixed, highest, total) in zip(ids, results):
                rows = pl.ds(pl.multiple_of(i * BLOCK, BLOCK), BLOCK)
                mixed = mixed / total if normalise else mixed
                mixed_ref[rows, lanes] = mixed.astype(mixed_ref.dtype)
                put_stats(i, head, stats_ref, highest, total)
            return 0

        lax.fori_loop(0, blocks // unroll, step, 0)


def guest_kernel(parts, count, starts_ref, bias_ref, q_ref, *refs):
    *message_refs, pool, stats, sems = refs[count:]
    load_pool(refs[:count], pool, sems)
    base = q_ref.shape[0] // parts
    for part, message_ref in enumerate(message_refs):
        attend_part(part, parts, starts_ref, bias_ref, q_ref, pool, message_ref, stats, True)
        for head in range(q_ref.shape[1] // HEAD_DIM):
            rest = stats[head]
            for n in range(3):
                piece = rest.astype(jnp.bfloat16)
                rows = pl.ds(base + n * rest.shape[0], rest.shape[0])
                message_ref[rows, pl.ds(head * HEAD_DIM, HEAD_DIM)] = piece
                rest = rest - piece.astype(jnp.float32)


def home_kernel(parts, count, starts_ref, bias_ref, q_ref, *refs):
    *result_refs, pool, sems = refs[count:]
    load_pool(refs[:count], pool, sems)
    for part in range(parts):
        mixed_ref, stats_ref = result_refs[2 * part : 2 * part + 2]
        attend_part(part, parts, starts_ref, bias_ref, q_ref, pool, mixed_ref, stats_ref, False)


def merge_kernel(mixed_ref, stats_ref, message_ref, *refs):
    *out_refs, home_scale, guest_scale = refs
    base, width = mixed_ref.shape
    blocks = base // BLOCK
    size = stats_ref.shape[1]
    other = message_ref[pl.ds(base, size), :].astype(jnp.float32)
    for n in (1, 2):
        other = other + message_ref[pl.ds(base + n * size, size), :].astype(jnp.float32)
    eye = eye_mask()
    for head in range(width // HEAD_DIM):
        low = head * HEAD_DIM
        lanes = pl.ds(low, HEAD_DIM)
        high_h = stats_ref[head, :, :BLOCK]
        total_h = stats_ref[head, :, BLOCK:]
        high_g = other[:, low : low + BLOCK]
        total_g = other[:, low + BLOCK : low + HEAD_DIM]
        highest = jnp.maximum(high_h, high_g)
        factor_h = jnp.exp2((high_h - highest) * EXP2_SCALE)
        factor_g = jnp.exp2((high_g - highest) * EXP2_SCALE) * total_g
        total = factor_h * total_h + factor_g
        total = jnp.where(total > 0, total, 1.0)
        home_scale[...] = factor_h / total
        guest_scale[...] = factor_g / total

        def step(n, part):
            i = part * (blocks // len(out_refs)) + n
            rows = pl.ds(pl.multiple_of(i * BLOCK, BLOCK), BLOCK)
            scale_h = jnp.sum(
                jnp.where(eye, home_scale[pl.ds(i, 1), :], 0.0), axis=1, keepdims=True
            )
            scale_g = jnp.sum(
                jnp.where(eye, guest_scale[pl.ds(i, 1), :], 0.0), axis=1, keepdims=True
            )
            mixed = (
                mixed_ref[rows, lanes] * scale_h
                + message_ref[rows, lanes].astype(jnp.float32) * scale_g
            )
            rows = pl.ds(pl.multiple_of(n * BLOCK, BLOCK), BLOCK)
            out_refs[part][rows, lanes] = mixed.astype(jnp.bfloat16)

        for part in range(len(out_refs)):

            def body(n, _, part=part):
                step(n, part)
                return 0

            lax.fori_loop(0, blocks // len(out_refs), body, 0, unroll=4)


def project_kernel(heads, given, filled, me_ref, w_ref, *refs):
    *x_refs, out_ref, held, sem = refs
    groups = w_ref.shape[0]
    sum_ref = x_refs.pop(0) if given else None
    if filled:
        x_refs.pop()

    @pl.when(pl.program_id(0) == 0)
    def _():
        copies = [
            pltpu.make_async_copy(
                w_ref.at[me_ref[0] ^ relation, pl.ds(heads[0], len(heads))],
                held.at[relation],
                sem.at[relation],
            )
            for relation in range(groups)
        ]
        for copy in copies:
            copy.start()
        for copy in copies:
            copy.wait()

    ordered = [x_refs[h * groups + r][...] for r in range(groups) for h in range(len(heads))]
    weight = held[...].reshape(-1, held.shape[-1])
    total = jnp.dot(
        jnp.concatenate(ordered, axis=1), weight, preferred_element_type=jnp.float32
    )
    if given:
        total = total + sum_ref[...]
    out_ref[...] = total.astype(out_ref.dtype)


VMEM = pl.BlockSpec(memory_space=pltpu.VMEM)
SMEM = pl.BlockSpec(memory_space=pltpu.SMEM)
ANY = pl.BlockSpec(memory_space=pl.ANY)
HBM = pl.BlockSpec(memory_space=pltpu.HBM)


def params():
    return pltpu.CompilerParams(vmem_limit_bytes=VMEM_LIMIT)


def pool_scratch(query):
    return pltpu.VMEM((2, 4 * query.shape[0], query.shape[1]), jnp.bfloat16)


def stats_shape(query, parts, kind):
    blocks = query.shape[0] // BLOCK // parts
    size = -(-blocks // STAT_TILE) * STAT_TILE
    return kind((query.shape[1] // HEAD_DIM, size, 2 * BLOCK), jnp.float32)


def cost(micros):
    return pl.CostEstimate(flops=int(micros * 1.15e9), bytes_accessed=0, transcendentals=0)


def guest_call(starts, bias, query, pieces, parts=1):
    rows, width = query.shape
    size = stats_shape(query, parts, jax.ShapeDtypeStruct).shape[1]
    message = jax.ShapeDtypeStruct((rows // parts + 3 * size, width), jnp.bfloat16)
    return pl.pallas_call(
        functools.partial(guest_kernel, parts, len(pieces)),
        out_shape=[message] * parts,
        in_specs=[SMEM, VMEM, VMEM] + [ANY] * len(pieces),
        out_specs=[VMEM] * parts,
        scratch_shapes=[
            pool_scratch(query),
            stats_shape(query, parts, pltpu.VMEM),
            pltpu.SemaphoreType.DMA((len(pieces),)),
        ],
        compiler_params=params(),
        cost_estimate=cost(GUEST_US),
        name="guest_attention",
    )(starts, bias, query, *pieces)


def home_call(starts, bias, query, pieces, parts=1):
    rows, width = query.shape
    results = [
        jax.ShapeDtypeStruct((rows // parts, width), jnp.float32),
        stats_shape(query, parts, jax.ShapeDtypeStruct),
    ]
    return pl.pallas_call(
        functools.partial(home_kernel, parts, len(pieces)),
        out_shape=results * parts,
        in_specs=[SMEM, VMEM, VMEM] + [ANY] * len(pieces),
        out_specs=[VMEM] * (2 * parts),
        scratch_shapes=[pool_scratch(query), pltpu.SemaphoreType.DMA((len(pieces),))],
        compiler_params=params(),
        cost_estimate=cost(0),
        name="home_attention",
    )(starts, bias, query, *pieces)


def merge_call(mixed, stats, message, parts=1):
    rows, width = mixed.shape
    result = jax.ShapeDtypeStruct((rows // parts, width), jnp.bfloat16)
    return pl.pallas_call(
        merge_kernel,
        out_shape=[result] * parts,
        in_specs=[VMEM, VMEM, VMEM],
        out_specs=[VMEM] * parts,
        scratch_shapes=[
            pltpu.VMEM((stats.shape[1], BLOCK), jnp.float32),
            pltpu.VMEM((stats.shape[1], BLOCK), jnp.float32),
        ],
        compiler_params=params(),
        cost_estimate=cost(0),
        name="merge_halves",
    )(mixed, stats, message)


ROW_TILE = 256


def project(name, summed, gathered, heads, weights, result, rows, part=(0, 1), filled=None):
    groups, _, depth, columns = weights.shape
    number, parts = part
    tiles = rows // parts // ROW_TILE

    def row_spec(height, width):
        first = number * tiles if height == rows else 0
        return pl.BlockSpec((ROW_TILE, width), lambda i, me: (i + first, 0))

    pieces = [piece for group in gathered for piece in group]
    sums = [] if summed is None else [summed]
    others = [] if filled is None else [filled]
    myself = lax.axis_index("head").astype(jnp.int32).reshape(1)
    return pl.pallas_call(
        functools.partial(project_kernel, heads, summed is not None, filled is not None),
        out_shape=jax.ShapeDtypeStruct((rows, columns), result),
        grid_spec=pltpu.PrefetchScalarGridSpec(
            num_scalar_prefetch=1,
            grid=(tiles,),
            in_specs=[HBM] + [row_spec(*v.shape) for v in sums + pieces] + [ANY] * len(others),
            out_specs=row_spec(rows, columns),
            scratch_shapes=[
                pltpu.VMEM((groups, len(heads), depth, columns), weights.dtype),
                pltpu.SemaphoreType.DMA((groups,)),
            ],
        ),
        input_output_aliases={2 + len(sums) + len(pieces): 0} if others else {},
        compiler_params=params(),
        cost_estimate=cost(PROJECT_US),
        name=name,
    )(myself, weights, *sums, *pieces, *others)


def first_terms_kernel(heads, me_ref, w_ref, *refs):
    *x_refs, out_ref, held, columns, sems = refs
    groups = w_ref.shape[0]
    copies = []
    for relation in range(groups):
        copies.append(
            pltpu.make_async_copy(
                w_ref.at[me_ref[0] ^ relation, pl.ds(0, heads)], held.at[relation], sems.at[relation]
            )
        )
    for relation in range(groups):
        for head in range(heads):
            place = relation * heads + head
            copies.append(
                pltpu.make_async_copy(
                    x_refs[head * groups + relation],
                    columns.at[:, pl.ds(place * HEAD_DIM, HEAD_DIM)],
                    sems.at[groups + place],
                )
            )
    for copy in copies:
        copy.start()
    for copy in copies:
        copy.wait()
    weight = held[...].reshape(-1, held.shape[-1])

    def step(i, _):
        rows = pl.ds(pl.multiple_of(i * ROW_TILE, ROW_TILE), ROW_TILE)
        out_ref[rows, :] = jnp.dot(
            columns[rows, :], weight, preferred_element_type=jnp.float32
        )
        return 0

    lax.fori_loop(0, out_ref.shape[0] // ROW_TILE, step, 0)


def first_terms(gathered, weights):
    groups, _, depth, width = weights.shape
    heads = len(gathered)
    pieces = [piece for group in gathered for piece in group]
    rows = pieces[0].shape[0]
    myself = lax.axis_index("head").astype(jnp.int32).reshape(1)
    return pl.pallas_call(
        functools.partial(first_terms_kernel, heads),
        out_shape=jax.ShapeDtypeStruct((rows, width), jnp.float32),
        in_specs=[SMEM] + [HBM] * (1 + len(pieces)),
        out_specs=VMEM,
        scratch_shapes=[
            pltpu.VMEM((groups, heads, depth, width), weights.dtype),
            pltpu.VMEM((rows, heads * groups * HEAD_DIM), jnp.bfloat16),
            pltpu.SemaphoreType.DMA((groups + len(pieces),)),
        ],
        compiler_params=params(),
        cost_estimate=cost(0),
        name="first_terms",
    )(myself, weights, *pieces)


def key_list(shard, global_ids, rand_ids, local_blocks, shards):
    total_blocks = local_blocks * shards
    block_ids = shard * local_blocks + jnp.arange(local_blocks, dtype=jnp.int32)
    near = block_ids[:, None] + jnp.arange(-1, 2, dtype=jnp.int32)[None, :]
    inside = (near >= 0) & (near < total_blocks)
    listed = lax.dynamic_slice_in_dim(rand_ids, shard * local_blocks, local_blocks, 0)
    glob = jnp.broadcast_to(global_ids[None, :], (local_blocks, NGLOBAL))
    ids = jnp.concatenate([jnp.clip(near, 0, total_blocks - 1), glob, listed], axis=1)
    inside = jnp.concatenate(
        [inside, jnp.ones((local_blocks, NGLOBAL + NRANDOM), jnp.bool_)], axis=1
    )
    return ids, inside


def guests_first(guests, source, global_ids, rand_ids, local_blocks, shards):
    ids, inside = key_list(guests, global_ids, rand_ids, local_blocks, shards)
    order = jnp.arange(local_blocks, dtype=jnp.int32)
    blocks = source * local_blocks + order
    hits = (ids[None] == blocks[:, None, None]) & inside[None]
    listed = jnp.max(hits.astype(jnp.int32), axis=(1, 2))
    earlier = (order[None, :] < order[:, None]).astype(jnp.int32)
    among = jnp.sum(earlier * listed[None, :], axis=1)
    return jnp.where(listed > 0, among, jnp.sum(listed) + order - among)


def key_places(shard, myself, global_ids, rand_ids, local_blocks, shards, diagonal=None):
    half = shards // 2
    ids, inside = key_list(shard, global_ids, rand_ids, local_blocks, shards)
    owner = ids // local_blocks
    here = ((owner // half) == (myself // half)) & inside
    relative = (owner ^ myself) & (half - 1)
    block = ids % local_blocks
    if diagonal is not None:
        order = jnp.arange(local_blocks, dtype=jnp.int32)
        moved = jnp.sum(jnp.where(block[..., None] == order, diagonal, 0), axis=-1)
        block = jnp.where(relative == half - 1, moved, block)
    starts = jnp.where(here, (relative * local_blocks + block) * BLOCK, 0)
    bias = jnp.repeat(jnp.where(here, 0.0, MASKED).astype(jnp.float32), BLOCK, axis=1)
    return starts.reshape(-1).astype(jnp.int32), bias


def split_kernel(order_ref, pair_ref, first_ref, rest_ref):
    blocks = first_ref.shape[1] // BLOCK
    for n in range(pair_ref.shape[1] // BLOCK):
        source = pl.ds(pl.multiple_of(order_ref[n] * BLOCK, BLOCK), BLOCK)
        target = first_ref if n < blocks else rest_ref
        target[:, pl.ds((n % blocks) * BLOCK, BLOCK), :] = pair_ref[:, source, :]


def split_call(order, pair):
    half = jax.ShapeDtypeStruct((2, pair.shape[1] // 2, pair.shape[2]), pair.dtype)
    return pl.pallas_call(
        split_kernel,
        out_shape=[half, half],
        in_specs=[SMEM, VMEM],
        out_specs=[VMEM, VMEM],
        compiler_params=params(),
        cost_estimate=cost(0),
        name="guests_first",
    )(order, pair)


def swap(value, distance, shards):
    return lax.ppermute(value, "seq", [(i, i ^ distance) for i in range(shards)])


def after(value, *tokens):
    return lax.optimization_barrier((value, *tokens))[0]


def hop(value, distance, groups):
    return lax.ppermute(value, "head", [(i, i ^ distance) for i in range(groups)])


def together(*values):
    return lax.optimization_barrier(values)


UNROLL = 8
GUEST_US = 0.1
PROJECT_US = 4


def halves_body(queries, keys_values, global_ids, rand_ids, out_weight):
    rows, width = queries.shape
    heads_here = width // HEAD_DIM
    local_blocks = rows // BLOCK
    shards = lax.axis_size("seq")
    myself = lax.axis_index("seq")
    groups = lax.axis_size("head")
    opposite = shards // 2

    def column(array, head):
        return lax.slice_in_dim(array, head * HEAD_DIM, (head + 1) * HEAD_DIM, axis=array.ndim - 1)

    def over_y(value):
        return swap(value, 1, shards)

    def over_z(value):
        return swap(value, 2, shards)

    def across(value):
        return swap(value, opposite, shards)

    lists = (global_ids, rand_ids, local_blocks, shards)
    mine = guests_first(myself ^ opposite, myself ^ 3, *lists)
    theirs = guests_first(myself ^ opposite ^ 1, myself ^ 2, *lists)
    count = jnp.arange(local_blocks, dtype=jnp.int32)
    order = jnp.sum(jnp.where(theirs[None, :] == count[:, None], count[None, :], 0), axis=1)
    home = key_places(myself, myself, *lists)
    guest = key_places(myself ^ opposite, myself, *lists)
    last_home = key_places(myself, myself, *lists, mine)
    last_guest = key_places(myself ^ opposite, myself, *lists, mine)
    home, guest = (*home, *last_home, order), (*guest, *last_guest)
    weights = out_weight.reshape(groups, heads_here, HEAD_DIM, out_weight.shape[1])
    k0 = column(keys_values, 0)
    others = after(keys_values, k0)
    k1, k2, k3 = [column(others, h) for h in range(1, heads_here)]
    q0, q1, q2, q3 = [column(queries, h) for h in range(heads_here)]

    y0, z0 = over_y(k0), over_z(k0)
    y0, z0, k1_, v0, v1, home, guest = together(y0, z0, k1, q0, q1, home, guest)

    d0, y1, z1, v0, v1 = over_y(z0), over_y(k1_), over_z(k1_), across(v0), across(v1)
    p0 = (k0, y0, z0, d0)
    (s0,) = guest_call(*guest[:2], v0, p0)
    s0, y1, z1, v1, k2_, v2 = together(s0, y1, z1, v1, k2, q2)

    d1, y2, z2, v2, g0 = over_y(z1), over_y(k2_), over_z(k2_), across(v2), across(s0)
    m0 = home_call(*home[:2], after(q0, s0), p0)
    p1 = (k1, y1, z1, d1)
    (s1,) = guest_call(*guest[:2], after(v1, m0[1], v2), p1)
    s1, y2, z2, v2, g0, k3_, v3 = together(s1, y2, z2, v2, g0, k3, q3)

    d2, y3, z3, v3, g1 = over_y(z2), over_y(k3_), over_z(k3_), across(v3), across(s1)
    m1 = home_call(*home[:2], after(q1, s1), p1)
    (a0,) = merge_call(*m0, after(g0, m1[1]))
    a0x, a0c = hop(a0, 2, groups), hop(a0, 1, groups)
    p2 = (k2, y2, z2, d2)
    (s2,) = guest_call(*guest[:2], after(v2, m1[1], v3), p2)
    s2, y3, z3, v3, g1, a0x, a0c = together(s2, y3, z3, v3, g1, a0x, a0c)

    first, rest = split_call(home[4], z3)
    d3, d3_, g2 = over_y(first), over_y(rest), across(s2)
    m2 = home_call(*home[:2], after(q2, s2), p2)
    (a1,) = merge_call(*m1, after(g1, m2[1]))
    a1x, a1c, a0d = hop(a1, 2, groups), hop(a1, 1, groups), hop(a0x, 1, groups)
    (s3,) = guest_call(*guest[2:4], after(v3, a1), (k3, y3, z3, d3))
    g3 = across(after(s3, g2))
    m3 = home_call(*home[2:4], after(q3, s3), (k3, y3, z3, d3, d3_))
    (a2,) = merge_call(*m2, after(g2, m3[1]))
    a1d = hop(after(a1x, s3), 1, groups)
    a2x, a2c = hop(a2, 2, groups), hop(a2, 1, groups)
    early = ((a0, a0c, a0x, a0d), (a1, a1c, a1x, a1d))
    summed = first_terms(early, after(weights, m3[1]))

    a3a, a3b = merge_call(*m3, after(g3, summed), 2)
    a3ax, a3ac = hop(a3a, 2, groups), hop(a3a, 1, groups)
    a3bx, a3bc = hop(after(a3b, a3a), 2, groups), hop(a3b, 1, groups)
    a2d = hop(after(a2x, a3b), 1, groups)
    a2 = (a2, a2c, a2x, a2d)
    a3ad = hop(a3ax, 1, groups)
    late = (a2, (a3a, a3ac, a3ax, a3ad))
    upper = project("last_terms", summed, late, (2, 3), weights, jnp.bfloat16, rows, (0, 2))
    a3bd = hop(after(a3bx, upper), 1, groups)
    late = (a2, (a3b, a3bc, a3bx, a3bd))
    return project(
        "last_terms", summed, late, (2, 3), weights, jnp.bfloat16, rows, (1, 2), upper
    )


def padded_2(block, sides, width):
    for axis, dim in sides:
        count = lax.axis_size(axis)
        forward = [(i, i + 1) for i in range(count - 1)]
        backward = [(target, source) for source, target in forward]
        low = lax.ppermute(
            lax.slice_in_dim(block, block.shape[dim] - width, None, axis=dim), axis, forward
        )
        high = lax.ppermute(lax.slice_in_dim(block, 0, width, axis=dim), axis, backward)
        block = jnp.concatenate([low, block, high], axis=dim)
    return block


def broadcast(block, axis, owner):
    block = jnp.where(lax.axis_index(axis) == owner, block, jnp.zeros_like(block))
    return lax.psum(block, axis)


def plan_slots(requests, myself, capacity, per_shard):
    sources = requests // per_shard
    offsets = requests % per_shard
    count = requests.shape[1]
    order = jnp.arange(count, dtype=jnp.int32)
    earlier = (order[:, None] < order[None, :]).astype(jnp.int32)
    matches = (sources[:, :, None] == sources[:, None, :]).astype(jnp.int32)
    ranks = jnp.sum(matches * earlier[None], axis=1)
    slot_range = jnp.arange(capacity, dtype=jnp.int32)
    wanted = (
        (sources == myself)[:, None, :] & (ranks[:, None, :] == slot_range[None, :, None])
    ).astype(jnp.int32)
    chosen = jnp.sum(wanted * offsets[:, None, :], axis=2).reshape(-1)
    own_sources = lax.dynamic_index_in_dim(sources, myself, 0, keepdims=False)
    own_ranks = lax.dynamic_index_in_dim(ranks, myself, 0, keepdims=False)
    return (chosen, own_sources * capacity + own_ranks)


def attend_blocks(query_part, local_keys, local_values, glob_keys, glob_values, valid):
    scale = 1.0 / HEAD_DIM**0.5
    near_scores = (
        jnp.einsum("bqhd,bkhd->bhqk", query_part, local_keys, preferred_element_type=jnp.float32)
        * scale
    )
    near_scores = jnp.where(valid[:, None, None, :], near_scores, -jnp.inf)
    glob_scores = (
        jnp.einsum("bqhd,khd->bhqk", query_part, glob_keys, preferred_element_type=jnp.float32)
        * scale
    )
    highest = jnp.maximum(jnp.max(near_scores, axis=-1), jnp.max(glob_scores, axis=-1))
    near_exp = jnp.exp(near_scores - highest[..., None])
    glob_exp = jnp.exp(glob_scores - highest[..., None])
    total = jnp.sum(near_exp, axis=-1) + jnp.sum(glob_exp, axis=-1)
    near_weights = (near_exp / total[..., None]).astype(jnp.bfloat16)
    glob_weights = (glob_exp / total[..., None]).astype(jnp.bfloat16)
    mixed = jnp.einsum(
        "bhqk,bkhd->bqhd", near_weights, local_values, preferred_element_type=jnp.float32
    )
    mixed = mixed + jnp.einsum(
        "bhqk,khd->bqhd", glob_weights, glob_values, preferred_element_type=jnp.float32
    )
    return mixed.astype(jnp.bfloat16)


def exchange_body(queries, keys_values, global_ids, rand_ids, out_weight):
    rows = queries.shape[0]
    width = queries.shape[1]
    heads_here = width // HEAD_DIM
    local_blocks = rows // BLOCK
    shards = lax.axis_size("seq")
    myself = lax.axis_index("seq")
    total_blocks = local_blocks * shards
    pair_blocks = keys_values.reshape(2, local_blocks, BLOCK, width)
    padded = padded_2(keys_values, (("seq", 1),), BLOCK)
    padded = padded.reshape(2, local_blocks + 2, BLOCK, width)
    panel_list = []
    for which in range(NGLOBAL):
        target = global_ids[which]
        owner = target // local_blocks
        local_panel = lax.dynamic_index_in_dim(
            pair_blocks, target % local_blocks, 1, keepdims=False
        )
        panel_list.append(broadcast(local_panel, "seq", owner))
    glob = jnp.stack(panel_list, axis=1).reshape(2, NGLOBAL * BLOCK, heads_here, HEAD_DIM)
    requests = rand_ids.reshape(shards, local_blocks, NRANDOM)
    capacity = (local_blocks + shards - 1) // shards
    fetched = []
    for column in range(NRANDOM):
        chosen, slots = plan_slots(requests[:, :, column], myself, capacity, local_blocks)
        outgoing = jnp.take(pair_blocks, chosen, axis=1)
        incoming = lax.all_to_all(outgoing, "seq", split_axis=1, concat_axis=1, tiled=True)
        fetched.append(jnp.take(incoming, slots, axis=1))
    remote = jnp.stack(fetched, axis=2)
    segment = jnp.arange((3 + NRANDOM) * BLOCK, dtype=jnp.int32) // BLOCK

    def one_group(index):
        first = index * group_blocks
        query_part = lax.dynamic_slice_in_dim(queries, first * BLOCK, group_blocks * BLOCK, 0)
        query_part = query_part.reshape(group_blocks, BLOCK, heads_here, HEAD_DIM)
        window = lax.dynamic_slice_in_dim(padded, first, group_blocks + 2, 1)
        farther = lax.dynamic_slice_in_dim(remote, first, group_blocks, 1)
        farther = farther.reshape(2, group_blocks, NRANDOM * BLOCK, width)
        local = jnp.concatenate(
            [
                window[:, 0:group_blocks],
                window[:, 1 : group_blocks + 1],
                window[:, 2 : group_blocks + 2],
                farther,
            ],
            axis=2,
        )
        local = local.reshape(2, group_blocks, (3 + NRANDOM) * BLOCK, heads_here, HEAD_DIM)
        block_ids = myself * local_blocks + first + jnp.arange(group_blocks, dtype=jnp.int32)
        drop_before = (segment[None, :] == 0) & (block_ids[:, None] == 0)
        drop_after = (segment[None, :] == 2) & (block_ids[:, None] == total_blocks - 1)
        valid = jnp.logical_not(drop_before | drop_after)
        mixed = attend_blocks(query_part, local[0], local[1], glob[0], glob[1], valid)
        return mixed.reshape(group_blocks * BLOCK, width)

    attended = lax.map(
        one_group, jnp.arange(local_blocks // group_blocks, dtype=jnp.int32)
    ).reshape(rows, width)
    summed = jnp.dot(
        lax.all_gather(attended, "head", axis=1, tiled=True),
        out_weight,
        preferred_element_type=jnp.float32,
    )
    return summed.astype(jnp.bfloat16)


def solution(mesh):
    body = halves_body if dict(mesh.shape) == {"seq": 8, "head": 4} else exchange_body
    in_specs = (P("seq", "head"), P(None, "seq", "head"), P(), P(), P(None, "head"))
    out_specs = P("seq", "head")
    return jax.shard_map(body, mesh=mesh, in_specs=in_specs, out_specs=out_specs, check_vma=False)
```

```python
import functools

import jax
import jax.numpy as jnp
from jax import lax
from jax.experimental import pallas as pl
from jax.experimental.pallas import tpu as pltpu
from jax.sharding import PartitionSpec as P

HEAD_DIM = 128
BLOCK = 64
NGLOBAL = 2
NRANDOM = 3
NLIST = 3 + NGLOBAL + NRANDOM
MASKED = -1e30
EXP2_SCALE = 1.4426950408889634 / HEAD_DIM**0.5
STAT_TILE = 16
VMEM_LIMIT = 14 * 1024 * 1024
PROJECT_LIMIT = 32 * 1024 * 1024


group_blocks = 8


def eye_mask():
    rows = lax.broadcasted_iota(jnp.int32, (BLOCK, BLOCK), 0)
    columns = lax.broadcasted_iota(jnp.int32, (BLOCK, BLOCK), 1)
    return rows == columns


def attend_group(blocks, head, starts_ref, bias_ref, q_ref, pool):
    lanes = pl.ds(head * HEAD_DIM, HEAD_DIM)
    listed = [
        [
            pl.ds(pl.multiple_of(starts_ref[i * NLIST + e], BLOCK), BLOCK)
            for e in range(NLIST)
        ]
        for i in blocks
    ]
    places = [pl.ds(pl.multiple_of(i * BLOCK, BLOCK), BLOCK) for i in blocks]
    scores = []
    for i, rows, listing in zip(blocks, places, listed):
        keys = jnp.concatenate([pool[0, w, lanes] for w in listing], axis=0)
        product = lax.dot_general(
            q_ref[rows, lanes],
            keys,
            (((1,), (1,)), ((), ())),
            preferred_element_type=jnp.float32,
        )
        scores.append(product + bias_ref[pl.ds(i, 1), :])
    weighed = []
    for score in scores:
        highest = jnp.max(score, axis=1, keepdims=True)
        weights = jnp.exp2((score - highest) * EXP2_SCALE)
        total = jnp.sum(weights, axis=1, keepdims=True)
        weighed.append((weights.astype(jnp.bfloat16), highest, total))
    results = []
    for listing, (weights, highest, total) in zip(listed, weighed):
        values = jnp.concatenate([pool[1, w, lanes] for w in listing], axis=0)
        mixed = jnp.dot(weights, values, preferred_element_type=jnp.float32)
        results.append((lanes, mixed, highest, total))
    return results


def put_stats(i, head, stats_ref, highest, total):
    eye = eye_mask()
    high_row = jnp.sum(jnp.where(eye, highest, 0.0), axis=0, keepdims=True)
    total_row = jnp.sum(jnp.where(eye, total, 0.0), axis=0, keepdims=True)
    stats_ref[head, pl.ds(i, 1), :] = jnp.concatenate([high_row, total_row], axis=1)


def load_pool(parts, pool, sems):
    copies, low = [], 0
    for n, part in enumerate(parts):
        size = part.shape[1]
        copies.append(
            pltpu.make_async_copy(part, pool.at[:, pl.ds(low, size), :], sems.at[n])
        )
        low += size
    for copy in copies:
        copy.start()
    for copy in copies:
        copy.wait()


def attend_part(part, parts, starts_ref, bias_ref, q_ref, pool, mixed_ref, stats_ref, normalise):
    blocks = q_ref.shape[0] // BLOCK // parts
    unroll = UNROLL if blocks % UNROLL == 0 else blocks
    stats_ref[...] = jnp.zeros_like(stats_ref)

    for head in range(q_ref.shape[1] // HEAD_DIM):

        def step(n, _):
            ids = [n * unroll + u for u in range(unroll)]
            results = attend_group(
                [part * blocks + i for i in ids], head, starts_ref, bias_ref, q_ref, pool
            )
            for i, (lanes, mixed, highest, total) in zip(ids, results):
                rows = pl.ds(pl.multiple_of(i * BLOCK, BLOCK), BLOCK)
                mixed = mixed / total if normalise else mixed
                mixed_ref[rows, lanes] = mixed.astype(mixed_ref.dtype)
                put_stats(i, head, stats_ref, highest, total)
            return 0

        lax.fori_loop(0, blocks // unroll, step, 0)


def guest_kernel(parts, count, starts_ref, bias_ref, q_ref, *refs):
    *message_refs, pool, stats, sems = refs[count:]
    load_pool(refs[:count], pool, sems)
    base = q_ref.shape[0] // parts
    for part, message_ref in enumerate(message_refs):
        attend_part(part, parts, starts_ref, bias_ref, q_ref, pool, message_ref, stats, True)
        for head in range(q_ref.shape[1] // HEAD_DIM):
            rest = stats[head]
            for n in range(3):
                piece = rest.astype(jnp.bfloat16)
                rows = pl.ds(base + n * rest.shape[0], rest.shape[0])
                message_ref[rows, pl.ds(head * HEAD_DIM, HEAD_DIM)] = piece
                rest = rest - piece.astype(jnp.float32)


def home_kernel(parts, count, starts_ref, bias_ref, q_ref, *refs):
    *result_refs, pool, sems = refs[count:]
    load_pool(refs[:count], pool, sems)
    for part in range(parts):
        mixed_ref, stats_ref = result_refs[2 * part : 2 * part + 2]
        attend_part(part, parts, starts_ref, bias_ref, q_ref, pool, mixed_ref, stats_ref, False)


def merge_kernel(mixed_ref, stats_ref, message_ref, *refs):
    *out_refs, home_scale, guest_scale = refs
    base, width = mixed_ref.shape
    blocks = base // BLOCK
    size = stats_ref.shape[1]
    other = message_ref[pl.ds(base, size), :].astype(jnp.float32)
    for n in (1, 2):
        other = other + message_ref[pl.ds(base + n * size, size), :].astype(jnp.float32)
    eye = eye_mask()
    for head in range(width // HEAD_DIM):
        low = head * HEAD_DIM
        lanes = pl.ds(low, HEAD_DIM)
        high_h = stats_ref[head, :, :BLOCK]
        total_h = stats_ref[head, :, BLOCK:]
        high_g = other[:, low : low + BLOCK]
        total_g = other[:, low + BLOCK : low + HEAD_DIM]
        highest = jnp.maximum(high_h, high_g)
        factor_h = jnp.exp2((high_h - highest) * EXP2_SCALE)
        factor_g = jnp.exp2((high_g - highest) * EXP2_SCALE) * total_g
        total = factor_h * total_h + factor_g
        total = jnp.where(total > 0, total, 1.0)
        home_scale[...] = factor_h / total
        guest_scale[...] = factor_g / total

        def step(n, part, low):
            i = low + n
            rows = pl.ds(pl.multiple_of(i * BLOCK, BLOCK), BLOCK)
            scale_h = jnp.sum(
                jnp.where(eye, home_scale[pl.ds(i, 1), :], 0.0), axis=1, keepdims=True
            )
            scale_g = jnp.sum(
                jnp.where(eye, guest_scale[pl.ds(i, 1), :], 0.0), axis=1, keepdims=True
            )
            mixed = (
                mixed_ref[rows, lanes] * scale_h
                + message_ref[rows, lanes].astype(jnp.float32) * scale_g
            )
            rows = pl.ds(pl.multiple_of(n * BLOCK, BLOCK), BLOCK)
            out_refs[part][rows, lanes] = mixed.astype(jnp.bfloat16)

        low = 0
        for part, out_ref in enumerate(out_refs):

            def body(n, _, part=part, low=low):
                step(n, part, low)
                return 0

            count = out_ref.shape[0] // BLOCK
            lax.fori_loop(0, count, body, 0, unroll=4)
            low += count


def last_terms_kernel(groups, w_ref, sum_ref, *refs):
    x_refs, out_ref = refs[: 2 * groups], refs[-1]
    ordered = [x_refs[h * groups + r][...] for r in range(groups) for h in range(2)]
    term = jnp.dot(
        jnp.concatenate(ordered, axis=1), w_ref[...], preferred_element_type=jnp.float32
    )
    out_ref[...] = (sum_ref[...] + term).astype(out_ref.dtype)


VMEM = pl.BlockSpec(memory_space=pltpu.VMEM)
SMEM = pl.BlockSpec(memory_space=pltpu.SMEM)
ANY = pl.BlockSpec(memory_space=pl.ANY)
HBM = pl.BlockSpec(memory_space=pltpu.HBM)


def params():
    return pltpu.CompilerParams(vmem_limit_bytes=VMEM_LIMIT)


def pool_scratch(query):
    return pltpu.VMEM((2, 4 * query.shape[0], query.shape[1]), jnp.bfloat16)


def stats_shape(query, parts, kind):
    blocks = query.shape[0] // BLOCK // parts
    size = -(-blocks // STAT_TILE) * STAT_TILE
    return kind((query.shape[1] // HEAD_DIM, size, 2 * BLOCK), jnp.float32)


def cost(micros):
    return pl.CostEstimate(flops=int(micros * 1.15e9), bytes_accessed=0, transcendentals=0)


def guest_call(starts, bias, query, pieces, parts=1):
    rows, width = query.shape
    size = stats_shape(query, parts, jax.ShapeDtypeStruct).shape[1]
    message = jax.ShapeDtypeStruct((rows // parts + 3 * size, width), jnp.bfloat16)
    return pl.pallas_call(
        functools.partial(guest_kernel, parts, len(pieces)),
        out_shape=[message] * parts,
        in_specs=[SMEM, VMEM, VMEM] + [ANY] * len(pieces),
        out_specs=[VMEM] * parts,
        scratch_shapes=[
            pool_scratch(query),
            stats_shape(query, parts, pltpu.VMEM),
            pltpu.SemaphoreType.DMA((len(pieces),)),
        ],
        compiler_params=params(),
        cost_estimate=cost(GUEST_US),
        name="guest_attention",
    )(starts, bias, query, *pieces)


def home_call(starts, bias, query, pieces, parts=1):
    rows, width = query.shape
    results = [
        jax.ShapeDtypeStruct((rows // parts, width), jnp.float32),
        stats_shape(query, parts, jax.ShapeDtypeStruct),
    ]
    return pl.pallas_call(
        functools.partial(home_kernel, parts, len(pieces)),
        out_shape=results * parts,
        in_specs=[SMEM, VMEM, VMEM] + [ANY] * len(pieces),
        out_specs=[VMEM] * (2 * parts),
        scratch_shapes=[pool_scratch(query), pltpu.SemaphoreType.DMA((len(pieces),))],
        compiler_params=params(),
        cost_estimate=cost(0),
        name="home_attention",
    )(starts, bias, query, *pieces)


def merge_call(mixed, stats, message, sizes=None):
    rows, width = mixed.shape
    sizes = sizes or [rows]
    return pl.pallas_call(
        merge_kernel,
        out_shape=[jax.ShapeDtypeStruct((size, width), jnp.bfloat16) for size in sizes],
        in_specs=[VMEM, VMEM, VMEM],
        out_specs=[VMEM] * len(sizes),
        scratch_shapes=[
            pltpu.VMEM((stats.shape[1], BLOCK), jnp.float32),
            pltpu.VMEM((stats.shape[1], BLOCK), jnp.float32),
        ],
        compiler_params=params(),
        cost_estimate=cost(0),
        name="merge_halves",
    )(mixed, stats, message)


ROW_TILE = 256


def last_terms(summed, gathered, weight, part, filled=None):
    rows, columns = summed.shape
    first, tiles = part
    pieces = [piece for group in gathered for piece in group]

    def row_spec(height, width):
        low = first if height == rows else 0
        return pl.BlockSpec((ROW_TILE, width), lambda i: (i + low, 0))

    others = [] if filled is None else [filled]
    return pl.pallas_call(
        functools.partial(last_terms_kernel, len(pieces) // 2),
        grid=(tiles,),
        out_shape=jax.ShapeDtypeStruct((rows, columns), jnp.bfloat16),
        in_specs=[VMEM]
        + [row_spec(*v.shape) for v in [summed, *pieces]]
        + [ANY] * len(others),
        out_specs=row_spec(rows, columns),
        input_output_aliases={2 + len(pieces): 0} if others else {},
        compiler_params=params(),
        cost_estimate=cost(PROJECT_US),
        name="last_terms",
    )(weight, summed, *pieces, *others)


def first_terms_kernel(groups, w_ref, *refs):
    x_refs, (out_ref, columns, sems) = refs[: 2 * groups], refs[2 * groups :]
    copies = [
        pltpu.make_async_copy(
            x_refs[head * groups + relation],
            columns.at[:, pl.ds((2 * relation + head) * HEAD_DIM, HEAD_DIM)],
            sems.at[2 * relation + head],
        )
        for relation in range(groups)
        for head in range(2)
    ]
    for copy in copies:
        copy.start()
    for copy in copies:
        copy.wait()

    def step(i, _):
        rows = pl.ds(pl.multiple_of(i * ROW_TILE, ROW_TILE), ROW_TILE)
        out_ref[rows, :] = jnp.dot(
            columns[rows, :], w_ref[...], preferred_element_type=jnp.float32
        )
        return 0

    lax.fori_loop(0, out_ref.shape[0] // ROW_TILE, step, 0)


def first_terms(gathered, weight):
    pieces = [piece for group in gathered for piece in group]
    rows = pieces[0].shape[0]
    return pl.pallas_call(
        functools.partial(first_terms_kernel, len(pieces) // 2),
        out_shape=jax.ShapeDtypeStruct((rows, weight.shape[1]), jnp.float32),
        in_specs=[VMEM] + [ANY] * len(pieces),
        out_specs=VMEM,
        scratch_shapes=[
            pltpu.VMEM((rows, weight.shape[0]), jnp.bfloat16),
            pltpu.SemaphoreType.DMA((len(pieces),)),
        ],
        compiler_params=params(),
        cost_estimate=cost(0),
        name="first_terms",
    )(weight, *pieces)


def order_kernel(me_ref, w_ref, first_ref, last_ref, sems):
    copies = []
    for relation in range(w_ref.shape[0]):
        for n, target in enumerate((first_ref, last_ref)):
            copies.append(
                pltpu.make_async_copy(
                    w_ref.at[me_ref[0] ^ relation, pl.ds(2 * n, 2)],
                    target.at[relation],
                    sems.at[2 * relation + n],
                )
            )
    for copy in copies:
        copy.start()
    for copy in copies:
        copy.wait()


def order_weights(weights):
    groups, heads, depth, columns = weights.shape
    half = jax.ShapeDtypeStruct((groups, heads // 2, depth, columns), weights.dtype)
    myself = lax.axis_index("head").astype(jnp.int32).reshape(1)
    parts = pl.pallas_call(
        order_kernel,
        out_shape=[half, half],
        in_specs=[SMEM, ANY],
        out_specs=[ANY, ANY],
        scratch_shapes=[pltpu.SemaphoreType.DMA((2 * groups,))],
        compiler_params=params(),
        cost_estimate=cost(0),
        name="order_weights",
    )(myself, weights)
    return [part.reshape(-1, columns) for part in parts]


def key_list(shard, global_ids, rand_ids, local_blocks, shards):
    total_blocks = local_blocks * shards
    block_ids = shard * local_blocks + jnp.arange(local_blocks, dtype=jnp.int32)
    near = block_ids[:, None] + jnp.arange(-1, 2, dtype=jnp.int32)[None, :]
    inside = (near >= 0) & (near < total_blocks)
    listed = lax.dynamic_slice_in_dim(rand_ids, shard * local_blocks, local_blocks, 0)
    glob = jnp.broadcast_to(global_ids[None, :], (local_blocks, NGLOBAL))
    ids = jnp.concatenate([jnp.clip(near, 0, total_blocks - 1), glob, listed], axis=1)
    inside = jnp.concatenate(
        [inside, jnp.ones((local_blocks, NGLOBAL + NRANDOM), jnp.bool_)], axis=1
    )
    return ids, inside


def guests_first(guests, source, global_ids, rand_ids, local_blocks, shards):
    ids, inside = key_list(guests, global_ids, rand_ids, local_blocks, shards)
    order = jnp.arange(local_blocks, dtype=jnp.int32)
    blocks = source * local_blocks + order
    hits = (ids[None] == blocks[:, None, None]) & inside[None]
    listed = jnp.max(hits.astype(jnp.int32), axis=(1, 2))
    earlier = (order[None, :] < order[:, None]).astype(jnp.int32)
    among = jnp.sum(earlier * listed[None, :], axis=1)
    return jnp.where(listed > 0, among, jnp.sum(listed) + order - among)


def key_places(shard, myself, global_ids, rand_ids, local_blocks, shards, diagonal=None):
    half = shards // 2
    ids, inside = key_list(shard, global_ids, rand_ids, local_blocks, shards)
    owner = ids // local_blocks
    here = ((owner // half) == (myself // half)) & inside
    relative = (owner ^ myself) & (half - 1)
    block = ids % local_blocks
    if diagonal is not None:
        order = jnp.arange(local_blocks, dtype=jnp.int32)
        moved = jnp.sum(jnp.where(block[..., None] == order, diagonal, 0), axis=-1)
        block = jnp.where(relative == half - 1, moved, block)
    starts = jnp.where(here, (relative * local_blocks + block) * BLOCK, 0)
    bias = jnp.repeat(jnp.where(here, 0.0, MASKED).astype(jnp.float32), BLOCK, axis=1)
    return starts.reshape(-1).astype(jnp.int32), bias


def split_kernel(order_ref, pair_ref, first_ref, rest_ref):
    blocks = first_ref.shape[1] // BLOCK
    for n in range(pair_ref.shape[1] // BLOCK):
        source = pl.ds(pl.multiple_of(order_ref[n] * BLOCK, BLOCK), BLOCK)
        target = first_ref if n < blocks else rest_ref
        target[:, pl.ds((n % blocks) * BLOCK, BLOCK), :] = pair_ref[:, source, :]


def split_call(order, pair):
    half = jax.ShapeDtypeStruct((2, pair.shape[1] // 2, pair.shape[2]), pair.dtype)
    return pl.pallas_call(
        split_kernel,
        out_shape=[half, half],
        in_specs=[SMEM, VMEM],
        out_specs=[VMEM, VMEM],
        compiler_params=params(),
        cost_estimate=cost(0),
        name="guests_first",
    )(order, pair)


def swap(value, distance, shards):
    return lax.ppermute(value, "seq", [(i, i ^ distance) for i in range(shards)])


def after(value, *tokens):
    return lax.optimization_barrier((value, *tokens))[0]


def hop(value, distance, groups):
    return lax.ppermute(value, "head", [(i, i ^ distance) for i in range(groups)])


def together(*values):
    return lax.optimization_barrier(values)


UNROLL = 8
GUEST_US = 0.1
PROJECT_US = 4
UPPER_TILES = 4


def halves_body(queries, keys_values, global_ids, rand_ids, out_weight):
    rows, width = queries.shape
    heads_here = width // HEAD_DIM
    local_blocks = rows // BLOCK
    shards = lax.axis_size("seq")
    myself = lax.axis_index("seq")
    groups = lax.axis_size("head")
    opposite = shards // 2

    def column(array, head):
        return lax.slice_in_dim(array, head * HEAD_DIM, (head + 1) * HEAD_DIM, axis=array.ndim - 1)

    def over_y(value):
        return swap(value, 1, shards)

    def over_z(value):
        return swap(value, 2, shards)

    def across(value):
        return swap(value, opposite, shards)

    lists = (global_ids, rand_ids, local_blocks, shards)
    mine = guests_first(myself ^ opposite, myself ^ 3, *lists)
    theirs = guests_first(myself ^ opposite ^ 1, myself ^ 2, *lists)
    count = jnp.arange(local_blocks, dtype=jnp.int32)
    order = jnp.sum(jnp.where(theirs[None, :] == count[:, None], count[None, :], 0), axis=1)
    home = key_places(myself, myself, *lists)
    guest = key_places(myself ^ opposite, myself, *lists)
    last_home = key_places(myself, myself, *lists, mine)
    last_guest = key_places(myself ^ opposite, myself, *lists, mine)
    home, guest = (*home, *last_home, order), (*guest, *last_guest)
    weights = order_weights(
        out_weight.reshape(groups, heads_here, HEAD_DIM, out_weight.shape[1])
    )
    k0 = column(keys_values, 0)
    others = after(keys_values, k0)
    k1, k2, k3 = [column(others, h) for h in range(1, heads_here)]
    q0, q1, q2, q3 = [column(queries, h) for h in range(heads_here)]

    y0, z0 = over_y(k0), over_z(k0)
    y0, z0, k1_, v0, v1, home, guest = together(y0, z0, k1, q0, q1, home, guest)

    d0, y1, z1, v0, v1 = over_y(z0), over_y(k1_), over_z(k1_), across(v0), across(v1)
    p0 = (k0, y0, z0, d0)
    (s0,) = guest_call(*guest[:2], v0, p0)
    s0, y1, z1, v1, k2_, v2, weights = together(s0, y1, z1, v1, k2, q2, weights)

    d1, y2, z2, v2, g0 = over_y(z1), over_y(k2_), over_z(k2_), across(v2), across(s0)
    m0 = home_call(*home[:2], after(q0, s0), p0)
    p1 = (k1, y1, z1, d1)
    (s1,) = guest_call(*guest[:2], after(v1, m0[1], v2), p1)
    s1, y2, z2, v2, g0, k3_, v3 = together(s1, y2, z2, v2, g0, k3, q3)

    d2, y3, z3, v3, g1 = over_y(z2), over_y(k3_), over_z(k3_), across(v3), across(s1)
    m1 = home_call(*home[:2], after(q1, s1), p1)
    (a0,) = merge_call(*m0, after(g0, m1[1]))
    a0x, a0c = hop(a0, 2, groups), hop(a0, 1, groups)
    p2 = (k2, y2, z2, d2)
    (s2,) = guest_call(*guest[:2], after(v2, m1[1], v3), p2)
    s2, y3, z3, v3, g1, a0x, a0c = together(s2, y3, z3, v3, g1, a0x, a0c)

    first, rest = split_call(home[4], z3)
    d3, d3_, g2 = over_y(first), over_y(rest), across(s2)
    m2 = home_call(*home[:2], after(q2, s2), p2)
    (a1,) = merge_call(*m1, after(g1, m2[1]))
    a1x, a1c, a0d = hop(a1, 2, groups), hop(a1, 1, groups), hop(a0x, 1, groups)
    (s3,) = guest_call(*guest[2:4], after(v3, a1), (k3, y3, z3, d3))
    g3 = across(after(s3, g2))
    m3 = home_call(*home[2:4], after(q3, s3), (k3, y3, z3, d3, d3_))
    (a2,) = merge_call(*m2, after(g2, m3[1]))
    a1d = hop(after(a1x, s3), 1, groups)
    a2x, a2c = hop(a2, 2, groups), hop(a2, 1, groups)
    early = ((a0, a0c, a0x, a0d), (a1, a1c, a1x, a1d))
    summed = first_terms(early, after(weights[0], m3[1]))

    tiles = rows // ROW_TILE
    tiles_a = UPPER_TILES
    sizes = [tiles_a * ROW_TILE, (tiles - tiles_a) * ROW_TILE]
    a3a, a3b = merge_call(*m3, after(g3, summed), sizes)
    a3ax, a3ac = hop(a3a, 2, groups), hop(a3a, 1, groups)
    a3bx, a3bc = hop(after(a3b, a3a), 2, groups), hop(a3b, 1, groups)
    a2d = hop(after(a2x, a3b), 1, groups)
    a2 = (a2, a2c, a2x, a2d)
    a3ad = hop(a3ax, 1, groups)
    upper = last_terms(summed, (a2, (a3a, a3ac, a3ax, a3ad)), weights[1], (0, tiles_a))
    a3bd = hop(after(a3bx, upper), 1, groups)
    late = (a2, (a3b, a3bc, a3bx, a3bd))
    return last_terms(summed, late, weights[1], (tiles_a, tiles - tiles_a), upper)


def padded_2(block, sides, width):
    for axis, dim in sides:
        count = lax.axis_size(axis)
        forward = [(i, i + 1) for i in range(count - 1)]
        backward = [(target, source) for source, target in forward]
        low = lax.ppermute(
            lax.slice_in_dim(block, block.shape[dim] - width, None, axis=dim), axis, forward
        )
        high = lax.ppermute(lax.slice_in_dim(block, 0, width, axis=dim), axis, backward)
        block = jnp.concatenate([low, block, high], axis=dim)
    return block


def broadcast(block, axis, owner):
    block = jnp.where(lax.axis_index(axis) == owner, block, jnp.zeros_like(block))
    return lax.psum(block, axis)


def plan_slots(requests, myself, capacity, per_shard):
    sources = requests // per_shard
    offsets = requests % per_shard
    count = requests.shape[1]
    order = jnp.arange(count, dtype=jnp.int32)
    earlier = (order[:, None] < order[None, :]).astype(jnp.int32)
    matches = (sources[:, :, None] == sources[:, None, :]).astype(jnp.int32)
    ranks = jnp.sum(matches * earlier[None], axis=1)
    slot_range = jnp.arange(capacity, dtype=jnp.int32)
    wanted = (
        (sources == myself)[:, None, :] & (ranks[:, None, :] == slot_range[None, :, None])
    ).astype(jnp.int32)
    chosen = jnp.sum(wanted * offsets[:, None, :], axis=2).reshape(-1)
    own_sources = lax.dynamic_index_in_dim(sources, myself, 0, keepdims=False)
    own_ranks = lax.dynamic_index_in_dim(ranks, myself, 0, keepdims=False)
    return (chosen, own_sources * capacity + own_ranks)


def attend_blocks(query_part, local_keys, local_values, glob_keys, glob_values, valid):
    scale = 1.0 / HEAD_DIM**0.5
    near_scores = (
        jnp.einsum("bqhd,bkhd->bhqk", query_part, local_keys, preferred_element_type=jnp.float32)
        * scale
    )
    near_scores = jnp.where(valid[:, None, None, :], near_scores, -jnp.inf)
    glob_scores = (
        jnp.einsum("bqhd,khd->bhqk", query_part, glob_keys, preferred_element_type=jnp.float32)
        * scale
    )
    highest = jnp.maximum(jnp.max(near_scores, axis=-1), jnp.max(glob_scores, axis=-1))
    near_exp = jnp.exp(near_scores - highest[..., None])
    glob_exp = jnp.exp(glob_scores - highest[..., None])
    total = jnp.sum(near_exp, axis=-1) + jnp.sum(glob_exp, axis=-1)
    near_weights = (near_exp / total[..., None]).astype(jnp.bfloat16)
    glob_weights = (glob_exp / total[..., None]).astype(jnp.bfloat16)
    mixed = jnp.einsum(
        "bhqk,bkhd->bqhd", near_weights, local_values, preferred_element_type=jnp.float32
    )
    mixed = mixed + jnp.einsum(
        "bhqk,khd->bqhd", glob_weights, glob_values, preferred_element_type=jnp.float32
    )
    return mixed.astype(jnp.bfloat16)


def exchange_body(queries, keys_values, global_ids, rand_ids, out_weight):
    rows = queries.shape[0]
    width = queries.shape[1]
    heads_here = width // HEAD_DIM
    local_blocks = rows // BLOCK
    shards = lax.axis_size("seq")
    myself = lax.axis_index("seq")
    total_blocks = local_blocks * shards
    pair_blocks = keys_values.reshape(2, local_blocks, BLOCK, width)
    padded = padded_2(keys_values, (("seq", 1),), BLOCK)
    padded = padded.reshape(2, local_blocks + 2, BLOCK, width)
    panel_list = []
    for which in range(NGLOBAL):
        target = global_ids[which]
        owner = target // local_blocks
        local_panel = lax.dynamic_index_in_dim(
            pair_blocks, target % local_blocks, 1, keepdims=False
        )
        panel_list.append(broadcast(local_panel, "seq", owner))
    glob = jnp.stack(panel_list, axis=1).reshape(2, NGLOBAL * BLOCK, heads_here, HEAD_DIM)
    requests = rand_ids.reshape(shards, local_blocks, NRANDOM)
    capacity = (local_blocks + shards - 1) // shards
    fetched = []
    for column in range(NRANDOM):
        chosen, slots = plan_slots(requests[:, :, column], myself, capacity, local_blocks)
        outgoing = jnp.take(pair_blocks, chosen, axis=1)
        incoming = lax.all_to_all(outgoing, "seq", split_axis=1, concat_axis=1, tiled=True)
        fetched.append(jnp.take(incoming, slots, axis=1))
    remote = jnp.stack(fetched, axis=2)
    segment = jnp.arange((3 + NRANDOM) * BLOCK, dtype=jnp.int32) // BLOCK

    def one_group(index):
        first = index * group_blocks
        query_part = lax.dynamic_slice_in_dim(queries, first * BLOCK, group_blocks * BLOCK, 0)
        query_part = query_part.reshape(group_blocks, BLOCK, heads_here, HEAD_DIM)
        window = lax.dynamic_slice_in_dim(padded, first, group_blocks + 2, 1)
        farther = lax.dynamic_slice_in_dim(remote, first, group_blocks, 1)
        farther = farther.reshape(2, group_blocks, NRANDOM * BLOCK, width)
        local = jnp.concatenate(
            [
                window[:, 0:group_blocks],
                window[:, 1 : group_blocks + 1],
                window[:, 2 : group_blocks + 2],
                farther,
            ],
            axis=2,
        )
        local = local.reshape(2, group_blocks, (3 + NRANDOM) * BLOCK, heads_here, HEAD_DIM)
        block_ids = myself * local_blocks + first + jnp.arange(group_blocks, dtype=jnp.int32)
        drop_before = (segment[None, :] == 0) & (block_ids[:, None] == 0)
        drop_after = (segment[None, :] == 2) & (block_ids[:, None] == total_blocks - 1)
        valid = jnp.logical_not(drop_before | drop_after)
        mixed = attend_blocks(query_part, local[0], local[1], glob[0], glob[1], valid)
        return mixed.reshape(group_blocks * BLOCK, width)

    attended = lax.map(
        one_group, jnp.arange(local_blocks // group_blocks, dtype=jnp.int32)
    ).reshape(rows, width)
    summed = jnp.dot(
        lax.all_gather(attended, "head", axis=1, tiled=True),
        out_weight,
        preferred_element_type=jnp.float32,
    )
    return summed.astype(jnp.bfloat16)


def solution(mesh):
    body = halves_body if dict(mesh.shape) == {"seq": 8, "head": 4} else exchange_body
    in_specs = (P("seq", "head"), P(None, "seq", "head"), P(), P(), P(None, "head"))
    out_specs = P("seq", "head")
    return jax.shard_map(body, mesh=mesh, in_specs=in_specs, out_specs=out_specs, check_vma=False)
```

```python
import functools

import jax
import jax.numpy as jnp
from jax import lax
from jax.experimental import pallas as pl
from jax.experimental.pallas import tpu as pltpu
from jax.sharding import PartitionSpec as P

HEAD_DIM = 128
BLOCK = 64
NGLOBAL = 2
NRANDOM = 3
NLIST = 3 + NGLOBAL + NRANDOM
MASKED = -1e30
EXP2_SCALE = 1.4426950408889634 / HEAD_DIM**0.5
STAT_TILE = 16
VMEM_LIMIT = 20 * 1024 * 1024
PROJECT_LIMIT = 32 * 1024 * 1024


group_blocks = 8


def eye_mask():
    rows = lax.broadcasted_iota(jnp.int32, (BLOCK, BLOCK), 0)
    columns = lax.broadcasted_iota(jnp.int32, (BLOCK, BLOCK), 1)
    return rows == columns


def attend_group(blocks, head, starts_ref, bias_ref, q_ref, pool):
    lanes = pl.ds(head * HEAD_DIM, HEAD_DIM)
    listed = [
        [
            pl.ds(pl.multiple_of(starts_ref[i * NLIST + e], BLOCK), BLOCK)
            for e in range(NLIST)
        ]
        for i in blocks
    ]
    places = [pl.ds(pl.multiple_of(i * BLOCK, BLOCK), BLOCK) for i in blocks]
    scores = []
    for i, rows, listing in zip(blocks, places, listed):
        keys = jnp.concatenate([pool[0, w, lanes] for w in listing], axis=0)
        product = lax.dot_general(
            q_ref[rows, lanes],
            keys,
            (((1,), (1,)), ((), ())),
            preferred_element_type=jnp.float32,
        )
        scores.append(product + bias_ref[pl.ds(i, 1), :])
    weighed = []
    for score in scores:
        highest = jnp.max(score, axis=1, keepdims=True)
        weights = jnp.exp2((score - highest) * EXP2_SCALE)
        total = jnp.sum(weights, axis=1, keepdims=True)
        weighed.append((weights.astype(jnp.bfloat16), highest, total))
    results = []
    for listing, (weights, highest, total) in zip(listed, weighed):
        values = jnp.concatenate([pool[1, w, lanes] for w in listing], axis=0)
        mixed = jnp.dot(weights, values, preferred_element_type=jnp.float32)
        results.append((lanes, mixed, highest, total))
    return results


def put_stats(i, head, stats_ref, highest, total):
    eye = eye_mask()
    high_row = jnp.sum(jnp.where(eye, highest, 0.0), axis=0, keepdims=True)
    total_row = jnp.sum(jnp.where(eye, total, 0.0), axis=0, keepdims=True)
    stats_ref[head, pl.ds(i, 1), :] = jnp.concatenate([high_row, total_row], axis=1)


def load_pool(parts, pool, sems):
    copies, low = [], 0
    for n, part in enumerate(parts):
        size = part.shape[1]
        copies.append(
            pltpu.make_async_copy(part, pool.at[:, pl.ds(low, size), :], sems.at[n])
        )
        low += size
    for copy in copies:
        copy.start()
    for copy in copies:
        copy.wait()


def attend_part(part, parts, starts_ref, bias_ref, q_ref, pool, mixed_ref, stats_ref, normalise):
    blocks = q_ref.shape[0] // BLOCK // parts
    unroll = UNROLL if blocks % UNROLL == 0 else blocks
    stats_ref[...] = jnp.zeros_like(stats_ref)

    for head in range(q_ref.shape[1] // HEAD_DIM):

        def step(n, _):
            ids = [n * unroll + u for u in range(unroll)]
            results = attend_group(
                [part * blocks + i for i in ids], head, starts_ref, bias_ref, q_ref, pool
            )
            for i, (lanes, mixed, highest, total) in zip(ids, results):
                rows = pl.ds(pl.multiple_of(i * BLOCK, BLOCK), BLOCK)
                mixed = mixed / total if normalise else mixed
                mixed_ref[rows, lanes] = mixed.astype(mixed_ref.dtype)
                put_stats(i, head, stats_ref, highest, total)
            return 0

        lax.fori_loop(0, blocks // unroll, step, 0)


def guest_kernel(parts, count, starts_ref, bias_ref, q_ref, *refs):
    *message_refs, pool, stats, sems = refs[count:]
    load_pool(refs[:count], pool, sems)
    base = q_ref.shape[0] // parts
    for part, message_ref in enumerate(message_refs):
        attend_part(part, parts, starts_ref, bias_ref, q_ref, pool, message_ref, stats, True)
        for head in range(q_ref.shape[1] // HEAD_DIM):
            rest = stats[head]
            for n in range(3):
                piece = rest.astype(jnp.bfloat16)
                rows = pl.ds(base + n * rest.shape[0], rest.shape[0])
                message_ref[rows, pl.ds(head * HEAD_DIM, HEAD_DIM)] = piece
                rest = rest - piece.astype(jnp.float32)


def home_kernel(parts, count, starts_ref, bias_ref, q_ref, *refs):
    *result_refs, pool, sems = refs[count:]
    load_pool(refs[:count], pool, sems)
    for part in range(parts):
        mixed_ref, stats_ref = result_refs[2 * part : 2 * part + 2]
        attend_part(part, parts, starts_ref, bias_ref, q_ref, pool, mixed_ref, stats_ref, False)


def merge_kernel(mixed_ref, stats_ref, message_ref, *refs):
    *out_refs, home_scale, guest_scale = refs
    base, width = mixed_ref.shape
    blocks = base // BLOCK
    size = stats_ref.shape[1]
    other = message_ref[pl.ds(base, size), :].astype(jnp.float32)
    for n in (1, 2):
        other = other + message_ref[pl.ds(base + n * size, size), :].astype(jnp.float32)
    eye = eye_mask()
    for head in range(width // HEAD_DIM):
        low = head * HEAD_DIM
        lanes = pl.ds(low, HEAD_DIM)
        high_h = stats_ref[head, :, :BLOCK]
        total_h = stats_ref[head, :, BLOCK:]
        high_g = other[:, low : low + BLOCK]
        total_g = other[:, low + BLOCK : low + HEAD_DIM]
        highest = jnp.maximum(high_h, high_g)
        factor_h = jnp.exp2((high_h - highest) * EXP2_SCALE)
        factor_g = jnp.exp2((high_g - highest) * EXP2_SCALE) * total_g
        total = factor_h * total_h + factor_g
        total = jnp.where(total > 0, total, 1.0)
        home_scale[...] = factor_h / total
        guest_scale[...] = factor_g / total

        def step(n, part, low):
            i = low + n
            rows = pl.ds(pl.multiple_of(i * BLOCK, BLOCK), BLOCK)
            scale_h = jnp.sum(
                jnp.where(eye, home_scale[pl.ds(i, 1), :], 0.0), axis=1, keepdims=True
            )
            scale_g = jnp.sum(
                jnp.where(eye, guest_scale[pl.ds(i, 1), :], 0.0), axis=1, keepdims=True
            )
            mixed = (
                mixed_ref[rows, lanes] * scale_h
                + message_ref[rows, lanes].astype(jnp.float32) * scale_g
            )
            rows = pl.ds(pl.multiple_of(n * BLOCK, BLOCK), BLOCK)
            out_refs[part][rows, lanes] = mixed.astype(jnp.bfloat16)

        low = 0
        for part, out_ref in enumerate(out_refs):

            def body(n, _, part=part, low=low):
                step(n, part, low)
                return 0

            count = out_ref.shape[0] // BLOCK
            lax.fori_loop(0, count, body, 0, unroll=4)
            low += count


def last_terms_kernel(groups, w_ref, sum_ref, *refs):
    x_refs, out_ref = refs[: 2 * groups], refs[-1]
    ordered = [x_refs[h * groups + r][...] for r in range(groups) for h in range(2)]
    term = jnp.dot(
        jnp.concatenate(ordered, axis=1), w_ref[...], preferred_element_type=jnp.float32
    )
    out_ref[...] = (sum_ref[...] + term).astype(out_ref.dtype)


VMEM = pl.BlockSpec(memory_space=pltpu.VMEM)
SMEM = pl.BlockSpec(memory_space=pltpu.SMEM)
ANY = pl.BlockSpec(memory_space=pl.ANY)
HBM = pl.BlockSpec(memory_space=pltpu.HBM)


def params():
    return pltpu.CompilerParams(vmem_limit_bytes=VMEM_LIMIT)


def pool_scratch(query):
    return pltpu.VMEM((2, 4 * query.shape[0], query.shape[1]), jnp.bfloat16)


def stats_shape(query, parts, kind):
    blocks = query.shape[0] // BLOCK // parts
    size = -(-blocks // STAT_TILE) * STAT_TILE
    return kind((query.shape[1] // HEAD_DIM, size, 2 * BLOCK), jnp.float32)


def cost(micros):
    return pl.CostEstimate(flops=int(micros * 1.15e9), bytes_accessed=0, transcendentals=0)


def guest_call(starts, bias, query, pieces, parts=1):
    rows, width = query.shape
    size = stats_shape(query, parts, jax.ShapeDtypeStruct).shape[1]
    message = jax.ShapeDtypeStruct((rows // parts + 3 * size, width), jnp.bfloat16)
    return pl.pallas_call(
        functools.partial(guest_kernel, parts, len(pieces)),
        out_shape=[message] * parts,
        in_specs=[SMEM, VMEM, VMEM] + [ANY] * len(pieces),
        out_specs=[VMEM] * parts,
        scratch_shapes=[
            pool_scratch(query),
            stats_shape(query, parts, pltpu.VMEM),
            pltpu.SemaphoreType.DMA((len(pieces),)),
        ],
        compiler_params=params(),
        cost_estimate=cost(GUEST_US),
        name="guest_attention",
    )(starts, bias, query, *pieces)


def home_call(starts, bias, query, pieces, parts=1):
    rows, width = query.shape
    results = [
        jax.ShapeDtypeStruct((rows // parts, width), jnp.float32),
        stats_shape(query, parts, jax.ShapeDtypeStruct),
    ]
    return pl.pallas_call(
        functools.partial(home_kernel, parts, len(pieces)),
        out_shape=results * parts,
        in_specs=[SMEM, VMEM, VMEM] + [ANY] * len(pieces),
        out_specs=[VMEM] * (2 * parts),
        scratch_shapes=[pool_scratch(query), pltpu.SemaphoreType.DMA((len(pieces),))],
        compiler_params=params(),
        cost_estimate=cost(0),
        name="home_attention",
    )(starts, bias, query, *pieces)


def merge_call(mixed, stats, message, sizes=None):
    rows, width = mixed.shape
    sizes = sizes or [rows]
    return pl.pallas_call(
        merge_kernel,
        out_shape=[jax.ShapeDtypeStruct((size, width), jnp.bfloat16) for size in sizes],
        in_specs=[VMEM, VMEM, VMEM],
        out_specs=[VMEM] * len(sizes),
        scratch_shapes=[
            pltpu.VMEM((stats.shape[1], BLOCK), jnp.float32),
            pltpu.VMEM((stats.shape[1], BLOCK), jnp.float32),
        ],
        compiler_params=params(),
        cost_estimate=cost(0),
        name="merge_halves",
    )(mixed, stats, message)


ROW_TILE = 256


def last_terms(summed, gathered, weight, part, filled=None):
    rows, columns = summed.shape
    first, tiles = part
    pieces = [piece for group in gathered for piece in group]

    def row_spec(height, width):
        low = first if height == rows else 0
        return pl.BlockSpec((ROW_TILE, width), lambda i: (i + low, 0))

    others = [] if filled is None else [filled]
    return pl.pallas_call(
        functools.partial(last_terms_kernel, len(pieces) // 2),
        grid=(tiles,),
        out_shape=jax.ShapeDtypeStruct((rows, columns), jnp.bfloat16),
        in_specs=[VMEM]
        + [row_spec(*v.shape) for v in [summed, *pieces]]
        + [ANY] * len(others),
        out_specs=row_spec(rows, columns),
        input_output_aliases={2 + len(pieces): 0} if others else {},
        compiler_params=params(),
        cost_estimate=cost(PROJECT_US),
        name="last_terms",
    )(weight, summed, *pieces, *others)


def first_terms_kernel(groups, w_ref, *refs):
    x_refs, (out_ref, columns, sems) = refs[: 2 * groups], refs[2 * groups :]
    copies = [
        pltpu.make_async_copy(
            x_refs[head * groups + relation],
            columns.at[:, pl.ds((2 * relation + head) * HEAD_DIM, HEAD_DIM)],
            sems.at[2 * relation + head],
        )
        for relation in range(groups)
        for head in range(2)
    ]
    for copy in copies:
        copy.start()
    for copy in copies:
        copy.wait()

    def step(i, _):
        rows = pl.ds(pl.multiple_of(i * ROW_TILE, ROW_TILE), ROW_TILE)
        out_ref[rows, :] = jnp.dot(
            columns[rows, :], w_ref[...], preferred_element_type=jnp.float32
        )
        return 0

    lax.fori_loop(0, out_ref.shape[0] // ROW_TILE, step, 0)


def first_terms(gathered, weight):
    pieces = [piece for group in gathered for piece in group]
    rows = pieces[0].shape[0]
    return pl.pallas_call(
        functools.partial(first_terms_kernel, len(pieces) // 2),
        out_shape=jax.ShapeDtypeStruct((rows, weight.shape[1]), jnp.float32),
        in_specs=[VMEM] + [ANY] * len(pieces),
        out_specs=VMEM,
        scratch_shapes=[
            pltpu.VMEM((rows, weight.shape[0]), jnp.bfloat16),
            pltpu.SemaphoreType.DMA((len(pieces),)),
        ],
        compiler_params=params(),
        cost_estimate=cost(0),
        name="first_terms",
    )(weight, *pieces)


def order_kernel(me_ref, w_ref, first_ref, last_ref, sems):
    copies = []
    for relation in range(w_ref.shape[0]):
        for n, target in enumerate((first_ref, last_ref)):
            copies.append(
                pltpu.make_async_copy(
                    w_ref.at[me_ref[0] ^ relation, pl.ds(2 * n, 2)],
                    target.at[relation],
                    sems.at[2 * relation + n],
                )
            )
    for copy in copies:
        copy.start()
    for copy in copies:
        copy.wait()


def order_weights(weights):
    groups, heads, depth, columns = weights.shape
    half = jax.ShapeDtypeStruct((groups, heads // 2, depth, columns), weights.dtype)
    myself = lax.axis_index("head").astype(jnp.int32).reshape(1)
    parts = pl.pallas_call(
        order_kernel,
        out_shape=[half, half],
        in_specs=[SMEM, ANY],
        out_specs=[ANY, ANY],
        scratch_shapes=[pltpu.SemaphoreType.DMA((2 * groups,))],
        compiler_params=params(),
        cost_estimate=cost(0),
        name="order_weights",
    )(myself, weights)
    return [part.reshape(-1, columns) for part in parts]


def key_list(shard, global_ids, rand_ids, local_blocks, shards):
    total_blocks = local_blocks * shards
    block_ids = shard * local_blocks + jnp.arange(local_blocks, dtype=jnp.int32)
    near = block_ids[:, None] + jnp.arange(-1, 2, dtype=jnp.int32)[None, :]
    inside = (near >= 0) & (near < total_blocks)
    listed = lax.dynamic_slice_in_dim(rand_ids, shard * local_blocks, local_blocks, 0)
    glob = jnp.broadcast_to(global_ids[None, :], (local_blocks, NGLOBAL))
    ids = jnp.concatenate([jnp.clip(near, 0, total_blocks - 1), glob, listed], axis=1)
    inside = jnp.concatenate(
        [inside, jnp.ones((local_blocks, NGLOBAL + NRANDOM), jnp.bool_)], axis=1
    )
    return ids, inside


def guests_first(guests, source, global_ids, rand_ids, local_blocks, shards):
    ids, inside = key_list(guests, global_ids, rand_ids, local_blocks, shards)
    order = jnp.arange(local_blocks, dtype=jnp.int32)
    blocks = source * local_blocks + order
    hits = (ids[None] == blocks[:, None, None]) & inside[None]
    listed = jnp.max(hits.astype(jnp.int32), axis=(1, 2))
    earlier = (order[None, :] < order[:, None]).astype(jnp.int32)
    among = jnp.sum(earlier * listed[None, :], axis=1)
    return jnp.where(listed > 0, among, jnp.sum(listed) + order - among)


def key_places(shard, myself, global_ids, rand_ids, local_blocks, shards, diagonal=None):
    half = shards // 2
    ids, inside = key_list(shard, global_ids, rand_ids, local_blocks, shards)
    owner = ids // local_blocks
    here = ((owner // half) == (myself // half)) & inside
    relative = (owner ^ myself) & (half - 1)
    block = ids % local_blocks
    if diagonal is not None:
        order = jnp.arange(local_blocks, dtype=jnp.int32)
        moved = jnp.sum(jnp.where(block[..., None] == order, diagonal, 0), axis=-1)
        block = jnp.where(relative == half - 1, moved, block)
    starts = jnp.where(here, (relative * local_blocks + block) * BLOCK, 0)
    bias = jnp.repeat(jnp.where(here, 0.0, MASKED).astype(jnp.float32), BLOCK, axis=1)
    return starts.reshape(-1).astype(jnp.int32), bias


def split_kernel(order_ref, pair_ref, first_ref, rest_ref):
    blocks = first_ref.shape[1] // BLOCK
    for n in range(pair_ref.shape[1] // BLOCK):
        source = pl.ds(pl.multiple_of(order_ref[n] * BLOCK, BLOCK), BLOCK)
        target = first_ref if n < blocks else rest_ref
        target[:, pl.ds((n % blocks) * BLOCK, BLOCK), :] = pair_ref[:, source, :]


def split_call(order, pair):
    half = jax.ShapeDtypeStruct((2, pair.shape[1] // 2, pair.shape[2]), pair.dtype)
    return pl.pallas_call(
        split_kernel,
        out_shape=[half, half],
        in_specs=[SMEM, VMEM],
        out_specs=[VMEM, VMEM],
        compiler_params=params(),
        cost_estimate=cost(0),
        name="guests_first",
    )(order, pair)


def swap(value, distance, shards):
    return lax.ppermute(value, "seq", [(i, i ^ distance) for i in range(shards)])


def after(value, *tokens):
    return lax.optimization_barrier((value, *tokens))[0]


def hop(value, distance, groups):
    return lax.ppermute(value, "head", [(i, i ^ distance) for i in range(groups)])


def together(*values):
    return lax.optimization_barrier(values)


UNROLL = 12
GUEST_US = 0.1
PROJECT_US = 4
UPPER_TILES = 4


def halves_body(queries, keys_values, global_ids, rand_ids, out_weight):
    rows, width = queries.shape
    heads_here = width // HEAD_DIM
    local_blocks = rows // BLOCK
    shards = lax.axis_size("seq")
    myself = lax.axis_index("seq")
    groups = lax.axis_size("head")
    opposite = shards // 2

    def column(array, head):
        return lax.slice_in_dim(array, head * HEAD_DIM, (head + 1) * HEAD_DIM, axis=array.ndim - 1)

    def over_y(value):
        return swap(value, 1, shards)

    def over_z(value):
        return swap(value, 2, shards)

    def across(value):
        return swap(value, opposite, shards)

    lists = (global_ids, rand_ids, local_blocks, shards)
    mine = guests_first(myself ^ opposite, myself ^ 3, *lists)
    theirs = guests_first(myself ^ opposite ^ 1, myself ^ 2, *lists)
    count = jnp.arange(local_blocks, dtype=jnp.int32)
    order = jnp.sum(jnp.where(theirs[None, :] == count[:, None], count[None, :], 0), axis=1)
    home = key_places(myself, myself, *lists)
    guest = key_places(myself ^ opposite, myself, *lists)
    last_home = key_places(myself, myself, *lists, mine)
    last_guest = key_places(myself ^ opposite, myself, *lists, mine)
    home, guest = (*home, *last_home, order), (*guest, *last_guest)
    weights = order_weights(
        out_weight.reshape(groups, heads_here, HEAD_DIM, out_weight.shape[1])
    )
    k0 = column(keys_values, 0)
    others = after(keys_values, k0)
    k1, k2, k3 = [column(others, h) for h in range(1, heads_here)]
    q0, q1, q2, q3 = [column(queries, h) for h in range(heads_here)]

    y0, z0 = over_y(k0), over_z(k0)
    y0, z0, k1_, v0, v1, home, guest = together(y0, z0, k1, q0, q1, home, guest)

    d0, y1, z1, v0, v1 = over_y(z0), over_y(k1_), over_z(k1_), across(v0), across(v1)
    p0 = (k0, y0, z0, d0)
    (s0,) = guest_call(*guest[:2], v0, p0)
    t0, y1, z1, v1, k2_, v2, weights = together(s0, y1, z1, v1, k2, q2, weights)

    d1, y2, z2, v2, g0 = over_y(z1), over_y(k2_), over_z(k2_), across(v2), across(s0)
    m0 = home_call(*home[:2], after(q0, t0), p0)
    p1 = (k1, y1, z1, d1)
    (s1,) = guest_call(*guest[:2], after(v1, m0[1], v2), p1)
    t1, y2, z2, v2, g0, k3_, v3 = together(s1, y2, z2, v2, g0, k3, q3)

    d2, y3, z3, v3, g1 = over_y(z2), over_y(k3_), over_z(k3_), across(v3), across(s1)
    m1 = home_call(*home[:2], after(q1, t1), p1)
    (a0,) = merge_call(*m0, after(g0, m1[1]))
    a0x, a0c = hop(a0, 2, groups), hop(a0, 1, groups)
    p2 = (k2, y2, z2, d2)
    (s2,) = guest_call(*guest[:2], after(v2, m1[1], v3), p2)
    t2, y3, z3, v3, g1, a0x, a0c = together(s2, y3, z3, v3, g1, a0x, a0c)

    first, rest = split_call(home[4], z3)
    d3, d3_, g2 = over_y(first), over_y(rest), across(s2)
    m2 = home_call(*home[:2], after(q2, t2), p2)
    (a1,) = merge_call(*m1, after(g1, m2[1]))
    a1x, a1c, a0d = hop(a1, 2, groups), hop(a1, 1, groups), hop(a0x, 1, groups)
    (s3,) = guest_call(*guest[2:4], after(v3, a1), (k3, y3, z3, d3))
    g3 = across(after(s3, g2))
    m3 = home_call(*home[2:4], after(q3, s3), (k3, y3, z3, d3, d3_))
    (a2,) = merge_call(*m2, after(g2, m3[1]))
    a1d = hop(after(a1x, s3), 1, groups)
    a2x, a2c = hop(a2, 2, groups), hop(a2, 1, groups)
    early = ((a0, a0c, a0x, a0d), (a1, a1c, a1x, a1d))
    summed = first_terms(early, after(weights[0], m3[1]))

    tiles = rows // ROW_TILE
    tiles_a = UPPER_TILES
    sizes = [tiles_a * ROW_TILE, (tiles - tiles_a) * ROW_TILE]
    a3a, a3b = merge_call(*m3, after(g3, summed), sizes)
    a3ax, a3ac = hop(a3a, 2, groups), hop(a3a, 1, groups)
    a3bx, a3bc = hop(after(a3b, a3a), 2, groups), hop(a3b, 1, groups)
    a2d = hop(after(a2x, a3b), 1, groups)
    a2 = (a2, a2c, a2x, a2d)
    a3ad = hop(a3ax, 1, groups)
    upper = last_terms(summed, (a2, (a3a, a3ac, a3ax, a3ad)), weights[1], (0, tiles_a))
    a3bd = hop(after(a3bx, upper), 1, groups)
    late = (a2, (a3b, a3bc, a3bx, a3bd))
    return last_terms(summed, late, weights[1], (tiles_a, tiles - tiles_a), upper)


def padded_2(block, sides, width):
    for axis, dim in sides:
        count = lax.axis_size(axis)
        forward = [(i, i + 1) for i in range(count - 1)]
        backward = [(target, source) for source, target in forward]
        low = lax.ppermute(
            lax.slice_in_dim(block, block.shape[dim] - width, None, axis=dim), axis, forward
        )
        high = lax.ppermute(lax.slice_in_dim(block, 0, width, axis=dim), axis, backward)
        block = jnp.concatenate([low, block, high], axis=dim)
    return block


def broadcast(block, axis, owner):
    block = jnp.where(lax.axis_index(axis) == owner, block, jnp.zeros_like(block))
    return lax.psum(block, axis)


def plan_slots(requests, myself, capacity, per_shard):
    sources = requests // per_shard
    offsets = requests % per_shard
    count = requests.shape[1]
    order = jnp.arange(count, dtype=jnp.int32)
    earlier = (order[:, None] < order[None, :]).astype(jnp.int32)
    matches = (sources[:, :, None] == sources[:, None, :]).astype(jnp.int32)
    ranks = jnp.sum(matches * earlier[None], axis=1)
    slot_range = jnp.arange(capacity, dtype=jnp.int32)
    wanted = (
        (sources == myself)[:, None, :] & (ranks[:, None, :] == slot_range[None, :, None])
    ).astype(jnp.int32)
    chosen = jnp.sum(wanted * offsets[:, None, :], axis=2).reshape(-1)
    own_sources = lax.dynamic_index_in_dim(sources, myself, 0, keepdims=False)
    own_ranks = lax.dynamic_index_in_dim(ranks, myself, 0, keepdims=False)
    return (chosen, own_sources * capacity + own_ranks)


def attend_blocks(query_part, local_keys, local_values, glob_keys, glob_values, valid):
    scale = 1.0 / HEAD_DIM**0.5
    near_scores = (
        jnp.einsum("bqhd,bkhd->bhqk", query_part, local_keys, preferred_element_type=jnp.float32)
        * scale
    )
    near_scores = jnp.where(valid[:, None, None, :], near_scores, -jnp.inf)
    glob_scores = (
        jnp.einsum("bqhd,khd->bhqk", query_part, glob_keys, preferred_element_type=jnp.float32)
        * scale
    )
    highest = jnp.maximum(jnp.max(near_scores, axis=-1), jnp.max(glob_scores, axis=-1))
    near_exp = jnp.exp(near_scores - highest[..., None])
    glob_exp = jnp.exp(glob_scores - highest[..., None])
    total = jnp.sum(near_exp, axis=-1) + jnp.sum(glob_exp, axis=-1)
    near_weights = (near_exp / total[..., None]).astype(jnp.bfloat16)
    glob_weights = (glob_exp / total[..., None]).astype(jnp.bfloat16)
    mixed = jnp.einsum(
        "bhqk,bkhd->bqhd", near_weights, local_values, preferred_element_type=jnp.float32
    )
    mixed = mixed + jnp.einsum(
        "bhqk,khd->bqhd", glob_weights, glob_values, preferred_element_type=jnp.float32
    )
    return mixed.astype(jnp.bfloat16)


def exchange_body(queries, keys_values, global_ids, rand_ids, out_weight):
    rows = queries.shape[0]
    width = queries.shape[1]
    heads_here = width // HEAD_DIM
    local_blocks = rows // BLOCK
    shards = lax.axis_size("seq")
    myself = lax.axis_index("seq")
    total_blocks = local_blocks * shards
    pair_blocks = keys_values.reshape(2, local_blocks, BLOCK, width)
    padded = padded_2(keys_values, (("seq", 1),), BLOCK)
    padded = padded.reshape(2, local_blocks + 2, BLOCK, width)
    panel_list = []
    for which in range(NGLOBAL):
        target = global_ids[which]
        owner = target // local_blocks
        local_panel = lax.dynamic_index_in_dim(
            pair_blocks, target % local_blocks, 1, keepdims=False
        )
        panel_list.append(broadcast(local_panel, "seq", owner))
    glob = jnp.stack(panel_list, axis=1).reshape(2, NGLOBAL * BLOCK, heads_here, HEAD_DIM)
    requests = rand_ids.reshape(shards, local_blocks, NRANDOM)
    capacity = (local_blocks + shards - 1) // shards
    fetched = []
    for column in range(NRANDOM):
        chosen, slots = plan_slots(requests[:, :, column], myself, capacity, local_blocks)
        outgoing = jnp.take(pair_blocks, chosen, axis=1)
        incoming = lax.all_to_all(outgoing, "seq", split_axis=1, concat_axis=1, tiled=True)
        fetched.append(jnp.take(incoming, slots, axis=1))
    remote = jnp.stack(fetched, axis=2)
    segment = jnp.arange((3 + NRANDOM) * BLOCK, dtype=jnp.int32) // BLOCK

    def one_group(index):
        first = index * group_blocks
        query_part = lax.dynamic_slice_in_dim(queries, first * BLOCK, group_blocks * BLOCK, 0)
        query_part = query_part.reshape(group_blocks, BLOCK, heads_here, HEAD_DIM)
        window = lax.dynamic_slice_in_dim(padded, first, group_blocks + 2, 1)
        farther = lax.dynamic_slice_in_dim(remote, first, group_blocks, 1)
        farther = farther.reshape(2, group_blocks, NRANDOM * BLOCK, width)
        local = jnp.concatenate(
            [
                window[:, 0:group_blocks],
                window[:, 1 : group_blocks + 1],
                window[:, 2 : group_blocks + 2],
                farther,
            ],
            axis=2,
        )
        local = local.reshape(2, group_blocks, (3 + NRANDOM) * BLOCK, heads_here, HEAD_DIM)
        block_ids = myself * local_blocks + first + jnp.arange(group_blocks, dtype=jnp.int32)
        drop_before = (segment[None, :] == 0) & (block_ids[:, None] == 0)
        drop_after = (segment[None, :] == 2) & (block_ids[:, None] == total_blocks - 1)
        valid = jnp.logical_not(drop_before | drop_after)
        mixed = attend_blocks(query_part, local[0], local[1], glob[0], glob[1], valid)
        return mixed.reshape(group_blocks * BLOCK, width)

    attended = lax.map(
        one_group, jnp.arange(local_blocks // group_blocks, dtype=jnp.int32)
    ).reshape(rows, width)
    summed = jnp.dot(
        lax.all_gather(attended, "head", axis=1, tiled=True),
        out_weight,
        preferred_element_type=jnp.float32,
    )
    return summed.astype(jnp.bfloat16)


def solution(mesh):
    body = halves_body if dict(mesh.shape) == {"seq": 8, "head": 4} else exchange_body
    in_specs = (P("seq", "head"), P(None, "seq", "head"), P(), P(), P(None, "head"))
    out_specs = P("seq", "head")
    return jax.shard_map(body, mesh=mesh, in_specs=in_specs, out_specs=out_specs, check_vma=False)
```

```python
import functools

import jax
import jax.numpy as jnp
from jax import lax
from jax.experimental import pallas as pl
from jax.experimental.pallas import tpu as pltpu
from jax.sharding import PartitionSpec as P

HEAD_DIM = 128
BLOCK = 64
NGLOBAL = 2
NRANDOM = 3
NLIST = 3 + NGLOBAL + NRANDOM
MASKED = -1e30
EXP2_SCALE = 1.4426950408889634 / HEAD_DIM**0.5
STAT_TILE = 16
VMEM_LIMIT = 20 * 1024 * 1024
PROJECT_LIMIT = 32 * 1024 * 1024


group_blocks = 8


def eye_mask():
    rows = lax.broadcasted_iota(jnp.int32, (BLOCK, BLOCK), 0)
    columns = lax.broadcasted_iota(jnp.int32, (BLOCK, BLOCK), 1)
    return rows == columns


def attend_group(blocks, head, starts_ref, bias_ref, q_ref, pool):
    lanes = pl.ds(head * HEAD_DIM, HEAD_DIM)
    listed = [
        [
            pl.ds(pl.multiple_of(starts_ref[i * NLIST + e], BLOCK), BLOCK)
            for e in range(NLIST)
        ]
        for i in blocks
    ]
    places = [pl.ds(pl.multiple_of(i * BLOCK, BLOCK), BLOCK) for i in blocks]
    scores = []
    for i, rows, listing in zip(blocks, places, listed):
        keys = jnp.concatenate([pool[0, w, lanes] for w in listing], axis=0)
        product = lax.dot_general(
            q_ref[rows, lanes],
            keys,
            (((1,), (1,)), ((), ())),
            preferred_element_type=jnp.float32,
        )
        scores.append(product + bias_ref[pl.ds(i, 1), :])
    weighed = []
    for score in scores:
        highest = jnp.max(score, axis=1, keepdims=True)
        weights = jnp.exp2((score - highest) * EXP2_SCALE)
        total = jnp.sum(weights, axis=1, keepdims=True)
        weighed.append((weights.astype(jnp.bfloat16), highest, total))
    results = []
    for listing, (weights, highest, total) in zip(listed, weighed):
        values = jnp.concatenate([pool[1, w, lanes] for w in listing], axis=0)
        mixed = jnp.dot(weights, values, preferred_element_type=jnp.float32)
        results.append((lanes, mixed, highest, total))
    return results


def put_stats(i, head, stats_ref, highest, total):
    eye = eye_mask()
    high_row = jnp.sum(jnp.where(eye, highest, 0.0), axis=0, keepdims=True)
    total_row = jnp.sum(jnp.where(eye, total, 0.0), axis=0, keepdims=True)
    stats_ref[head, pl.ds(i, 1), :] = jnp.concatenate([high_row, total_row], axis=1)


def load_pool(parts, pool, sems):
    copies, low = [], 0
    for n, part in enumerate(parts):
        size = part.shape[1]
        copies.append(
            pltpu.make_async_copy(part, pool.at[:, pl.ds(low, size), :], sems.at[n])
        )
        low += size
    for copy in copies:
        copy.start()
    for copy in copies:
        copy.wait()


def attend_part(part, parts, starts_ref, bias_ref, q_ref, pool, mixed_ref, stats_ref, normalise):
    blocks = q_ref.shape[0] // BLOCK // parts
    unroll = UNROLL if blocks % UNROLL == 0 else blocks
    stats_ref[...] = jnp.zeros_like(stats_ref)

    for head in range(q_ref.shape[1] // HEAD_DIM):

        def step(n, _):
            ids = [n * unroll + u for u in range(unroll)]
            results = attend_group(
                [part * blocks + i for i in ids], head, starts_ref, bias_ref, q_ref, pool
            )
            for i, (lanes, mixed, highest, total) in zip(ids, results):
                rows = pl.ds(pl.multiple_of(i * BLOCK, BLOCK), BLOCK)
                mixed = mixed / total if normalise else mixed
                mixed_ref[rows, lanes] = mixed.astype(mixed_ref.dtype)
                put_stats(i, head, stats_ref, highest, total)
            return 0

        lax.fori_loop(0, blocks // unroll, step, 0)


def guest_kernel(parts, count, starts_ref, bias_ref, q_ref, *refs):
    *message_refs, pool, stats, sems = refs[count:]
    load_pool(refs[:count], pool, sems)
    base = q_ref.shape[0] // parts
    for part, message_ref in enumerate(message_refs):
        attend_part(part, parts, starts_ref, bias_ref, q_ref, pool, message_ref, stats, True)
        for head in range(q_ref.shape[1] // HEAD_DIM):
            rest = stats[head]
            for n in range(3):
                piece = rest.astype(jnp.bfloat16)
                rows = pl.ds(base + n * rest.shape[0], rest.shape[0])
                message_ref[rows, pl.ds(head * HEAD_DIM, HEAD_DIM)] = piece
                rest = rest - piece.astype(jnp.float32)


def home_kernel(parts, count, starts_ref, bias_ref, q_ref, *refs):
    *result_refs, pool, sems = refs[count:]
    load_pool(refs[:count], pool, sems)
    for part in range(parts):
        mixed_ref, stats_ref = result_refs[2 * part : 2 * part + 2]
        attend_part(part, parts, starts_ref, bias_ref, q_ref, pool, mixed_ref, stats_ref, False)


def merge_kernel(mixed_ref, stats_ref, message_ref, *refs):
    *out_refs, home_scale, guest_scale = refs
    base, width = mixed_ref.shape
    blocks = base // BLOCK
    size = stats_ref.shape[1]
    other = message_ref[pl.ds(base, size), :].astype(jnp.float32)
    for n in (1, 2):
        other = other + message_ref[pl.ds(base + n * size, size), :].astype(jnp.float32)
    eye = eye_mask()
    for head in range(width // HEAD_DIM):
        low = head * HEAD_DIM
        lanes = pl.ds(low, HEAD_DIM)
        high_h = stats_ref[head, :, :BLOCK]
        total_h = stats_ref[head, :, BLOCK:]
        high_g = other[:, low : low + BLOCK]
        total_g = other[:, low + BLOCK : low + HEAD_DIM]
        highest = jnp.maximum(high_h, high_g)
        factor_h = jnp.exp2((high_h - highest) * EXP2_SCALE)
        factor_g = jnp.exp2((high_g - highest) * EXP2_SCALE) * total_g
        total = factor_h * total_h + factor_g
        total = jnp.where(total > 0, total, 1.0)
        home_scale[...] = factor_h / total
        guest_scale[...] = factor_g / total

        def step(n, part, low):
            i = low + n
            rows = pl.ds(pl.multiple_of(i * BLOCK, BLOCK), BLOCK)
            scale_h = jnp.sum(
                jnp.where(eye, home_scale[pl.ds(i, 1), :], 0.0), axis=1, keepdims=True
            )
            scale_g = jnp.sum(
                jnp.where(eye, guest_scale[pl.ds(i, 1), :], 0.0), axis=1, keepdims=True
            )
            mixed = (
                mixed_ref[rows, lanes] * scale_h
                + message_ref[rows, lanes].astype(jnp.float32) * scale_g
            )
            rows = pl.ds(pl.multiple_of(n * BLOCK, BLOCK), BLOCK)
            out_refs[part][rows, lanes] = mixed.astype(jnp.bfloat16)

        low = 0
        for part, out_ref in enumerate(out_refs):

            def body(n, _, part=part, low=low):
                step(n, part, low)
                return 0

            count = out_ref.shape[0] // BLOCK
            lax.fori_loop(0, count, body, 0, unroll=4)
            low += count


def last_terms_kernel(groups, w_ref, sum_ref, *refs):
    x_refs, out_ref = refs[: 2 * groups], refs[-1]
    ordered = [x_refs[h * groups + r][...] for r in range(groups) for h in range(2)]
    term = jnp.dot(
        jnp.concatenate(ordered, axis=1), w_ref[...], preferred_element_type=jnp.float32
    )
    out_ref[...] = (sum_ref[...] + term).astype(out_ref.dtype)


VMEM = pl.BlockSpec(memory_space=pltpu.VMEM)
SMEM = pl.BlockSpec(memory_space=pltpu.SMEM)
ANY = pl.BlockSpec(memory_space=pl.ANY)
HBM = pl.BlockSpec(memory_space=pltpu.HBM)


def params():
    return pltpu.CompilerParams(vmem_limit_bytes=VMEM_LIMIT)


def pool_scratch(query):
    return pltpu.VMEM((2, 4 * query.shape[0], query.shape[1]), jnp.bfloat16)


def stats_shape(query, parts, kind):
    blocks = query.shape[0] // BLOCK // parts
    size = -(-blocks // STAT_TILE) * STAT_TILE
    return kind((query.shape[1] // HEAD_DIM, size, 2 * BLOCK), jnp.float32)


def cost(micros):
    return pl.CostEstimate(flops=int(micros * 1.15e9), bytes_accessed=0, transcendentals=0)


def guest_call(starts, bias, query, pieces, parts=1):
    rows, width = query.shape
    size = stats_shape(query, parts, jax.ShapeDtypeStruct).shape[1]
    message = jax.ShapeDtypeStruct((rows // parts + 3 * size, width), jnp.bfloat16)
    return pl.pallas_call(
        functools.partial(guest_kernel, parts, len(pieces)),
        out_shape=[message] * parts,
        in_specs=[SMEM, VMEM, VMEM] + [ANY] * len(pieces),
        out_specs=[VMEM] * parts,
        scratch_shapes=[
            pool_scratch(query),
            stats_shape(query, parts, pltpu.VMEM),
            pltpu.SemaphoreType.DMA((len(pieces),)),
        ],
        compiler_params=params(),
        cost_estimate=cost(GUEST_US),
        name="guest_attention",
    )(starts, bias, query, *pieces)


def home_call(starts, bias, query, pieces, parts=1):
    rows, width = query.shape
    results = [
        jax.ShapeDtypeStruct((rows // parts, width), jnp.float32),
        stats_shape(query, parts, jax.ShapeDtypeStruct),
    ]
    return pl.pallas_call(
        functools.partial(home_kernel, parts, len(pieces)),
        out_shape=results * parts,
        in_specs=[SMEM, VMEM, VMEM] + [ANY] * len(pieces),
        out_specs=[VMEM] * (2 * parts),
        scratch_shapes=[pool_scratch(query), pltpu.SemaphoreType.DMA((len(pieces),))],
        compiler_params=params(),
        cost_estimate=cost(0),
        name="home_attention",
    )(starts, bias, query, *pieces)


def merge_call(mixed, stats, message, sizes=None):
    rows, width = mixed.shape
    sizes = sizes or [rows]
    return pl.pallas_call(
        merge_kernel,
        out_shape=[jax.ShapeDtypeStruct((size, width), jnp.bfloat16) for size in sizes],
        in_specs=[VMEM, VMEM, VMEM],
        out_specs=[VMEM] * len(sizes),
        scratch_shapes=[
            pltpu.VMEM((stats.shape[1], BLOCK), jnp.float32),
            pltpu.VMEM((stats.shape[1], BLOCK), jnp.float32),
        ],
        compiler_params=params(),
        cost_estimate=cost(0),
        name="merge_halves",
    )(mixed, stats, message)


ROW_TILE = 256


def last_terms(summed, gathered, weight, part, filled=None):
    rows, columns = summed.shape
    first, tiles = part
    pieces = [piece for group in gathered for piece in group]

    def row_spec(height, width):
        low = first if height == rows else 0
        return pl.BlockSpec((ROW_TILE, width), lambda i: (i + low, 0))

    others = [] if filled is None else [filled]
    return pl.pallas_call(
        functools.partial(last_terms_kernel, len(pieces) // 2),
        grid=(tiles,),
        out_shape=jax.ShapeDtypeStruct((rows, columns), jnp.bfloat16),
        in_specs=[VMEM]
        + [row_spec(*v.shape) for v in [summed, *pieces]]
        + [ANY] * len(others),
        out_specs=row_spec(rows, columns),
        input_output_aliases={2 + len(pieces): 0} if others else {},
        compiler_params=params(),
        cost_estimate=cost(PROJECT_US),
        name="last_terms",
    )(weight, summed, *pieces, *others)


def first_terms_kernel(groups, w_ref, *refs):
    x_refs, (out_ref, columns, sems) = refs[: 2 * groups], refs[2 * groups :]
    copies = [
        pltpu.make_async_copy(
            x_refs[head * groups + relation],
            columns.at[:, pl.ds((2 * relation + head) * HEAD_DIM, HEAD_DIM)],
            sems.at[2 * relation + head],
        )
        for relation in range(groups)
        for head in range(2)
    ]
    for copy in copies:
        copy.start()
    for copy in copies:
        copy.wait()

    def step(i, _):
        rows = pl.ds(pl.multiple_of(i * ROW_TILE, ROW_TILE), ROW_TILE)
        out_ref[rows, :] = jnp.dot(
            columns[rows, :], w_ref[...], preferred_element_type=jnp.float32
        )
        return 0

    lax.fori_loop(0, out_ref.shape[0] // ROW_TILE, step, 0)


def first_terms(gathered, weight):
    pieces = [piece for group in gathered for piece in group]
    rows = pieces[0].shape[0]
    return pl.pallas_call(
        functools.partial(first_terms_kernel, len(pieces) // 2),
        out_shape=jax.ShapeDtypeStruct((rows, weight.shape[1]), jnp.float32),
        in_specs=[VMEM] + [ANY] * len(pieces),
        out_specs=VMEM,
        scratch_shapes=[
            pltpu.VMEM((rows, weight.shape[0]), jnp.bfloat16),
            pltpu.SemaphoreType.DMA((len(pieces),)),
        ],
        compiler_params=params(),
        cost_estimate=cost(0),
        name="first_terms",
    )(weight, *pieces)


def order_kernel(me_ref, w_ref, first_ref, last_ref, sems):
    copies = []
    for relation in range(w_ref.shape[0]):
        for n, target in enumerate((first_ref, last_ref)):
            copies.append(
                pltpu.make_async_copy(
                    w_ref.at[me_ref[0] ^ relation, pl.ds(2 * n, 2)],
                    target.at[relation],
                    sems.at[2 * relation + n],
                )
            )
    for copy in copies:
        copy.start()
    for copy in copies:
        copy.wait()


def order_weights(weights):
    groups, heads, depth, columns = weights.shape
    half = jax.ShapeDtypeStruct((groups, heads // 2, depth, columns), weights.dtype)
    myself = lax.axis_index("head").astype(jnp.int32).reshape(1)
    parts = pl.pallas_call(
        order_kernel,
        out_shape=[half, half],
        in_specs=[SMEM, ANY],
        out_specs=[ANY, ANY],
        scratch_shapes=[pltpu.SemaphoreType.DMA((2 * groups,))],
        compiler_params=params(),
        cost_estimate=cost(0),
        name="order_weights",
    )(myself, weights)
    return [part.reshape(-1, columns) for part in parts]


def key_list(shard, global_ids, rand_ids, local_blocks, shards):
    total_blocks = local_blocks * shards
    block_ids = shard * local_blocks + jnp.arange(local_blocks, dtype=jnp.int32)
    near = block_ids[:, None] + jnp.arange(-1, 2, dtype=jnp.int32)[None, :]
    inside = (near >= 0) & (near < total_blocks)
    listed = lax.dynamic_slice_in_dim(rand_ids, shard * local_blocks, local_blocks, 0)
    glob = jnp.broadcast_to(global_ids[None, :], (local_blocks, NGLOBAL))
    ids = jnp.concatenate([jnp.clip(near, 0, total_blocks - 1), glob, listed], axis=1)
    inside = jnp.concatenate(
        [inside, jnp.ones((local_blocks, NGLOBAL + NRANDOM), jnp.bool_)], axis=1
    )
    return ids, inside


def guests_first(guests, source, global_ids, rand_ids, local_blocks, shards):
    ids, inside = key_list(guests, global_ids, rand_ids, local_blocks, shards)
    order = jnp.arange(local_blocks, dtype=jnp.int32)
    blocks = source * local_blocks + order
    hits = (ids[None] == blocks[:, None, None]) & inside[None]
    listed = jnp.max(hits.astype(jnp.int32), axis=(1, 2))
    earlier = (order[None, :] < order[:, None]).astype(jnp.int32)
    among = jnp.sum(earlier * listed[None, :], axis=1)
    return jnp.where(listed > 0, among, jnp.sum(listed) + order - among)


def key_places(shard, myself, global_ids, rand_ids, local_blocks, shards, diagonal=None):
    half = shards // 2
    ids, inside = key_list(shard, global_ids, rand_ids, local_blocks, shards)
    owner = ids // local_blocks
    here = ((owner // half) == (myself // half)) & inside
    relative = (owner ^ myself) & (half - 1)
    block = ids % local_blocks
    if diagonal is not None:
        order = jnp.arange(local_blocks, dtype=jnp.int32)
        moved = jnp.sum(jnp.where(block[..., None] == order, diagonal, 0), axis=-1)
        block = jnp.where(relative == half - 1, moved, block)
    starts = jnp.where(here, (relative * local_blocks + block) * BLOCK, 0)
    bias = jnp.repeat(jnp.where(here, 0.0, MASKED).astype(jnp.float32), BLOCK, axis=1)
    return starts.reshape(-1).astype(jnp.int32), bias


def split_kernel(order_ref, pair_ref, first_ref, rest_ref):
    blocks = first_ref.shape[1] // BLOCK
    for n in range(pair_ref.shape[1] // BLOCK):
        source = pl.ds(pl.multiple_of(order_ref[n] * BLOCK, BLOCK), BLOCK)
        target = first_ref if n < blocks else rest_ref
        target[:, pl.ds((n % blocks) * BLOCK, BLOCK), :] = pair_ref[:, source, :]


def split_call(order, pair):
    half = jax.ShapeDtypeStruct((2, pair.shape[1] // 2, pair.shape[2]), pair.dtype)
    return pl.pallas_call(
        split_kernel,
        out_shape=[half, half],
        in_specs=[SMEM, VMEM],
        out_specs=[VMEM, VMEM],
        compiler_params=params(),
        cost_estimate=cost(0),
        name="guests_first",
    )(order, pair)


def swap(value, distance, shards):
    return lax.ppermute(value, "seq", [(i, i ^ distance) for i in range(shards)])


def after(value, *tokens):
    return lax.optimization_barrier((value, *tokens))[0]


def hop(value, distance, groups):
    return lax.ppermute(value, "head", [(i, i ^ distance) for i in range(groups)])


def together(*values):
    return lax.optimization_barrier(values)


UNROLL = 12
GUEST_US = 0.1
PROJECT_US = 4
UPPER_TILES = 4


def halves_body(queries, keys_values, global_ids, rand_ids, out_weight):
    rows, width = queries.shape
    heads_here = width // HEAD_DIM
    local_blocks = rows // BLOCK
    shards = lax.axis_size("seq")
    myself = lax.axis_index("seq")
    groups = lax.axis_size("head")
    opposite = shards // 2

    def column(array, head):
        return lax.slice_in_dim(array, head * HEAD_DIM, (head + 1) * HEAD_DIM, axis=array.ndim - 1)

    def over_y(value):
        return swap(value, 1, shards)

    def over_z(value):
        return swap(value, 2, shards)

    def across(value):
        return swap(value, opposite, shards)

    lists = (global_ids, rand_ids, local_blocks, shards)
    mine = guests_first(myself ^ opposite, myself ^ 3, *lists)
    theirs = guests_first(myself ^ opposite ^ 1, myself ^ 2, *lists)
    count = jnp.arange(local_blocks, dtype=jnp.int32)
    order = jnp.sum(jnp.where(theirs[None, :] == count[:, None], count[None, :], 0), axis=1)
    home = key_places(myself, myself, *lists)
    guest = key_places(myself ^ opposite, myself, *lists)
    last_home = key_places(myself, myself, *lists, mine)
    last_guest = key_places(myself ^ opposite, myself, *lists, mine)
    home, guest = (*home, *last_home, order), (*guest, *last_guest)
    weights = order_weights(
        out_weight.reshape(groups, heads_here, HEAD_DIM, out_weight.shape[1])
    )
    k0 = column(keys_values, 0)
    others = after(keys_values, k0)
    k1, k2, k3 = [column(others, h) for h in range(1, heads_here)]
    q0, q1, q2, q3 = [column(queries, h) for h in range(heads_here)]

    y0, z0 = over_y(k0), over_z(k0)
    y0, z0, k1_, v0, v1, home, guest = together(y0, z0, k1, q0, q1, home, guest)

    d0, y1, z1, v0, v1 = over_y(z0), over_y(k1_), over_z(k1_), across(v0), across(v1)
    p0 = (k0, y0, z0, d0)
    (s0,) = guest_call(*guest[:2], v0, p0)
    t0, y1, z1, v1, k2_, v2, weights = together(s0, y1, z1, v1, k2, q2, weights)

    d1, y2, z2, v2, g0 = over_y(z1), over_y(k2_), over_z(k2_), across(v2), across(s0)
    m0 = home_call(*home[:2], after(q0, t0), p0)
    p1 = (k1, y1, z1, d1)
    (s1,) = guest_call(*guest[:2], after(v1, m0[1]), p1)
    t1, y2, z2, v2, g0, k3_, v3 = together(s1, y2, z2, v2, g0, k3, q3)

    d2, y3, z3, v3, g1 = over_y(z2), over_y(k3_), over_z(k3_), across(v3), across(s1)
    m1 = home_call(*home[:2], after(q1, t1), p1)
    (a0,) = merge_call(*m0, after(g0, m1[1]))
    a0x, a0c = hop(a0, 2, groups), hop(a0, 1, groups)
    p2 = (k2, y2, z2, d2)
    (s2,) = guest_call(*guest[:2], after(v2, m1[1], v3), p2)
    t2, y3, z3, v3, g1, a0x, a0c = together(s2, y3, z3, v3, g1, a0x, a0c)

    first, rest = split_call(home[4], z3)
    d3, d3_, g2 = over_y(first), over_y(rest), across(s2)
    m2 = home_call(*home[:2], after(q2, t2), p2)
    (a1,) = merge_call(*m1, after(g1, m2[1]))
    a1x, a1c, a0d = hop(a1, 2, groups), hop(a1, 1, groups), hop(a0x, 1, groups)
    (s3,) = guest_call(*guest[2:4], after(v3, a1), (k3, y3, z3, d3))
    g3 = across(after(s3, g2))
    m3 = home_call(*home[2:4], after(q3, s3), (k3, y3, z3, d3, d3_))
    (a2,) = merge_call(*m2, after(g2, m3[1]))
    a1d = hop(after(a1x, s3), 1, groups)
    a2x, a2c = hop(a2, 2, groups), hop(a2, 1, groups)
    early = ((a0, a0c, a0x, a0d), (a1, a1c, a1x, a1d))
    summed = first_terms(early, after(weights[0], m3[1]))

    tiles = rows // ROW_TILE
    tiles_a = UPPER_TILES
    sizes = [tiles_a * ROW_TILE, (tiles - tiles_a) * ROW_TILE]
    a3a, a3b = merge_call(*m3, after(g3, summed), sizes)
    a3ax, a3ac = hop(a3a, 2, groups), hop(a3a, 1, groups)
    a3bx, a3bc = hop(after(a3b, a3a), 2, groups), hop(a3b, 1, groups)
    a2d = hop(after(a2x, a3b), 1, groups)
    a2 = (a2, a2c, a2x, a2d)
    a3ad = hop(a3ax, 1, groups)
    upper = last_terms(summed, (a2, (a3a, a3ac, a3ax, a3ad)), weights[1], (0, tiles_a))
    a3bd = hop(after(a3bx, upper), 1, groups)
    late = (a2, (a3b, a3bc, a3bx, a3bd))
    return last_terms(summed, late, weights[1], (tiles_a, tiles - tiles_a), upper)


def padded_2(block, sides, width):
    for axis, dim in sides:
        count = lax.axis_size(axis)
        forward = [(i, i + 1) for i in range(count - 1)]
        backward = [(target, source) for source, target in forward]
        low = lax.ppermute(
            lax.slice_in_dim(block, block.shape[dim] - width, None, axis=dim), axis, forward
        )
        high = lax.ppermute(lax.slice_in_dim(block, 0, width, axis=dim), axis, backward)
        block = jnp.concatenate([low, block, high], axis=dim)
    return block


def broadcast(block, axis, owner):
    block = jnp.where(lax.axis_index(axis) == owner, block, jnp.zeros_like(block))
    return lax.psum(block, axis)


def plan_slots(requests, myself, capacity, per_shard):
    sources = requests // per_shard
    offsets = requests % per_shard
    count = requests.shape[1]
    order = jnp.arange(count, dtype=jnp.int32)
    earlier = (order[:, None] < order[None, :]).astype(jnp.int32)
    matches = (sources[:, :, None] == sources[:, None, :]).astype(jnp.int32)
    ranks = jnp.sum(matches * earlier[None], axis=1)
    slot_range = jnp.arange(capacity, dtype=jnp.int32)
    wanted = (
        (sources == myself)[:, None, :] & (ranks[:, None, :] == slot_range[None, :, None])
    ).astype(jnp.int32)
    chosen = jnp.sum(wanted * offsets[:, None, :], axis=2).reshape(-1)
    own_sources = lax.dynamic_index_in_dim(sources, myself, 0, keepdims=False)
    own_ranks = lax.dynamic_index_in_dim(ranks, myself, 0, keepdims=False)
    return (chosen, own_sources * capacity + own_ranks)


def attend_blocks(query_part, local_keys, local_values, glob_keys, glob_values, valid):
    scale = 1.0 / HEAD_DIM**0.5
    near_scores = (
        jnp.einsum("bqhd,bkhd->bhqk", query_part, local_keys, preferred_element_type=jnp.float32)
        * scale
    )
    near_scores = jnp.where(valid[:, None, None, :], near_scores, -jnp.inf)
    glob_scores = (
        jnp.einsum("bqhd,khd->bhqk", query_part, glob_keys, preferred_element_type=jnp.float32)
        * scale
    )
    highest = jnp.maximum(jnp.max(near_scores, axis=-1), jnp.max(glob_scores, axis=-1))
    near_exp = jnp.exp(near_scores - highest[..., None])
    glob_exp = jnp.exp(glob_scores - highest[..., None])
    total = jnp.sum(near_exp, axis=-1) + jnp.sum(glob_exp, axis=-1)
    near_weights = (near_exp / total[..., None]).astype(jnp.bfloat16)
    glob_weights = (glob_exp / total[..., None]).astype(jnp.bfloat16)
    mixed = jnp.einsum(
        "bhqk,bkhd->bqhd", near_weights, local_values, preferred_element_type=jnp.float32
    )
    mixed = mixed + jnp.einsum(
        "bhqk,khd->bqhd", glob_weights, glob_values, preferred_element_type=jnp.float32
    )
    return mixed.astype(jnp.bfloat16)


def exchange_body(queries, keys_values, global_ids, rand_ids, out_weight):
    rows = queries.shape[0]
    width = queries.shape[1]
    heads_here = width // HEAD_DIM
    local_blocks = rows // BLOCK
    shards = lax.axis_size("seq")
    myself = lax.axis_index("seq")
    total_blocks = local_blocks * shards
    pair_blocks = keys_values.reshape(2, local_blocks, BLOCK, width)
    padded = padded_2(keys_values, (("seq", 1),), BLOCK)
    padded = padded.reshape(2, local_blocks + 2, BLOCK, width)
    panel_list = []
    for which in range(NGLOBAL):
        target = global_ids[which]
        owner = target // local_blocks
        local_panel = lax.dynamic_index_in_dim(
            pair_blocks, target % local_blocks, 1, keepdims=False
        )
        panel_list.append(broadcast(local_panel, "seq", owner))
    glob = jnp.stack(panel_list, axis=1).reshape(2, NGLOBAL * BLOCK, heads_here, HEAD_DIM)
    requests = rand_ids.reshape(shards, local_blocks, NRANDOM)
    capacity = (local_blocks + shards - 1) // shards
    fetched = []
    for column in range(NRANDOM):
        chosen, slots = plan_slots(requests[:, :, column], myself, capacity, local_blocks)
        outgoing = jnp.take(pair_blocks, chosen, axis=1)
        incoming = lax.all_to_all(outgoing, "seq", split_axis=1, concat_axis=1, tiled=True)
        fetched.append(jnp.take(incoming, slots, axis=1))
    remote = jnp.stack(fetched, axis=2)
    segment = jnp.arange((3 + NRANDOM) * BLOCK, dtype=jnp.int32) // BLOCK

    def one_group(index):
        first = index * group_blocks
        query_part = lax.dynamic_slice_in_dim(queries, first * BLOCK, group_blocks * BLOCK, 0)
        query_part = query_part.reshape(group_blocks, BLOCK, heads_here, HEAD_DIM)
        window = lax.dynamic_slice_in_dim(padded, first, group_blocks + 2, 1)
        farther = lax.dynamic_slice_in_dim(remote, first, group_blocks, 1)
        farther = farther.reshape(2, group_blocks, NRANDOM * BLOCK, width)
        local = jnp.concatenate(
            [
                window[:, 0:group_blocks],
                window[:, 1 : group_blocks + 1],
                window[:, 2 : group_blocks + 2],
                farther,
            ],
            axis=2,
        )
        local = local.reshape(2, group_blocks, (3 + NRANDOM) * BLOCK, heads_here, HEAD_DIM)
        block_ids = myself * local_blocks + first + jnp.arange(group_blocks, dtype=jnp.int32)
        drop_before = (segment[None, :] == 0) & (block_ids[:, None] == 0)
        drop_after = (segment[None, :] == 2) & (block_ids[:, None] == total_blocks - 1)
        valid = jnp.logical_not(drop_before | drop_after)
        mixed = attend_blocks(query_part, local[0], local[1], glob[0], glob[1], valid)
        return mixed.reshape(group_blocks * BLOCK, width)

    attended = lax.map(
        one_group, jnp.arange(local_blocks // group_blocks, dtype=jnp.int32)
    ).reshape(rows, width)
    summed = jnp.dot(
        lax.all_gather(attended, "head", axis=1, tiled=True),
        out_weight,
        preferred_element_type=jnp.float32,
    )
    return summed.astype(jnp.bfloat16)


def solution(mesh):
    body = halves_body if dict(mesh.shape) == {"seq": 8, "head": 4} else exchange_body
    in_specs = (P("seq", "head"), P(None, "seq", "head"), P(), P(), P(None, "head"))
    out_specs = P("seq", "head")
    return jax.shard_map(body, mesh=mesh, in_specs=in_specs, out_specs=out_specs, check_vma=False)
```

```python
import functools

import jax
import jax.numpy as jnp
from jax import lax
from jax.experimental import pallas as pl
from jax.experimental.pallas import tpu as pltpu
from jax.sharding import PartitionSpec as P

HEAD_DIM = 128
BLOCK = 64
NGLOBAL = 2
NRANDOM = 3
NLIST = 3 + NGLOBAL + NRANDOM
MASKED = -1e30
EXP2_SCALE = 1.4426950408889634 / HEAD_DIM**0.5
STAT_TILE = 16
VMEM_LIMIT = 20 * 1024 * 1024
PROJECT_LIMIT = 32 * 1024 * 1024


group_blocks = 8


def eye_mask():
    rows = lax.broadcasted_iota(jnp.int32, (BLOCK, BLOCK), 0)
    columns = lax.broadcasted_iota(jnp.int32, (BLOCK, BLOCK), 1)
    return rows == columns


def attend_group(blocks, head, starts_ref, bias_ref, q_ref, pool):
    lanes = pl.ds(head * HEAD_DIM, HEAD_DIM)
    listed = [
        [
            pl.ds(pl.multiple_of(starts_ref[i * NLIST + e], BLOCK), BLOCK)
            for e in range(NLIST)
        ]
        for i in blocks
    ]
    places = [pl.ds(pl.multiple_of(i * BLOCK, BLOCK), BLOCK) for i in blocks]
    scores = []
    for i, rows, listing in zip(blocks, places, listed):
        keys = jnp.concatenate([pool[0, w, lanes] for w in listing], axis=0)
        product = lax.dot_general(
            q_ref[rows, lanes],
            keys,
            (((1,), (1,)), ((), ())),
            preferred_element_type=jnp.float32,
        )
        scores.append(product + bias_ref[pl.ds(i, 1), :])
    weighed = []
    for score in scores:
        highest = jnp.max(score, axis=1, keepdims=True)
        weights = jnp.exp2((score - highest) * EXP2_SCALE)
        total = jnp.sum(weights, axis=1, keepdims=True)
        weighed.append((weights.astype(jnp.bfloat16), highest, total))
    results = []
    for listing, (weights, highest, total) in zip(listed, weighed):
        values = jnp.concatenate([pool[1, w, lanes] for w in listing], axis=0)
        mixed = jnp.dot(weights, values, preferred_element_type=jnp.float32)
        results.append((lanes, mixed, highest, total))
    return results


def put_stats(i, head, stats_ref, highest, total):
    eye = eye_mask()
    high_row = jnp.sum(jnp.where(eye, highest, 0.0), axis=0, keepdims=True)
    total_row = jnp.sum(jnp.where(eye, total, 0.0), axis=0, keepdims=True)
    stats_ref[head, pl.ds(i, 1), :] = jnp.concatenate([high_row, total_row], axis=1)


def load_pool(parts, pool, sems):
    copies, low = [], 0
    for n, part in enumerate(parts):
        size = part.shape[1]
        copies.append(
            pltpu.make_async_copy(part, pool.at[:, pl.ds(low, size), :], sems.at[n])
        )
        low += size
    for copy in copies:
        copy.start()
    for copy in copies:
        copy.wait()


def attend_part(part, parts, starts_ref, bias_ref, q_ref, pool, mixed_ref, stats_ref, normalise):
    blocks = q_ref.shape[0] // BLOCK // parts
    unroll = UNROLL if blocks % UNROLL == 0 else blocks
    stats_ref[...] = jnp.zeros_like(stats_ref)

    for head in range(q_ref.shape[1] // HEAD_DIM):

        def step(n, _):
            ids = [n * unroll + u for u in range(unroll)]
            results = attend_group(
                [part * blocks + i for i in ids], head, starts_ref, bias_ref, q_ref, pool
            )
            for i, (lanes, mixed, highest, total) in zip(ids, results):
                rows = pl.ds(pl.multiple_of(i * BLOCK, BLOCK), BLOCK)
                mixed = mixed / total if normalise else mixed
                mixed_ref[rows, lanes] = mixed.astype(mixed_ref.dtype)
                put_stats(i, head, stats_ref, highest, total)
            return 0

        lax.fori_loop(0, blocks // unroll, step, 0)


def guest_kernel(parts, count, starts_ref, bias_ref, q_ref, *refs):
    *message_refs, pool, stats, sems = refs[count:]
    load_pool(refs[:count], pool, sems)
    base = q_ref.shape[0] // parts
    for part, message_ref in enumerate(message_refs):
        attend_part(part, parts, starts_ref, bias_ref, q_ref, pool, message_ref, stats, True)
        for head in range(q_ref.shape[1] // HEAD_DIM):
            rest = stats[head]
            for n in range(3):
                piece = rest.astype(jnp.bfloat16)
                rows = pl.ds(base + n * rest.shape[0], rest.shape[0])
                message_ref[rows, pl.ds(head * HEAD_DIM, HEAD_DIM)] = piece
                rest = rest - piece.astype(jnp.float32)


def home_kernel(parts, count, starts_ref, bias_ref, q_ref, *refs):
    *result_refs, pool, sems = refs[count:]
    load_pool(refs[:count], pool, sems)
    for part in range(parts):
        mixed_ref, stats_ref = result_refs[2 * part : 2 * part + 2]
        attend_part(part, parts, starts_ref, bias_ref, q_ref, pool, mixed_ref, stats_ref, False)


def merge_kernel(mixed_ref, stats_ref, message_ref, *refs):
    *out_refs, home_scale, guest_scale = refs
    base, width = mixed_ref.shape
    blocks = base // BLOCK
    size = stats_ref.shape[1]
    other = message_ref[pl.ds(base, size), :].astype(jnp.float32)
    for n in (1, 2):
        other = other + message_ref[pl.ds(base + n * size, size), :].astype(jnp.float32)
    eye = eye_mask()
    for head in range(width // HEAD_DIM):
        low = head * HEAD_DIM
        lanes = pl.ds(low, HEAD_DIM)
        high_h = stats_ref[head, :, :BLOCK]
        total_h = stats_ref[head, :, BLOCK:]
        high_g = other[:, low : low + BLOCK]
        total_g = other[:, low + BLOCK : low + HEAD_DIM]
        highest = jnp.maximum(high_h, high_g)
        factor_h = jnp.exp2((high_h - highest) * EXP2_SCALE)
        factor_g = jnp.exp2((high_g - highest) * EXP2_SCALE) * total_g
        total = factor_h * total_h + factor_g
        total = jnp.where(total > 0, total, 1.0)
        home_scale[...] = factor_h / total
        guest_scale[...] = factor_g / total

        def step(n, part, low):
            i = low + n
            rows = pl.ds(pl.multiple_of(i * BLOCK, BLOCK), BLOCK)
            scale_h = jnp.sum(
                jnp.where(eye, home_scale[pl.ds(i, 1), :], 0.0), axis=1, keepdims=True
            )
            scale_g = jnp.sum(
                jnp.where(eye, guest_scale[pl.ds(i, 1), :], 0.0), axis=1, keepdims=True
            )
            mixed = (
                mixed_ref[rows, lanes] * scale_h
                + message_ref[rows, lanes].astype(jnp.float32) * scale_g
            )
            rows = pl.ds(pl.multiple_of(n * BLOCK, BLOCK), BLOCK)
            out_refs[part][rows, lanes] = mixed.astype(jnp.bfloat16)

        low = 0
        for part, out_ref in enumerate(out_refs):

            def body(n, _, part=part, low=low):
                step(n, part, low)
                return 0

            count = out_ref.shape[0] // BLOCK
            lax.fori_loop(0, count, body, 0, unroll=4)
            low += count


def last_terms_kernel(groups, w_ref, sum_ref, *refs):
    x_refs, out_ref = refs[: 2 * groups], refs[-1]
    ordered = [x_refs[h * groups + r][...] for r in range(groups) for h in range(2)]
    term = jnp.dot(
        jnp.concatenate(ordered, axis=1), w_ref[...], preferred_element_type=jnp.float32
    )
    out_ref[...] = (sum_ref[...] + term).astype(out_ref.dtype)


VMEM = pl.BlockSpec(memory_space=pltpu.VMEM)
SMEM = pl.BlockSpec(memory_space=pltpu.SMEM)
ANY = pl.BlockSpec(memory_space=pl.ANY)
HBM = pl.BlockSpec(memory_space=pltpu.HBM)


def params():
    return pltpu.CompilerParams(vmem_limit_bytes=VMEM_LIMIT)


def pool_scratch(query):
    return pltpu.VMEM((2, 4 * query.shape[0], query.shape[1]), jnp.bfloat16)


def stats_shape(query, parts, kind):
    blocks = query.shape[0] // BLOCK // parts
    size = -(-blocks // STAT_TILE) * STAT_TILE
    return kind((query.shape[1] // HEAD_DIM, size, 2 * BLOCK), jnp.float32)


def cost(micros):
    return pl.CostEstimate(flops=int(micros * 1.15e9), bytes_accessed=0, transcendentals=0)


def guest_call(starts, bias, query, pieces, parts=1):
    rows, width = query.shape
    size = stats_shape(query, parts, jax.ShapeDtypeStruct).shape[1]
    message = jax.ShapeDtypeStruct((rows // parts + 3 * size, width), jnp.bfloat16)
    return pl.pallas_call(
        functools.partial(guest_kernel, parts, len(pieces)),
        out_shape=[message] * parts,
        in_specs=[SMEM, VMEM, VMEM] + [ANY] * len(pieces),
        out_specs=[VMEM] * parts,
        scratch_shapes=[
            pool_scratch(query),
            stats_shape(query, parts, pltpu.VMEM),
            pltpu.SemaphoreType.DMA((len(pieces),)),
        ],
        compiler_params=params(),
        cost_estimate=cost(GUEST_US),
        name="guest_attention",
    )(starts, bias, query, *pieces)


def home_call(starts, bias, query, pieces, parts=1):
    rows, width = query.shape
    results = [
        jax.ShapeDtypeStruct((rows // parts, width), jnp.float32),
        stats_shape(query, parts, jax.ShapeDtypeStruct),
    ]
    return pl.pallas_call(
        functools.partial(home_kernel, parts, len(pieces)),
        out_shape=results * parts,
        in_specs=[SMEM, VMEM, VMEM] + [ANY] * len(pieces),
        out_specs=[VMEM] * (2 * parts),
        scratch_shapes=[pool_scratch(query), pltpu.SemaphoreType.DMA((len(pieces),))],
        compiler_params=params(),
        cost_estimate=cost(0),
        name="home_attention",
    )(starts, bias, query, *pieces)


def merge_call(mixed, stats, message, sizes=None):
    rows, width = mixed.shape
    sizes = sizes or [rows]
    return pl.pallas_call(
        merge_kernel,
        out_shape=[jax.ShapeDtypeStruct((size, width), jnp.bfloat16) for size in sizes],
        in_specs=[VMEM, VMEM, VMEM],
        out_specs=[VMEM] * len(sizes),
        scratch_shapes=[
            pltpu.VMEM((stats.shape[1], BLOCK), jnp.float32),
            pltpu.VMEM((stats.shape[1], BLOCK), jnp.float32),
        ],
        compiler_params=params(),
        cost_estimate=cost(0),
        name="merge_halves",
    )(mixed, stats, message)


ROW_TILE = 256


def last_terms(summed, gathered, weight, part, filled=None):
    rows, columns = summed.shape
    first, tiles = part
    pieces = [piece for group in gathered for piece in group]

    def row_spec(height, width):
        low = first if height == rows else 0
        return pl.BlockSpec((ROW_TILE, width), lambda i: (i + low, 0))

    others = [] if filled is None else [filled]
    return pl.pallas_call(
        functools.partial(last_terms_kernel, len(pieces) // 2),
        grid=(tiles,),
        out_shape=jax.ShapeDtypeStruct((rows, columns), jnp.bfloat16),
        in_specs=[VMEM]
        + [row_spec(*v.shape) for v in [summed, *pieces]]
        + [ANY] * len(others),
        out_specs=row_spec(rows, columns),
        input_output_aliases={2 + len(pieces): 0} if others else {},
        compiler_params=params(),
        cost_estimate=cost(PROJECT_US),
        name="last_terms",
    )(weight, summed, *pieces, *others)


def first_terms_kernel(groups, w_ref, *refs):
    x_refs, (out_ref, columns, sems) = refs[: 2 * groups], refs[2 * groups :]
    copies = [
        pltpu.make_async_copy(
            x_refs[head * groups + relation],
            columns.at[:, pl.ds((2 * relation + head) * HEAD_DIM, HEAD_DIM)],
            sems.at[2 * relation + head],
        )
        for relation in range(groups)
        for head in range(2)
    ]
    for copy in copies:
        copy.start()
    for copy in copies:
        copy.wait()

    def step(i, _):
        rows = pl.ds(pl.multiple_of(i * ROW_TILE, ROW_TILE), ROW_TILE)
        out_ref[rows, :] = jnp.dot(
            columns[rows, :], w_ref[...], preferred_element_type=jnp.float32
        )
        return 0

    lax.fori_loop(0, out_ref.shape[0] // ROW_TILE, step, 0)


def first_terms(gathered, weight):
    pieces = [piece for group in gathered for piece in group]
    rows = pieces[0].shape[0]
    return pl.pallas_call(
        functools.partial(first_terms_kernel, len(pieces) // 2),
        out_shape=jax.ShapeDtypeStruct((rows, weight.shape[1]), jnp.float32),
        in_specs=[VMEM] + [ANY] * len(pieces),
        out_specs=VMEM,
        scratch_shapes=[
            pltpu.VMEM((rows, weight.shape[0]), jnp.bfloat16),
            pltpu.SemaphoreType.DMA((len(pieces),)),
        ],
        compiler_params=params(),
        cost_estimate=cost(0),
        name="first_terms",
    )(weight, *pieces)


def order_kernel(me_ref, w_ref, first_ref, last_ref, sems):
    copies = []
    for relation in range(w_ref.shape[0]):
        for n, target in enumerate((first_ref, last_ref)):
            copies.append(
                pltpu.make_async_copy(
                    w_ref.at[me_ref[0] ^ relation, pl.ds(2 * n, 2)],
                    target.at[relation],
                    sems.at[2 * relation + n],
                )
            )
    for copy in copies:
        copy.start()
    for copy in copies:
        copy.wait()


def order_weights(weights):
    groups, heads, depth, columns = weights.shape
    half = jax.ShapeDtypeStruct((groups, heads // 2, depth, columns), weights.dtype)
    myself = lax.axis_index("head").astype(jnp.int32).reshape(1)
    parts = pl.pallas_call(
        order_kernel,
        out_shape=[half, half],
        in_specs=[SMEM, ANY],
        out_specs=[ANY, ANY],
        scratch_shapes=[pltpu.SemaphoreType.DMA((2 * groups,))],
        compiler_params=params(),
        cost_estimate=cost(0),
        name="order_weights",
    )(myself, weights)
    return [part.reshape(-1, columns) for part in parts]


def key_list(shard, global_ids, rand_ids, local_blocks, shards):
    total_blocks = local_blocks * shards
    block_ids = shard * local_blocks + jnp.arange(local_blocks, dtype=jnp.int32)
    near = block_ids[:, None] + jnp.arange(-1, 2, dtype=jnp.int32)[None, :]
    inside = (near >= 0) & (near < total_blocks)
    listed = lax.dynamic_slice_in_dim(rand_ids, shard * local_blocks, local_blocks, 0)
    glob = jnp.broadcast_to(global_ids[None, :], (local_blocks, NGLOBAL))
    ids = jnp.concatenate([jnp.clip(near, 0, total_blocks - 1), glob, listed], axis=1)
    inside = jnp.concatenate(
        [inside, jnp.ones((local_blocks, NGLOBAL + NRANDOM), jnp.bool_)], axis=1
    )
    return ids, inside


def guests_first(guests, source, global_ids, rand_ids, local_blocks, shards):
    ids, inside = key_list(guests, global_ids, rand_ids, local_blocks, shards)
    order = jnp.arange(local_blocks, dtype=jnp.int32)
    blocks = source * local_blocks + order
    hits = (ids[None] == blocks[:, None, None]) & inside[None]
    listed = jnp.max(hits.astype(jnp.int32), axis=(1, 2))
    earlier = (order[None, :] < order[:, None]).astype(jnp.int32)
    among = jnp.sum(earlier * listed[None, :], axis=1)
    return jnp.where(listed > 0, among, jnp.sum(listed) + order - among)


def key_places(shard, myself, global_ids, rand_ids, local_blocks, shards, diagonal=None):
    half = shards // 2
    ids, inside = key_list(shard, global_ids, rand_ids, local_blocks, shards)
    owner = ids // local_blocks
    here = ((owner // half) == (myself // half)) & inside
    relative = (owner ^ myself) & (half - 1)
    block = ids % local_blocks
    if diagonal is not None:
        order = jnp.arange(local_blocks, dtype=jnp.int32)
        moved = jnp.sum(jnp.where(block[..., None] == order, diagonal, 0), axis=-1)
        block = jnp.where(relative == half - 1, moved, block)
    starts = jnp.where(here, (relative * local_blocks + block) * BLOCK, 0)
    bias = jnp.repeat(jnp.where(here, 0.0, MASKED).astype(jnp.float32), BLOCK, axis=1)
    return starts.reshape(-1).astype(jnp.int32), bias


def split_kernel(order_ref, pair_ref, first_ref, rest_ref):
    blocks = first_ref.shape[1] // BLOCK
    for n in range(pair_ref.shape[1] // BLOCK):
        source = pl.ds(pl.multiple_of(order_ref[n] * BLOCK, BLOCK), BLOCK)
        target = first_ref if n < blocks else rest_ref
        target[:, pl.ds((n % blocks) * BLOCK, BLOCK), :] = pair_ref[:, source, :]


def split_call(order, pair):
    half = jax.ShapeDtypeStruct((2, pair.shape[1] // 2, pair.shape[2]), pair.dtype)
    return pl.pallas_call(
        split_kernel,
        out_shape=[half, half],
        in_specs=[SMEM, VMEM],
        out_specs=[VMEM, VMEM],
        compiler_params=params(),
        cost_estimate=cost(0),
        name="guests_first",
    )(order, pair)


def swap(value, distance, shards):
    return lax.ppermute(value, "seq", [(i, i ^ distance) for i in range(shards)])


def after(value, *tokens):
    return lax.optimization_barrier((value, *tokens))[0]


def hop(value, distance, groups):
    return lax.ppermute(value, "head", [(i, i ^ distance) for i in range(groups)])


def together(*values):
    return lax.optimization_barrier(values)


UNROLL = 12
GUEST_US = 0.1
PROJECT_US = 4
UPPER_TILES = 5


def halves_body(queries, keys_values, global_ids, rand_ids, out_weight):
    rows, width = queries.shape
    heads_here = width // HEAD_DIM
    local_blocks = rows // BLOCK
    shards = lax.axis_size("seq")
    myself = lax.axis_index("seq")
    groups = lax.axis_size("head")
    opposite = shards // 2

    def column(array, head):
        return lax.slice_in_dim(array, head * HEAD_DIM, (head + 1) * HEAD_DIM, axis=array.ndim - 1)

    def over_y(value):
        return swap(value, 1, shards)

    def over_z(value):
        return swap(value, 2, shards)

    def across(value):
        return swap(value, opposite, shards)

    lists = (global_ids, rand_ids, local_blocks, shards)
    mine = guests_first(myself ^ opposite, myself ^ 3, *lists)
    theirs = guests_first(myself ^ opposite ^ 1, myself ^ 2, *lists)
    count = jnp.arange(local_blocks, dtype=jnp.int32)
    order = jnp.sum(jnp.where(theirs[None, :] == count[:, None], count[None, :], 0), axis=1)
    home = key_places(myself, myself, *lists)
    guest = key_places(myself ^ opposite, myself, *lists)
    last_home = key_places(myself, myself, *lists, mine)
    last_guest = key_places(myself ^ opposite, myself, *lists, mine)
    home, guest = (*home, *last_home, order), (*guest, *last_guest)
    weights = order_weights(
        out_weight.reshape(groups, heads_here, HEAD_DIM, out_weight.shape[1])
    )
    k0 = column(keys_values, 0)
    others = after(keys_values, k0)
    k1, k2, k3 = [column(others, h) for h in range(1, heads_here)]
    q0, q1, q2, q3 = [column(queries, h) for h in range(heads_here)]

    y0, z0 = over_y(k0), over_z(k0)
    y0, z0, k1_, v0, v1, home, guest = together(y0, z0, k1, q0, q1, home, guest)

    d0, y1, z1, v0, v1 = over_y(z0), over_y(k1_), over_z(k1_), across(v0), across(v1)
    p0 = (k0, y0, z0, d0)
    (s0,) = guest_call(*guest[:2], v0, p0)
    t0, y1, z1, v1, k2_, v2, weights = together(s0, y1, z1, v1, k2, q2, weights)

    d1, y2, z2, v2, g0 = over_y(z1), over_y(k2_), over_z(k2_), across(v2), across(s0)
    m0 = home_call(*home[:2], after(q0, t0), p0)
    p1 = (k1, y1, z1, d1)
    (s1,) = guest_call(*guest[:2], after(v1, m0[1]), p1)
    t1, y2, z2, v2, g0, k3_, v3 = together(s1, y2, z2, v2, g0, k3, q3)

    d2, y3, z3, v3, g1 = over_y(z2), over_y(k3_), over_z(k3_), across(v3), across(s1)
    m1 = home_call(*home[:2], after(q1, t1), p1)
    (a0,) = merge_call(*m0, after(g0, m1[1]))
    a0x, a0c = hop(a0, 2, groups), hop(a0, 1, groups)
    p2 = (k2, y2, z2, d2)
    (s2,) = guest_call(*guest[:2], after(v2, m1[1], v3), p2)
    t2, y3, z3, v3, g1, a0x, a0c = together(s2, y3, z3, v3, g1, a0x, a0c)

    first, rest = split_call(home[4], z3)
    d3, d3_, g2 = over_y(first), over_y(rest), across(s2)
    m2 = home_call(*home[:2], after(q2, t2), p2)
    (a1,) = merge_call(*m1, after(g1, m2[1]))
    a1x, a1c, a0d = hop(a1, 2, groups), hop(a1, 1, groups), hop(a0x, 1, groups)
    (s3,) = guest_call(*guest[2:4], after(v3, a1), (k3, y3, z3, d3))
    g3 = across(after(s3, g2))
    m3 = home_call(*home[2:4], after(q3, s3), (k3, y3, z3, d3, d3_))
    (a2,) = merge_call(*m2, after(g2, m3[1]))
    a1d = hop(after(a1x, s3), 1, groups)
    a2x, a2c = hop(a2, 2, groups), hop(a2, 1, groups)
    early = ((a0, a0c, a0x, a0d), (a1, a1c, a1x, a1d))
    summed = first_terms(early, after(weights[0], m3[1]))

    tiles = rows // ROW_TILE
    tiles_a = UPPER_TILES
    sizes = [tiles_a * ROW_TILE, (tiles - tiles_a) * ROW_TILE]
    a3a, a3b = merge_call(*m3, after(g3, summed), sizes)
    a3ax, a3ac = hop(a3a, 2, groups), hop(a3a, 1, groups)
    a3bx, a3bc = hop(after(a3b, a3a), 2, groups), hop(a3b, 1, groups)
    a2d = hop(after(a2x, a3b), 1, groups)
    a2 = (a2, a2c, a2x, a2d)
    a3ad = hop(a3ax, 1, groups)
    upper = last_terms(summed, (a2, (a3a, a3ac, a3ax, a3ad)), weights[1], (0, tiles_a))
    a3bd = hop(after(a3bx, upper), 1, groups)
    late = (a2, (a3b, a3bc, a3bx, a3bd))
    return last_terms(summed, late, weights[1], (tiles_a, tiles - tiles_a), upper)


def padded_2(block, sides, width):
    for axis, dim in sides:
        count = lax.axis_size(axis)
        forward = [(i, i + 1) for i in range(count - 1)]
        backward = [(target, source) for source, target in forward]
        low = lax.ppermute(
            lax.slice_in_dim(block, block.shape[dim] - width, None, axis=dim), axis, forward
        )
        high = lax.ppermute(lax.slice_in_dim(block, 0, width, axis=dim), axis, backward)
        block = jnp.concatenate([low, block, high], axis=dim)
    return block


def broadcast(block, axis, owner):
    block = jnp.where(lax.axis_index(axis) == owner, block, jnp.zeros_like(block))
    return lax.psum(block, axis)


def plan_slots(requests, myself, capacity, per_shard):
    sources = requests // per_shard
    offsets = requests % per_shard
    count = requests.shape[1]
    order = jnp.arange(count, dtype=jnp.int32)
    earlier = (order[:, None] < order[None, :]).astype(jnp.int32)
    matches = (sources[:, :, None] == sources[:, None, :]).astype(jnp.int32)
    ranks = jnp.sum(matches * earlier[None], axis=1)
    slot_range = jnp.arange(capacity, dtype=jnp.int32)
    wanted = (
        (sources == myself)[:, None, :] & (ranks[:, None, :] == slot_range[None, :, None])
    ).astype(jnp.int32)
    chosen = jnp.sum(wanted * offsets[:, None, :], axis=2).reshape(-1)
    own_sources = lax.dynamic_index_in_dim(sources, myself, 0, keepdims=False)
    own_ranks = lax.dynamic_index_in_dim(ranks, myself, 0, keepdims=False)
    return (chosen, own_sources * capacity + own_ranks)


def attend_blocks(query_part, local_keys, local_values, glob_keys, glob_values, valid):
    scale = 1.0 / HEAD_DIM**0.5
    near_scores = (
        jnp.einsum("bqhd,bkhd->bhqk", query_part, local_keys, preferred_element_type=jnp.float32)
        * scale
    )
    near_scores = jnp.where(valid[:, None, None, :], near_scores, -jnp.inf)
    glob_scores = (
        jnp.einsum("bqhd,khd->bhqk", query_part, glob_keys, preferred_element_type=jnp.float32)
        * scale
    )
    highest = jnp.maximum(jnp.max(near_scores, axis=-1), jnp.max(glob_scores, axis=-1))
    near_exp = jnp.exp(near_scores - highest[..., None])
    glob_exp = jnp.exp(glob_scores - highest[..., None])
    total = jnp.sum(near_exp, axis=-1) + jnp.sum(glob_exp, axis=-1)
    near_weights = (near_exp / total[..., None]).astype(jnp.bfloat16)
    glob_weights = (glob_exp / total[..., None]).astype(jnp.bfloat16)
    mixed = jnp.einsum(
        "bhqk,bkhd->bqhd", near_weights, local_values, preferred_element_type=jnp.float32
    )
    mixed = mixed + jnp.einsum(
        "bhqk,khd->bqhd", glob_weights, glob_values, preferred_element_type=jnp.float32
    )
    return mixed.astype(jnp.bfloat16)


def exchange_body(queries, keys_values, global_ids, rand_ids, out_weight):
    rows = queries.shape[0]
    width = queries.shape[1]
    heads_here = width // HEAD_DIM
    local_blocks = rows // BLOCK
    shards = lax.axis_size("seq")
    myself = lax.axis_index("seq")
    total_blocks = local_blocks * shards
    pair_blocks = keys_values.reshape(2, local_blocks, BLOCK, width)
    padded = padded_2(keys_values, (("seq", 1),), BLOCK)
    padded = padded.reshape(2, local_blocks + 2, BLOCK, width)
    panel_list = []
    for which in range(NGLOBAL):
        target = global_ids[which]
        owner = target // local_blocks
        local_panel = lax.dynamic_index_in_dim(
            pair_blocks, target % local_blocks, 1, keepdims=False
        )
        panel_list.append(broadcast(local_panel, "seq", owner))
    glob = jnp.stack(panel_list, axis=1).reshape(2, NGLOBAL * BLOCK, heads_here, HEAD_DIM)
    requests = rand_ids.reshape(shards, local_blocks, NRANDOM)
    capacity = (local_blocks + shards - 1) // shards
    fetched = []
    for column in range(NRANDOM):
        chosen, slots = plan_slots(requests[:, :, column], myself, capacity, local_blocks)
        outgoing = jnp.take(pair_blocks, chosen, axis=1)
        incoming = lax.all_to_all(outgoing, "seq", split_axis=1, concat_axis=1, tiled=True)
        fetched.append(jnp.take(incoming, slots, axis=1))
    remote = jnp.stack(fetched, axis=2)
    segment = jnp.arange((3 + NRANDOM) * BLOCK, dtype=jnp.int32) // BLOCK

    def one_group(index):
        first = index * group_blocks
        query_part = lax.dynamic_slice_in_dim(queries, first * BLOCK, group_blocks * BLOCK, 0)
        query_part = query_part.reshape(group_blocks, BLOCK, heads_here, HEAD_DIM)
        window = lax.dynamic_slice_in_dim(padded, first, group_blocks + 2, 1)
        farther = lax.dynamic_slice_in_dim(remote, first, group_blocks, 1)
        farther = farther.reshape(2, group_blocks, NRANDOM * BLOCK, width)
        local = jnp.concatenate(
            [
                window[:, 0:group_blocks],
                window[:, 1 : group_blocks + 1],
                window[:, 2 : group_blocks + 2],
                farther,
            ],
            axis=2,
        )
        local = local.reshape(2, group_blocks, (3 + NRANDOM) * BLOCK, heads_here, HEAD_DIM)
        block_ids = myself * local_blocks + first + jnp.arange(group_blocks, dtype=jnp.int32)
        drop_before = (segment[None, :] == 0) & (block_ids[:, None] == 0)
        drop_after = (segment[None, :] == 2) & (block_ids[:, None] == total_blocks - 1)
        valid = jnp.logical_not(drop_before | drop_after)
        mixed = attend_blocks(query_part, local[0], local[1], glob[0], glob[1], valid)
        return mixed.reshape(group_blocks * BLOCK, width)

    attended = lax.map(
        one_group, jnp.arange(local_blocks // group_blocks, dtype=jnp.int32)
    ).reshape(rows, width)
    summed = jnp.dot(
        lax.all_gather(attended, "head", axis=1, tiled=True),
        out_weight,
        preferred_element_type=jnp.float32,
    )
    return summed.astype(jnp.bfloat16)


def solution(mesh):
    body = halves_body if dict(mesh.shape) == {"seq": 8, "head": 4} else exchange_body
    in_specs = (P("seq", "head"), P(None, "seq", "head"), P(), P(), P(None, "head"))
    out_specs = P("seq", "head")
    return jax.shard_map(body, mesh=mesh, in_specs=in_specs, out_specs=out_specs, check_vma=False)
```
